512 devices in a mesh: prompt: 32 (over z, x), sample: 16 (over y, core).
Axes of the slice: x: 4, y: 8, z: 8, core: 2. Of those that a mesh axis runs over, the one named last changes fastest.
Arguments:
- prompt_q: bfloat16 [8192, 2048], P(('prompt', 'sample')), parts along dimension 0, may hold values from -6 to 6
- prompt_k: bfloat16 [8192, 512], P(('prompt', 'sample')), parts along dimension 0, may hold values from -6 to 6
- prompt_value_rows: bfloat16 [8192, 512], P(('prompt', 'sample')), parts along dimension 0, may hold values from -5 to 5
- prompt_dout: bfloat16 [8192, 2048], P(('prompt', 'sample')), parts along dimension 0, may hold values from -5 to 5
- comp_q: bfloat16 [512, 128, 2048], P(('prompt', 'sample')), parts along dimension 0, may hold values from -6 to 6
- completion_keys: bfloat16 [512, 128, 512], P(('prompt', 'sample')), parts along dimension 0, may hold values from -5 to 5
- completion_values: bfloat16 [512, 128, 512], P(('prompt', 'sample')), parts along dimension 0, may hold values from -5 to 5
- comp_dout: bfloat16 [512, 128, 2048], P(('prompt', 'sample')), parts along dimension 0, may hold values from -5 to 5
- comp_lengths: int32 [512], P(('prompt', 'sample')), parts along dimension 0, may hold values from 32 to 128, as said below
- prompt_length: int32 [32], P('prompt'), parts along dimension 0, may hold values from 224 to 256, as said below
Outputs:
- prompt_dq: bfloat16 [8192, 2048], P(('prompt', 'sample')), parts along dimension 0
- prompt_dk: bfloat16 [8192, 512], P(('prompt', 'sample')), parts along dimension 0
- prompt_dv: bfloat16 [8192, 512], P(('prompt', 'sample')), parts along dimension 0
- comp_dq: bfloat16 [512, 128, 2048], P(('prompt', 'sample')), parts along dimension 0
- comp_dk: bfloat16 [512, 128, 512], P(('prompt', 'sample')), parts along dimension 0
- comp_dv: bfloat16 [512, 128, 512], P(('prompt', 'sample')), parts along dimension 0
The draws below stay inside these ranges and needn't reach their ends.
There are 32 independent parts, one for each index of `prompt`. The reference program is written for one: setup_inputs(seed, part) draws one part's arguments, and reference() takes and returns one part's arrays. A program takes and returns all parts, laid end to end along the dimension named above; each array names one. Nothing has to cross between parts.
Inputs may be any that keep to these rules, and one draw needn't show every extreme that they name: `comp_lengths`: one completion of every prompt has exactly 128 tokens. Prompt rows at and after prompt_length are padding.
All inputs are finite; a program needn't handle non-finite values.
Results may differ from the reference program's by a relative error of at most 0.012.
The reference program's roundings to bfloat16 on the way (of `soft_b` and `score_grad_b`) count: a program that leaves them out, or rounds other values in their place, can miss the bound.
Values may be sent and summed in bfloat16 or wider, within the bound.
No kernel may reach another device: no remote copies, remote signals or barrier semaphores. Data moves between devices by JAX's collectives and lax.ppermute only.
A program may use at most 64 MiB of HBM per device.

```python
import jax
import jax.numpy as jnp
from jax import lax

QUERY_HEADS = 16
KEY_VALUE_HEADS = 4
HEAD_DIM = 128
COMPLETION_ROWS = 128
PDEV = 16
PROMPT_ROWS = 256
SAMPLE_COUNT = 16


def draw_prompt_q(key, part):
    key = jax.random.fold_in(key, 1)
    sampled_values = jax.random.truncated_normal(key, -4.0, 4.0, (PROMPT_ROWS, QUERY_HEADS * HEAD_DIM))
    return sampled_values.astype(jnp.float32).astype(jnp.bfloat16)


def draw_prompt_k(key, part):
    key = jax.random.fold_in(key, 3)
    sampled_values = jax.random.truncated_normal(key, -4.0, 4.0, (PROMPT_ROWS, KEY_VALUE_HEADS * HEAD_DIM))
    return sampled_values.astype(jnp.float32).astype(jnp.bfloat16)


def draw_comp_q(key, part):
    key = jax.random.fold_in(key, 4)
    sampled_values = jax.random.truncated_normal(key, -4.0, 4.0, (SAMPLE_COUNT, COMPLETION_ROWS, QUERY_HEADS * HEAD_DIM))
    return sampled_values.astype(jnp.float32).astype(jnp.bfloat16)


def draw_comp_lengths(key, part):
    key = jax.random.fold_in(key, 5)
    drawn_lengths = jax.random.randint(key, (SAMPLE_COUNT,), COMPLETION_ROWS // 4, COMPLETION_ROWS + 1)
    longest = jax.random.randint(jax.random.fold_in(key, 6), (), 0, SAMPLE_COUNT)
    return jnp.where(jnp.arange(SAMPLE_COUNT) == longest, COMPLETION_ROWS, drawn_lengths).astype(jnp.int32)


def draw_prompt_length(key, part):
    key = jax.random.fold_in(key, 7)
    shortfall = jax.random.randint(key, (1,), 1, 2 * PDEV + 1)
    offset = jax.random.randint(jax.random.fold_in(key, 8), (), 0, 4)
    phase = (part + offset) % 4
    shortfall = jnp.where(phase == 0, 0, jnp.where(phase == 2, 2 * PDEV, shortfall))
    return (PROMPT_ROWS - shortfall).astype(jnp.int32)


def shard_levels(own_key, extent, cuts, smallest, largest):
    gain = 1.0
    for dim, blocks in cuts:
        steps = jax.random.uniform(jax.random.fold_in(jax.random.fold_in(own_key, 6), dim), (blocks,), jnp.float32, smallest / len(cuts), largest / len(cuts))
        gain = gain * jnp.repeat(jnp.exp(steps), extent[dim] // blocks).reshape((-1,) + (1,) * (len(extent) - 1 - dim))
    return gain


def scatter_about(key, dims, width, limit, cuts=(), kind=jnp.bfloat16):
    loudness = shard_levels(key, dims, cuts, -0.22, 0.18) if cuts else 1.0
    result = jax.random.normal(key, dims, jnp.float32) * width * loudness
    return jnp.minimum(jnp.maximum(result, -limit), limit).astype(kind)


def setup_inputs(seed: int = 0, part: int = 0) -> dict:
    splits = jax.random.split(jax.random.key(seed), 11)
    part_splits = jax.random.split(jax.random.fold_in(splits[10], part), 11)
    prompt_q = draw_prompt_q(jax.random.fold_in(jax.random.fold_in(splits[10], part), 71), part)
    prompt_k = draw_prompt_k(jax.random.fold_in(jax.random.fold_in(splits[10], part), 71), part)
    prompt_value_rows = scatter_about(part_splits[2], (PROMPT_ROWS, KEY_VALUE_HEADS * HEAD_DIM), 1.0, 5.0, ((0, 16),))
    prompt_dout = scatter_about(part_splits[3], (PROMPT_ROWS, QUERY_HEADS * HEAD_DIM), 1.0, 5.0, ((0, 16),))
    comp_q = draw_comp_q(jax.random.fold_in(jax.random.fold_in(splits[10], part), 71), part)
    completion_keys = scatter_about(part_splits[5], (SAMPLE_COUNT, COMPLETION_ROWS, KEY_VALUE_HEADS * HEAD_DIM), 1.0, 5.0, ((0, 16),))
    completion_values = scatter_about(part_splits[6], (SAMPLE_COUNT, COMPLETION_ROWS, KEY_VALUE_HEADS * HEAD_DIM), 1.0, 5.0, ((0, 16),))
    comp_dout = scatter_about(part_splits[7], (SAMPLE_COUNT, COMPLETION_ROWS, QUERY_HEADS * HEAD_DIM), 1.0, 5.0, ((0, 16),))
    comp_lengths = draw_comp_lengths(jax.random.fold_in(jax.random.fold_in(splits[10], part), 71), part)
    prompt_length = draw_prompt_length(jax.random.fold_in(jax.random.fold_in(splits[10], part), 71), part)
    return {"prompt_q": prompt_q, "prompt_k": prompt_k, "prompt_value_rows": prompt_value_rows, "prompt_dout": prompt_dout, "comp_q": comp_q, "completion_keys": completion_keys, "completion_values": completion_values, "comp_dout": comp_dout, "comp_lengths": comp_lengths, "prompt_length": prompt_length}


def attend(query_rows, key_matrix, value_matrix, output_gradients, allowed):
    row_number = query_rows.shape[0]
    key_total = key_matrix.shape[0]
    group_width = QUERY_HEADS // KEY_VALUE_HEADS
    score_scale = HEAD_DIM ** -0.5
    query_rank_four = query_rows.astype(jnp.float32).reshape(row_number, KEY_VALUE_HEADS, group_width, HEAD_DIM)
    gradient_rank_four = output_gradients.astype(jnp.float32).reshape(row_number, KEY_VALUE_HEADS, group_width, HEAD_DIM)
    key_rank_three = key_matrix.astype(jnp.float32).reshape(key_total, KEY_VALUE_HEADS, HEAD_DIM)
    value_rank_three = value_matrix.astype(jnp.float32).reshape(key_total, KEY_VALUE_HEADS, HEAD_DIM)
    scores = jnp.einsum('rhgd,nhd->hgrn', query_rank_four, key_rank_three) * score_scale
    masked = jnp.where(allowed[None, None], scores, jnp.float32(-1e30))
    row_peak = jnp.max(masked, axis=-1, keepdims=True)
    weights = jnp.where(allowed[None, None], jnp.exp(masked - row_peak), jnp.float32(0.0))
    row_valid = jnp.any(allowed, axis=1)
    row_total = jnp.sum(weights, axis=-1, keepdims=True) + jnp.where(row_valid, 0.0, 1.0).astype(jnp.float32)[None, None, :, None]
    soft_weights = weights / row_total
    soft_b = lax.optimization_barrier(soft_weights.astype(jnp.bfloat16)).astype(jnp.float32)
    output = jnp.einsum('hgrn,nhd->rhgd', soft_b, value_rank_three)
    row_delta = jnp.sum(gradient_rank_four * output, axis=-1)
    soft_grad = jnp.einsum('rhgd,nhd->hgrn', gradient_rank_four, value_rank_three)
    score_grad = soft_weights * (soft_grad - jnp.transpose(row_delta, (1, 2, 0))[..., None])
    score_grad_b = lax.optimization_barrier(score_grad.astype(jnp.bfloat16)).astype(jnp.float32)
    value_gradient = jnp.einsum('hgrn,rhgd->nhd', soft_b, gradient_rank_four)
    query_gradient = jnp.einsum('hgrn,nhd->rhgd', score_grad_b, key_rank_three) * score_scale
    key_gradient = jnp.einsum('hgrn,rhgd->nhd', score_grad_b, query_rank_four) * score_scale
    return (query_gradient.reshape(row_number, QUERY_HEADS * HEAD_DIM), key_gradient.reshape(key_total, KEY_VALUE_HEADS * HEAD_DIM), value_gradient.reshape(key_total, KEY_VALUE_HEADS * HEAD_DIM))


def reference(prompt_q, prompt_k, prompt_value_rows, prompt_dout, comp_q, completion_keys, completion_values, comp_dout, comp_lengths, prompt_length):
    prompt_count = prompt_length[0]
    prompt_ids = jnp.arange(PROMPT_ROWS)
    allowed_self = (prompt_ids[None, :] <= prompt_ids[:, None]) & (prompt_ids[:, None] < prompt_count)
    self_dq, self_dk, self_dv = attend(prompt_q, prompt_k, prompt_value_rows, prompt_dout, allowed_self)
    step_ids = jnp.arange(COMPLETION_ROWS)
    col_ids = jnp.arange(PROMPT_ROWS + COMPLETION_ROWS)

    def per_sample(sample):
        comp_count = comp_lengths[sample]
        key_matrix = jnp.concatenate([prompt_k, completion_keys[sample]], axis=0)
        value_matrix = jnp.concatenate([prompt_value_rows, completion_values[sample]], axis=0)
        live_rows = step_ids[:, None] < comp_count
        allowed = live_rows & jnp.where(col_ids[None, :] < PROMPT_ROWS, col_ids[None, :] < prompt_count, (col_ids[None, :] - PROMPT_ROWS) <= step_ids[:, None])
        return attend(comp_q[sample], key_matrix, value_matrix, comp_dout[sample], allowed)

    comp_grad_q, key_grads, value_grads = lax.map(per_sample, jnp.arange(SAMPLE_COUNT))
    prompt_grad_k = self_dk + jnp.sum(key_grads[:, :PROMPT_ROWS], axis=0)
    prompt_grad_v = self_dv + jnp.sum(value_grads[:, :PROMPT_ROWS], axis=0)
    return (self_dq.astype(jnp.bfloat16), prompt_grad_k.astype(jnp.bfloat16), prompt_grad_v.astype(jnp.bfloat16), comp_grad_q.astype(jnp.bfloat16), key_grads[:, PROMPT_ROWS:].astype(jnp.bfloat16), value_grads[:, PROMPT_ROWS:].astype(jnp.bfloat16))
```

```python
import functools

import jax
import jax.numpy as jnp
from jax import lax
from jax.experimental import pallas as pl
from jax.experimental.pallas import tpu as pltpu
from jax.sharding import PartitionSpec as P

QUERY_HEADS = 16
KEY_VALUE_HEADS = 4
HEAD_DIM = 128
GROUP = QUERY_HEADS // KEY_VALUE_HEADS
SCALE = HEAD_DIM ** (-0.5)
LOG2E = 1.4426950408889634
CHIPS = 8
CORES = 2
MASKED = -1e30


def dot(a, b, contract):
    return lax.dot_general(a, b, (contract, ((), ())), preferred_element_type=jnp.float32)


NT = ((1,), (1,))
NN = ((1,), (0,))


def head_columns(ref, head):
    parts = [
        ref[:, (head * GROUP + g) * HEAD_DIM : (head * GROUP + g + 1) * HEAD_DIM]
        for g in range(GROUP)
    ]
    return jnp.concatenate(parts, axis=0)


def softmax_terms(scores, valid):
    factor = SCALE * LOG2E
    peak = jnp.max(scores, axis=0, keepdims=True)
    terms = jnp.exp2(scores * factor - peak * factor)
    total = jnp.sum(terms, axis=0, keepdims=True)
    return terms * (valid / total)


def score_gradient(soft, soft_b, soft_grad):
    delta = jnp.sum(soft_b.astype(jnp.float32) * soft_grad, axis=0, keepdims=True)
    return (soft * (soft_grad - delta)).astype(jnp.bfloat16)


def attend_kernel(
    plen_ref,
    clen_ref,
    pq_ref,
    pdo_ref,
    cq_ref,
    cdo_ref,
    ck_ref,
    cv_ref,
    near_ref,
    far_ref,
    pdq_ref,
    cdq_ref,
    cdk_ref,
    cdv_ref,
    part_ref,
    kv_ref,
):
    own = lax.axis_index("sample")
    chip = own // CORES
    core = lax.rem(own, CORES)
    for step in range(CHIPS):
        base = lax.rem(chip + step, CHIPS) * CORES
        kv_ref[base + core] = near_ref[step]
        kv_ref[base + 1 - core] = far_ref[step]
    plen = plen_ref[0]
    clen = clen_ref[0]
    slots = pq_ref.shape[0]
    blocks = kv_ref.shape[0]
    prompt_keys = blocks * slots
    rows = cq_ref.shape[0]
    width = KEY_VALUE_HEADS * HEAD_DIM
    safe = prompt_keys - 32

    row_lane = lax.rem(lax.broadcasted_iota(jnp.int32, (1, GROUP * rows), 1), rows)
    comp_valid = jnp.where(row_lane < clen, 1.0, 0.0).astype(jnp.float32)
    tail_ok = lax.broadcasted_iota(jnp.int32, (32, GROUP * rows), 0) + safe < plen
    own_ok = lax.broadcasted_iota(jnp.int32, (rows, GROUP * rows), 0) <= row_lane
    global_row = (
        lax.rem(lax.broadcasted_iota(jnp.int32, (1, GROUP * slots), 1), slots) + own * slots
    )
    prompt_valid = jnp.where(global_row < plen, 1.0, 0.0).astype(jnp.float32)
    prompt_ok = lax.broadcasted_iota(jnp.int32, (prompt_keys, GROUP * slots), 0) <= global_row

    for head in range(KEY_VALUE_HEADS):
        lower, upper = head * HEAD_DIM, (head + 1) * HEAD_DIM
        pk = kv_ref[:, :, lower:upper].reshape(prompt_keys, HEAD_DIM)
        pv = kv_ref[:, :, width + lower : width + upper].reshape(prompt_keys, HEAD_DIM)
        keys = jnp.concatenate([pk, ck_ref[:, lower:upper]], axis=0)
        values = jnp.concatenate([pv, cv_ref[:, lower:upper]], axis=0)
        q = head_columns(cq_ref, head)
        do = head_columns(cdo_ref, head)
        scores = dot(keys, q, NT)
        scores = jnp.concatenate(
            [
                scores[:safe],
                jnp.where(tail_ok, scores[safe:prompt_keys], MASKED),
                jnp.where(own_ok, scores[prompt_keys:], MASKED),
            ],
            axis=0,
        )
        soft = softmax_terms(scores, comp_valid)
        soft_b = soft.astype(jnp.bfloat16)
        grad_b = score_gradient(soft, soft_b, dot(values, do, NT))

        q_p = head_columns(pq_ref, head)
        do_p = head_columns(pdo_ref, head)
        scores_p = jnp.where(prompt_ok, dot(pk, q_p, NT), MASKED)
        soft_p = softmax_terms(scores_p, prompt_valid)
        soft_pb = soft_p.astype(jnp.bfloat16)
        grad_pb = score_gradient(soft_p, soft_pb, dot(pv, do_p, NT))

        dv = dot(soft_b, do, NN)
        dk = dot(grad_b, q, NN) * SCALE
        dv_p = dv[:prompt_keys] + dot(soft_pb, do_p, NN)
        dk_p = dk[:prompt_keys] + dot(grad_pb, q_p, NN) * SCALE
        part_ref[:, :, lower:upper] = dk_p.astype(jnp.bfloat16).reshape(blocks, slots, HEAD_DIM)
        part_ref[:, :, width + lower : width + upper] = dv_p.astype(jnp.bfloat16).reshape(
            blocks, slots, HEAD_DIM
        )
        cdk_ref[:, lower:upper] = dk[prompt_keys:].astype(jnp.bfloat16)
        cdv_ref[:, lower:upper] = dv[prompt_keys:].astype(jnp.bfloat16)

        dq_t = dot(keys.T, grad_b, NN) * SCALE
        dq_pt = dot(pk.T, grad_pb, NN) * SCALE
        dq_p = dq_pt.T.astype(jnp.bfloat16)
        for g in range(GROUP):
            column = (head * GROUP + g) * HEAD_DIM
            block = dq_t[:, g * rows : (g + 1) * rows]
            cdq_ref[:, column : column + HEAD_DIM] = block.T.astype(jnp.bfloat16)
            pdq_ref[:, column : column + HEAD_DIM] = dq_p[g * slots : (g + 1) * slots]


def total_kernel(terms_ref, dk_ref, dv_ref):
    width = dk_ref.shape[1]
    dk_ref[...] = jnp.sum(terms_ref[:, :, :width].astype(jnp.float32), axis=0).astype(jnp.bfloat16)
    dv_ref[...] = jnp.sum(terms_ref[:, :, width:].astype(jnp.float32), axis=0).astype(jnp.bfloat16)


def attend(prompt_length, comp_lengths, *arrays):
    slots, columns = arrays[0].shape
    rows = arrays[2].shape[0]
    width = KEY_VALUE_HEADS * HEAD_DIM
    blocks = CHIPS * CORES
    bf16 = jnp.bfloat16
    smem = pl.BlockSpec(memory_space=pltpu.SMEM)
    vmem = pl.BlockSpec(memory_space=pltpu.VMEM)
    return pl.pallas_call(
        attend_kernel,
        out_shape=(
            jax.ShapeDtypeStruct((slots, columns), bf16),
            jax.ShapeDtypeStruct((rows, columns), bf16),
            jax.ShapeDtypeStruct((rows, width), bf16),
            jax.ShapeDtypeStruct((rows, width), bf16),
            jax.ShapeDtypeStruct((blocks, slots, 2 * width), bf16),
        ),
        in_specs=[smem, smem] + [vmem] * len(arrays),
        out_specs=(vmem,) * 5,
        scratch_shapes=[pltpu.VMEM((blocks, slots, 2 * width), bf16)],
        compiler_params=pltpu.CompilerParams(vmem_limit_bytes=24 * 1024 * 1024),
        cost_estimate=pl.CostEstimate(
            flops=1_200_000_000, bytes_accessed=4_000_000, transcendentals=850_000
        ),
        name="attend",
    )(prompt_length, comp_lengths, *arrays)


def total(terms):
    _, slots, columns = terms.shape
    vmem = pl.BlockSpec(memory_space=pltpu.VMEM)
    shape = jax.ShapeDtypeStruct((slots, columns // 2), jnp.bfloat16)
    return pl.pallas_call(
        total_kernel,
        out_shape=(shape, shape),
        in_specs=[vmem],
        out_specs=(vmem, vmem),
        compiler_params=pltpu.CompilerParams(vmem_limit_bytes=4 * 1024 * 1024),
        cost_estimate=pl.CostEstimate(flops=600_000, bytes_accessed=560_000, transcendentals=0),
        name="total",
    )(terms)


def body(
    prompt_q,
    prompt_k,
    prompt_value_rows,
    prompt_dout,
    comp_q,
    completion_keys,
    completion_values,
    comp_dout,
    comp_lengths,
    prompt_length,
):
    own = jnp.concatenate([prompt_k, prompt_value_rows], axis=1)
    near = [own]
    for step in range(1, CHIPS):
        pairs = [
            (((y + step) % CHIPS) * CORES + c, y * CORES + c)
            for y in range(CHIPS)
            for c in range(CORES)
        ]
        near.append(lax.ppermute(own, "sample", pairs))
    near = jnp.stack(near)
    swap = [(d, d ^ 1) for d in range(CHIPS * CORES)]
    far = lax.ppermute(near, "sample", swap)
    pdq, cdq, cdk, cdv, part = attend(
        prompt_length,
        comp_lengths,
        prompt_q,
        prompt_dout,
        comp_q[0],
        comp_dout[0],
        completion_keys[0],
        completion_values[0],
        near,
        far,
    )
    terms = lax.all_to_all(part, "sample", split_axis=0, concat_axis=0, tiled=True)
    pdk, pdv = total(terms)
    return (pdq, pdk, pdv, cdq[None], cdk[None], cdv[None])


def solution(mesh):
    rows = P(("prompt", "sample"), None)
    blocks = P(("prompt", "sample"), None, None)
    in_specs = (rows,) * 4 + (blocks,) * 4 + (P(("prompt", "sample")), P("prompt"))
    out_specs = (rows,) * 3 + (blocks,) * 3
    return jax.shard_map(body, mesh=mesh, in_specs=in_specs, out_specs=out_specs, check_vma=False)
```

```python
import functools

import jax
import jax.numpy as jnp
from jax import lax
from jax.experimental import pallas as pl
from jax.experimental.pallas import tpu as pltpu
from jax.sharding import PartitionSpec as P

QUERY_HEADS = 16
KEY_VALUE_HEADS = 4
HEAD_DIM = 128
GROUP = QUERY_HEADS // KEY_VALUE_HEADS
SCALE = HEAD_DIM ** (-0.5)
LOG2E = 1.4426950408889634
CHIPS = 8
CORES = 2
MASKED = -1e30


def dot(a, b, contract):
    return lax.dot_general(a, b, (contract, ((), ())), preferred_element_type=jnp.float32)


NT = ((1,), (1,))
NN = ((1,), (0,))


def head_columns(ref, head):
    parts = [
        ref[:, (head * GROUP + g) * HEAD_DIM : (head * GROUP + g + 1) * HEAD_DIM]
        for g in range(GROUP)
    ]
    return jnp.concatenate(parts, axis=0)


def softmax_terms(scores, valid):
    factor = SCALE * LOG2E
    peak = jnp.max(scores, axis=0, keepdims=True)
    terms = jnp.exp2(scores * factor - peak * factor)
    total = jnp.sum(terms, axis=0, keepdims=True)
    return terms * (valid / total)


def score_gradient(soft, soft_b, soft_grad):
    delta = jnp.sum(soft_b.astype(jnp.float32) * soft_grad, axis=0, keepdims=True)
    return (soft * (soft_grad - delta)).astype(jnp.bfloat16)


def stage_kernel(*refs):
    sources, targets, sems = refs[:8], refs[8:-1], refs[-1]
    key_target, value_target = (
        targets[0].at[:, : sources[0].shape[1]],
        targets[0].at[:, sources[0].shape[1] :],
    )
    copies = [
        pltpu.make_async_copy(source, target, sems.at[n])
        for n, (source, target) in enumerate(
            zip(sources, (key_target, value_target) + tuple(targets[1:]))
        )
    ]
    for copy in copies:
        copy.start()
    for copy in copies:
        copy.wait()


def attend_kernel(
    plen_ref,
    clen_ref,
    pq_ref,
    pdo_ref,
    cq_ref,
    cdo_ref,
    ck_ref,
    cv_ref,
    kv_ref,
    pdq_ref,
    cdq_ref,
    cdk_ref,
    cdv_ref,
    keep_ref,
    send_ref,
):
    own = lax.axis_index("sample")
    first = lax.rem(own, CORES) == 0
    plen = plen_ref[0]
    clen = clen_ref[0]
    slots = pq_ref.shape[0]
    prompt_keys = kv_ref.shape[0]
    rows = cq_ref.shape[0]
    width = KEY_VALUE_HEADS * HEAD_DIM
    safe = prompt_keys - 32

    row_lane = lax.rem(lax.broadcasted_iota(jnp.int32, (1, GROUP * rows), 1), rows)
    comp_valid = jnp.where(row_lane < clen, 1.0, 0.0).astype(jnp.float32)
    tail_ok = lax.broadcasted_iota(jnp.int32, (32, GROUP * rows), 0) + safe < plen
    own_ok = lax.broadcasted_iota(jnp.int32, (rows, GROUP * rows), 0) <= row_lane
    global_row = (
        lax.rem(lax.broadcasted_iota(jnp.int32, (1, GROUP * slots), 1), slots) + own * slots
    )
    prompt_valid = jnp.where(global_row < plen, 1.0, 0.0).astype(jnp.float32)
    prompt_ok = lax.broadcasted_iota(jnp.int32, (prompt_keys, GROUP * slots), 0) <= global_row

    for head in range(KEY_VALUE_HEADS):
        lower, upper = head * HEAD_DIM, (head + 1) * HEAD_DIM
        pk = kv_ref[:, lower:upper]
        pv = kv_ref[:, width + lower : width + upper]
        keys = jnp.concatenate([pk, ck_ref[:, lower:upper]], axis=0)
        values = jnp.concatenate([pv, cv_ref[:, lower:upper]], axis=0)
        q = head_columns(cq_ref, head)
        do = head_columns(cdo_ref, head)
        scores = dot(keys, q, NT)
        scores = jnp.concatenate(
            [
                scores[:safe],
                jnp.where(tail_ok, scores[safe:prompt_keys], MASKED),
                jnp.where(own_ok, scores[prompt_keys:], MASKED),
            ],
            axis=0,
        )
        soft = softmax_terms(scores, comp_valid)
        soft_b = soft.astype(jnp.bfloat16)
        grad_b = score_gradient(soft, soft_b, dot(values, do, NT))

        q_p = head_columns(pq_ref, head)
        do_p = head_columns(pdo_ref, head)
        scores_p = jnp.where(prompt_ok, dot(pk, q_p, NT), MASKED)
        soft_p = softmax_terms(scores_p, prompt_valid)
        soft_pb = soft_p.astype(jnp.bfloat16)
        grad_pb = score_gradient(soft_p, soft_pb, dot(pv, do_p, NT))

        dv = dot(soft_b, do, NN)
        dk = dot(grad_b, q, NN) * SCALE
        dv_p = dv[:prompt_keys] + dot(soft_pb, do_p, NN)
        dk_p = dk[:prompt_keys] + dot(grad_pb, q_p, NN) * SCALE
        dk_p = dk_p.reshape(CHIPS, CORES, slots, HEAD_DIM)
        dv_p = dv_p.reshape(CHIPS, CORES, slots, HEAD_DIM)
        for start, grad in ((lower, dk_p), (width + lower, dv_p)):
            keep_ref[:, :, start : start + HEAD_DIM] = jnp.where(first, grad[:, 0], grad[:, 1])
            send_ref[:, :, start : start + HEAD_DIM] = jnp.where(first, grad[:, 1], grad[:, 0])
        cdk_ref[:, lower:upper] = dk[prompt_keys:].astype(jnp.bfloat16)
        cdv_ref[:, lower:upper] = dv[prompt_keys:].astype(jnp.bfloat16)

        dq_t = dot(keys.T, grad_b, NN) * SCALE
        dq_pt = dot(pk.T, grad_pb, NN) * SCALE
        dq_p = dq_pt.T.astype(jnp.bfloat16)
        for g in range(GROUP):
            column = (head * GROUP + g) * HEAD_DIM
            block = dq_t[:, g * rows : (g + 1) * rows]
            cdq_ref[:, column : column + HEAD_DIM] = block.T.astype(jnp.bfloat16)
            pdq_ref[:, column : column + HEAD_DIM] = dq_p[g * slots : (g + 1) * slots]


def pair_kernel(keep_ref, came_ref, sum_ref):
    sum_ref[...] = (keep_ref[...] + came_ref[...]).astype(jnp.bfloat16)


def total_kernel(terms_ref, dk_ref, dv_ref):
    width = dk_ref.shape[1]
    dk_ref[...] = jnp.sum(terms_ref[:, :, :width].astype(jnp.float32), axis=0).astype(jnp.bfloat16)
    dv_ref[...] = jnp.sum(terms_ref[:, :, width:].astype(jnp.float32), axis=0).astype(jnp.bfloat16)


def attend(prompt_length, comp_lengths, *arrays):
    slots, columns = arrays[0].shape
    rows = arrays[2].shape[0]
    width = KEY_VALUE_HEADS * HEAD_DIM
    bf16 = jnp.bfloat16
    smem = pl.BlockSpec(memory_space=pltpu.SMEM)
    vmem = pl.BlockSpec(memory_space=pltpu.VMEM)
    return pl.pallas_call(
        attend_kernel,
        out_shape=(
            jax.ShapeDtypeStruct((slots, columns), bf16),
            jax.ShapeDtypeStruct((rows, columns), bf16),
            jax.ShapeDtypeStruct((rows, width), bf16),
            jax.ShapeDtypeStruct((rows, width), bf16),
            jax.ShapeDtypeStruct((CHIPS, slots, 2 * width), jnp.float32),
            jax.ShapeDtypeStruct((CHIPS, slots, 2 * width), jnp.float32),
        ),
        in_specs=[smem, smem] + [vmem] * len(arrays),
        out_specs=(vmem,) * 6,
        compiler_params=pltpu.CompilerParams(vmem_limit_bytes=24 * 1024 * 1024),
        cost_estimate=pl.CostEstimate(
            flops=1_200_000_000, bytes_accessed=4_000_000, transcendentals=850_000
        ),
        name="attend",
    )(prompt_length, comp_lengths, *arrays)


def stage(keys, values, *rest):
    shapes = [(keys.shape[0], 2 * keys.shape[1])] + [a.shape for a in rest]
    return pl.pallas_call(
        stage_kernel,
        out_shape=tuple(jax.ShapeDtypeStruct(shape, keys.dtype) for shape in shapes),
        in_specs=[pl.BlockSpec(memory_space=pl.ANY)] * (2 + len(rest)),
        out_specs=(pl.BlockSpec(memory_space=pltpu.VMEM),) * len(shapes),
        scratch_shapes=[pltpu.SemaphoreType.DMA((2 + len(rest),))],
        compiler_params=pltpu.CompilerParams(vmem_limit_bytes=8 * 1024 * 1024),
        cost_estimate=pl.CostEstimate(flops=0, bytes_accessed=2_800_000, transcendentals=0),
        name="stage",
    )(*[pltpu.with_memory_space_constraint(a, pltpu.HBM) for a in (keys, values, *rest)])


def pair_sum(keep, came):
    vmem = pl.BlockSpec(memory_space=pltpu.VMEM)
    return pl.pallas_call(
        pair_kernel,
        out_shape=jax.ShapeDtypeStruct(keep.shape, jnp.bfloat16),
        in_specs=[vmem, vmem],
        out_specs=vmem,
        compiler_params=pltpu.CompilerParams(vmem_limit_bytes=8 * 1024 * 1024),
        cost_estimate=pl.CostEstimate(flops=140_000, bytes_accessed=1_300_000, transcendentals=0),
        name="pair_sum",
    )(keep, came)


def total(terms):
    _, slots, columns = terms.shape
    vmem = pl.BlockSpec(memory_space=pltpu.VMEM)
    shape = jax.ShapeDtypeStruct((slots, columns // 2), jnp.bfloat16)
    return pl.pallas_call(
        total_kernel,
        out_shape=(shape, shape),
        in_specs=[vmem],
        out_specs=(vmem, vmem),
        compiler_params=pltpu.CompilerParams(vmem_limit_bytes=4 * 1024 * 1024),
        cost_estimate=pl.CostEstimate(flops=600_000, bytes_accessed=560_000, transcendentals=0),
        name="total",
    )(terms)


def body(
    prompt_q,
    prompt_k,
    prompt_value_rows,
    prompt_dout,
    comp_q,
    completion_keys,
    completion_values,
    comp_dout,
    comp_lengths,
    prompt_length,
):
    own, *staged = stage(
        prompt_k,
        prompt_value_rows,
        prompt_q,
        prompt_dout,
        comp_q[0],
        comp_dout[0],
        completion_keys[0],
        completion_values[0],
    )
    gathered = lax.all_gather(own, "sample", axis=0, tiled=True)
    pdq, cdq, cdk, cdv, keep, send = attend(prompt_length, comp_lengths, *staged, gathered)
    swap = [(d, d ^ 1) for d in range(CHIPS * CORES)]
    came = lax.ppermute(send, "sample", swap)
    same_core = [[y * CORES + c for y in range(CHIPS)] for c in range(CORES)]
    terms = lax.all_to_all(
        pair_sum(keep, came),
        "sample",
        split_axis=0,
        concat_axis=0,
        axis_index_groups=same_core,
        tiled=True,
    )
    pdk, pdv = total(terms)
    return (pdq, pdk, pdv, cdq[None], cdk[None], cdv[None])


def solution(mesh):
    rows = P(("prompt", "sample"), None)
    blocks = P(("prompt", "sample"), None, None)
    in_specs = (rows,) * 4 + (blocks,) * 4 + (P(("prompt", "sample")), P("prompt"))
    out_specs = (rows,) * 3 + (blocks,) * 3
    return jax.shard_map(body, mesh=mesh, in_specs=in_specs, out_specs=out_specs, check_vma=False)
```

```python
import functools

import jax
import jax.numpy as jnp
from jax import lax
from jax.experimental import pallas as pl
from jax.experimental.pallas import tpu as pltpu
from jax.sharding import PartitionSpec as P

QUERY_HEADS = 16
KEY_VALUE_HEADS = 4
HEAD_DIM = 128
GROUP = QUERY_HEADS // KEY_VALUE_HEADS
SCALE = HEAD_DIM ** (-0.5)
LOG2E = 1.4426950408889634
CHIPS = 8
CORES = 2
MASKED = -1e30


def dot(a, b, contract):
    return lax.dot_general(a, b, (contract, ((), ())), preferred_element_type=jnp.float32)


NT = ((1,), (1,))
NN = ((1,), (0,))


def head_columns(ref, head):
    parts = [
        ref[:, (head * GROUP + g) * HEAD_DIM : (head * GROUP + g + 1) * HEAD_DIM]
        for g in range(GROUP)
    ]
    return jnp.concatenate(parts, axis=0)


def softmax_terms(scores, valid):
    factor = SCALE * LOG2E
    peak = jnp.max(scores, axis=0, keepdims=True)
    terms = jnp.exp2(scores * factor - peak * factor)
    total = jnp.sum(terms, axis=0, keepdims=True)
    return terms * (valid / total)


def score_gradient(soft, soft_b, soft_grad):
    delta = jnp.sum(soft_b.astype(jnp.float32) * soft_grad, axis=0, keepdims=True)
    return (soft * (soft_grad - delta)).astype(jnp.bfloat16)


def stage_kernel(*refs):
    sources, targets, sems = refs[:8], refs[8:-1], refs[-1]
    key_target, value_target = (
        targets[0].at[:, : sources[0].shape[1]],
        targets[0].at[:, sources[0].shape[1] :],
    )
    copies = [
        pltpu.make_async_copy(source, target, sems.at[n])
        for n, (source, target) in enumerate(
            zip(sources, (key_target, value_target) + tuple(targets[1:]))
        )
    ]
    for copy in copies:
        copy.start()
    for copy in copies:
        copy.wait()


def attend_kernel(
    plen_ref,
    clen_ref,
    pq_ref,
    pdo_ref,
    cq_ref,
    cdo_ref,
    ck_ref,
    cv_ref,
    near_ref,
    far_ref,
    pdq_ref,
    cdq_ref,
    cdk_ref,
    cdv_ref,
    keep_ref,
    send_ref,
):
    own = lax.axis_index("sample")
    core = lax.rem(own, CORES)
    plen = plen_ref[0]
    clen = clen_ref[0]
    slots = pq_ref.shape[0]
    half = near_ref.shape[0]
    prompt_keys = 2 * half
    rows = cq_ref.shape[0]
    width = KEY_VALUE_HEADS * HEAD_DIM
    safe = half - slots

    def positions(first_row, count, lanes, other):
        row = lax.broadcasted_iota(jnp.int32, (count, lanes), 0) + first_row
        side = lax.rem(core + other, CORES)
        return row // slots * (CORES * slots) + side * slots + lax.rem(row, slots)


    row_lane = lax.rem(lax.broadcasted_iota(jnp.int32, (1, GROUP * rows), 1), rows)
    comp_valid = jnp.where(row_lane < clen, 1.0, 0.0).astype(jnp.float32)
    near_ok = positions(safe, slots, GROUP * rows, 0) < plen
    far_ok = positions(safe, slots, GROUP * rows, 1) < plen
    own_ok = lax.broadcasted_iota(jnp.int32, (rows, GROUP * rows), 0) <= row_lane
    global_row = (
        lax.rem(lax.broadcasted_iota(jnp.int32, (1, GROUP * slots), 1), slots) + own * slots
    )
    prompt_valid = jnp.where(global_row < plen, 1.0, 0.0).astype(jnp.float32)
    prompt_ok = jnp.concatenate(
        [positions(0, half, GROUP * slots, other) <= global_row for other in range(CORES)], axis=0
    )

    for head in range(KEY_VALUE_HEADS):
        lower, upper = head * HEAD_DIM, (head + 1) * HEAD_DIM
        pk = jnp.concatenate([near_ref[:, lower:upper], far_ref[:, lower:upper]], axis=0)
        pv = jnp.concatenate(
            [ref[:, width + lower : width + upper] for ref in (near_ref, far_ref)], axis=0
        )
        keys = jnp.concatenate([pk, ck_ref[:, lower:upper]], axis=0)
        values = jnp.concatenate([pv, cv_ref[:, lower:upper]], axis=0)
        q = head_columns(cq_ref, head)
        do = head_columns(cdo_ref, head)
        scores = dot(keys, q, NT)
        scores = jnp.concatenate(
            [
                scores[:safe],
                jnp.where(near_ok, scores[safe:half], MASKED),
                scores[half : half + safe],
                jnp.where(far_ok, scores[half + safe : prompt_keys], MASKED),
                jnp.where(own_ok, scores[prompt_keys:], MASKED),
            ],
            axis=0,
        )
        soft = softmax_terms(scores, comp_valid)
        soft_b = soft.astype(jnp.bfloat16)
        grad_b = score_gradient(soft, soft_b, dot(values, do, NT))

        q_p = head_columns(pq_ref, head)
        do_p = head_columns(pdo_ref, head)
        scores_p = jnp.where(prompt_ok, dot(pk, q_p, NT), MASKED)
        soft_p = softmax_terms(scores_p, prompt_valid)
        soft_pb = soft_p.astype(jnp.bfloat16)
        grad_pb = score_gradient(soft_p, soft_pb, dot(pv, do_p, NT))

        dv = dot(soft_b, do, NN)
        dk = dot(grad_b, q, NN) * SCALE
        dv_p = dv[:prompt_keys] + dot(soft_pb, do_p, NN)
        dk_p = dk[:prompt_keys] + dot(grad_pb, q_p, NN) * SCALE
        for start, grad in ((lower, dk_p), (width + lower, dv_p)):
            keep_ref[:, start : start + HEAD_DIM] = grad[:half]
            send_ref[:, start : start + HEAD_DIM] = grad[half:]
        cdk_ref[:, lower:upper] = dk[prompt_keys:].astype(jnp.bfloat16)
        cdv_ref[:, lower:upper] = dv[prompt_keys:].astype(jnp.bfloat16)

        dq_t = dot(keys.T, grad_b, NN) * SCALE
        dq_pt = dot(pk.T, grad_pb, NN) * SCALE
        dq_p = dq_pt.T.astype(jnp.bfloat16)
        for g in range(GROUP):
            column = (head * GROUP + g) * HEAD_DIM
            block = dq_t[:, g * rows : (g + 1) * rows]
            cdq_ref[:, column : column + HEAD_DIM] = block.T.astype(jnp.bfloat16)
            pdq_ref[:, column : column + HEAD_DIM] = dq_p[g * slots : (g + 1) * slots]


def pair_kernel(keep_ref, came_ref, sum_ref):
    sum_ref[...] = keep_ref[...] + came_ref[...]


def total_kernel(terms_ref, dk_ref, dv_ref):
    width = dk_ref.shape[1]
    dk_ref[...] = terms_ref[:, :width].astype(jnp.bfloat16)
    dv_ref[...] = terms_ref[:, width:].astype(jnp.bfloat16)


def attend(prompt_length, comp_lengths, *arrays):
    slots, columns = arrays[0].shape
    rows = arrays[2].shape[0]
    width = KEY_VALUE_HEADS * HEAD_DIM
    bf16 = jnp.bfloat16
    smem = pl.BlockSpec(memory_space=pltpu.SMEM)
    vmem = pl.BlockSpec(memory_space=pltpu.VMEM)
    return pl.pallas_call(
        attend_kernel,
        out_shape=(
            jax.ShapeDtypeStruct((slots, columns), bf16),
            jax.ShapeDtypeStruct((rows, columns), bf16),
            jax.ShapeDtypeStruct((rows, width), bf16),
            jax.ShapeDtypeStruct((rows, width), bf16),
            jax.ShapeDtypeStruct((CHIPS * slots, 2 * width), jnp.float32),
            jax.ShapeDtypeStruct((CHIPS * slots, 2 * width), jnp.float32),
        ),
        in_specs=[smem, smem] + [vmem] * len(arrays),
        out_specs=(vmem,) * 6,
        compiler_params=pltpu.CompilerParams(vmem_limit_bytes=24 * 1024 * 1024),
        cost_estimate=pl.CostEstimate(
            flops=1_200_000_000, bytes_accessed=4_000_000, transcendentals=850_000
        ),
        name="attend",
    )(prompt_length, comp_lengths, *arrays)


def stage(keys, values, *rest):
    shapes = [(keys.shape[0], 2 * keys.shape[1])] + [a.shape for a in rest]
    return pl.pallas_call(
        stage_kernel,
        out_shape=tuple(jax.ShapeDtypeStruct(shape, keys.dtype) for shape in shapes),
        in_specs=[pl.BlockSpec(memory_space=pl.ANY)] * (2 + len(rest)),
        out_specs=(pl.BlockSpec(memory_space=pltpu.VMEM),) * len(shapes),
        scratch_shapes=[pltpu.SemaphoreType.DMA((2 + len(rest),))],
        compiler_params=pltpu.CompilerParams(vmem_limit_bytes=8 * 1024 * 1024),
        cost_estimate=pl.CostEstimate(flops=0, bytes_accessed=2_800_000, transcendentals=0),
        name="stage",
    )(*[pltpu.with_memory_space_constraint(a, pltpu.HBM) for a in (keys, values, *rest)])


def pair_sum(keep, came):
    vmem = pl.BlockSpec(memory_space=pltpu.VMEM)
    return pl.pallas_call(
        pair_kernel,
        out_shape=jax.ShapeDtypeStruct(keep.shape, keep.dtype),
        in_specs=[vmem, vmem],
        out_specs=vmem,
        compiler_params=pltpu.CompilerParams(vmem_limit_bytes=8 * 1024 * 1024),
        cost_estimate=pl.CostEstimate(flops=140_000, bytes_accessed=1_300_000, transcendentals=0),
        name="pair_sum",
    )(keep, came)


def total(terms):
    slots, columns = terms.shape
    vmem = pl.BlockSpec(memory_space=pltpu.VMEM)
    shape = jax.ShapeDtypeStruct((slots, columns // 2), jnp.bfloat16)
    return pl.pallas_call(
        total_kernel,
        out_shape=(shape, shape),
        in_specs=[vmem],
        out_specs=(vmem, vmem),
        compiler_params=pltpu.CompilerParams(vmem_limit_bytes=4 * 1024 * 1024),
        cost_estimate=pl.CostEstimate(flops=600_000, bytes_accessed=560_000, transcendentals=0),
        name="total",
    )(terms)


def body(
    prompt_q,
    prompt_k,
    prompt_value_rows,
    prompt_dout,
    comp_q,
    completion_keys,
    completion_values,
    comp_dout,
    comp_lengths,
    prompt_length,
):
    own, *staged = stage(
        prompt_k,
        prompt_value_rows,
        prompt_q,
        prompt_dout,
        comp_q[0],
        comp_dout[0],
        completion_keys[0],
        completion_values[0],
    )
    swap = [(d, d ^ 1) for d in range(CHIPS * CORES)]
    same_core = [[y * CORES + c for y in range(CHIPS)] for c in range(CORES)]
    near = lax.all_gather(own, "sample", axis=0, axis_index_groups=same_core, tiled=True)
    far = lax.ppermute(near, "sample", swap)
    pdq, cdq, cdk, cdv, keep, send = attend(prompt_length, comp_lengths, *staged, near, far)
    came = lax.ppermute(send, "sample", swap)
    terms = lax.psum_scatter(
        pair_sum(keep, came),
        "sample",
        scatter_dimension=0,
        axis_index_groups=same_core,
        tiled=True,
    )
    pdk, pdv = total(terms)
    return (pdq, pdk, pdv, cdq[None], cdk[None], cdv[None])


def solution(mesh):
    rows = P(("prompt", "sample"), None)
    blocks = P(("prompt", "sample"), None, None)
    in_specs = (rows,) * 4 + (blocks,) * 4 + (P(("prompt", "sample")), P("prompt"))
    out_specs = (rows,) * 3 + (blocks,) * 3
    return jax.shard_map(body, mesh=mesh, in_specs=in_specs, out_specs=out_specs, check_vma=False)
```

```python
import functools

import jax
import jax.numpy as jnp
from jax import lax
from jax.experimental import pallas as pl
from jax.experimental.pallas import tpu as pltpu
from jax.sharding import PartitionSpec as P

QUERY_HEADS = 16
KEY_VALUE_HEADS = 4
HEAD_DIM = 128
GROUP = QUERY_HEADS // KEY_VALUE_HEADS
SCALE = HEAD_DIM ** (-0.5)
LOG2E = 1.4426950408889634
CHIPS = 8
CORES = 2
MASKED = -1e30


def dot(a, b, contract):
    return lax.dot_general(a, b, (contract, ((), ())), preferred_element_type=jnp.float32)


NT = ((1,), (1,))
NN = ((1,), (0,))


def head_columns(ref, head):
    parts = [
        ref[:, (head * GROUP + g) * HEAD_DIM : (head * GROUP + g + 1) * HEAD_DIM]
        for g in range(GROUP)
    ]
    return jnp.concatenate(parts, axis=0)


def softmax_terms(scores, valid):
    factor = SCALE * LOG2E
    peak = jnp.max(scores, axis=0, keepdims=True)
    terms = jnp.exp2(scores * factor - peak * factor)
    total = jnp.sum(terms, axis=0, keepdims=True)
    return terms * (valid / total)


def score_gradient(soft, soft_b, soft_grad):
    delta = jnp.sum(soft_b.astype(jnp.float32) * soft_grad, axis=0, keepdims=True)
    return (soft * (soft_grad - delta)).astype(jnp.bfloat16)


def stage_kernel(*refs):
    sources, targets, sems = refs[:8], refs[8:-1], refs[-1]
    key_target, value_target = (
        targets[0].at[:, : sources[0].shape[1]],
        targets[0].at[:, sources[0].shape[1] :],
    )
    copies = [
        pltpu.make_async_copy(source, target, sems.at[n])
        for n, (source, target) in enumerate(
            zip(sources, (key_target, value_target) + tuple(targets[1:]))
        )
    ]
    for copy in copies:
        copy.start()
    for copy in copies:
        copy.wait()


def attend_kernel(
    plen_ref,
    clen_ref,
    pq_ref,
    pdo_ref,
    cq_ref,
    cdo_ref,
    ck_ref,
    cv_ref,
    kv_ref,
    keep_ref,
    send_ref,
    soft_ref,
    grad_ref,
    prompt_grad_ref,
):
    own = lax.axis_index("sample")
    core = lax.rem(own, CORES)
    plen = plen_ref[0]
    clen = clen_ref[0]
    slots = pq_ref.shape[0]
    half = CHIPS * slots
    prompt_keys = CORES * half
    rows = cq_ref.shape[0]
    width = KEY_VALUE_HEADS * HEAD_DIM
    safe = half - slots

    def positions(first_row, count, lanes, other):
        row = lax.broadcasted_iota(jnp.int32, (count, lanes), 0) + first_row
        side = lax.rem(core + other, CORES)
        return row // slots * (CORES * slots) + side * slots + lax.rem(row, slots)

    row_lane = lax.rem(lax.broadcasted_iota(jnp.int32, (1, GROUP * rows), 1), rows)
    comp_valid = jnp.where(row_lane < clen, 1.0, 0.0).astype(jnp.float32)
    near_ok = positions(safe, slots, GROUP * rows, 0) < plen
    far_ok = positions(safe, slots, GROUP * rows, 1) < plen
    own_ok = lax.broadcasted_iota(jnp.int32, (rows, GROUP * rows), 0) <= row_lane
    global_row = (
        lax.rem(lax.broadcasted_iota(jnp.int32, (1, GROUP * slots), 1), slots) + own * slots
    )
    prompt_valid = jnp.where(global_row < plen, 1.0, 0.0).astype(jnp.float32)
    prompt_ok = jnp.concatenate(
        [positions(0, half, GROUP * slots, other) <= global_row for other in range(CORES)], axis=0
    )

    for head in range(KEY_VALUE_HEADS):
        lower, upper = head * HEAD_DIM, (head + 1) * HEAD_DIM
        pk = prompt_head(kv_ref, core, lower)
        pv = prompt_head(kv_ref, core, width + lower)
        keys = jnp.concatenate([pk, ck_ref[:, lower:upper]], axis=0)
        values = jnp.concatenate([pv, cv_ref[:, lower:upper]], axis=0)
        q = head_columns(cq_ref, head)
        do = head_columns(cdo_ref, head)
        scores = dot(keys, q, NT)
        scores = jnp.concatenate(
            [
                scores[:safe],
                jnp.where(near_ok, scores[safe:half], MASKED),
                scores[half : half + safe],
                jnp.where(far_ok, scores[half + safe : prompt_keys], MASKED),
                jnp.where(own_ok, scores[prompt_keys:], MASKED),
            ],
            axis=0,
        )
        soft = softmax_terms(scores, comp_valid)
        soft_b = soft.astype(jnp.bfloat16)
        grad_b = score_gradient(soft, soft_b, dot(values, do, NT))

        q_p = head_columns(pq_ref, head)
        do_p = head_columns(pdo_ref, head)
        scores_p = jnp.where(prompt_ok, dot(pk, q_p, NT), MASKED)
        soft_p = softmax_terms(scores_p, prompt_valid)
        soft_pb = soft_p.astype(jnp.bfloat16)
        grad_pb = score_gradient(soft_p, soft_pb, dot(pv, do_p, NT))

        dv = dot(soft_b[:prompt_keys], do, NN) + dot(soft_pb, do_p, NN)
        dk = (dot(grad_b[:prompt_keys], q, NN) + dot(grad_pb, q_p, NN)) * SCALE
        for start, grad in ((lower, dk), (width + lower, dv)):
            keep_ref[:, start : start + HEAD_DIM] = grad[:half]
            send_ref[:, start : start + HEAD_DIM] = grad[half:]
        soft_ref[head] = soft_b[prompt_keys:]
        grad_ref[head] = grad_b
        prompt_grad_ref[head] = grad_pb


def prompt_head(kv_ref, core, lower):
    return jnp.concatenate(
        [
            kv_ref[:, lax.rem(core + other, CORES), :, lower : lower + HEAD_DIM].reshape(
                -1, HEAD_DIM
            )
            for other in range(CORES)
        ],
        axis=0,
    )


def grads_kernel(
    cq_ref,
    cdo_ref,
    ck_ref,
    kv_ref,
    soft_ref,
    grad_ref,
    prompt_grad_ref,
    pdq_ref,
    cdq_ref,
    cdk_ref,
    cdv_ref,
):
    core = lax.rem(lax.axis_index("sample"), CORES)
    slots = pdq_ref.shape[0]
    rows = cq_ref.shape[0]
    for head in range(KEY_VALUE_HEADS):
        lower, upper = head * HEAD_DIM, (head + 1) * HEAD_DIM
        pk = prompt_head(kv_ref, core, lower)
        prompt_keys = pk.shape[0]
        keys = jnp.concatenate([pk, ck_ref[:, lower:upper]], axis=0)
        grad_b = grad_ref[head]
        own_dv = dot(soft_ref[head], head_columns(cdo_ref, head), NN)
        own_dk = dot(grad_b[prompt_keys:], head_columns(cq_ref, head), NN) * SCALE
        cdk_ref[:, lower:upper] = own_dk.astype(jnp.bfloat16)
        cdv_ref[:, lower:upper] = own_dv.astype(jnp.bfloat16)
        dq_t = dot(keys.T, grad_b, NN) * SCALE
        dq_pt = dot(pk.T, prompt_grad_ref[head], NN) * SCALE
        dq_p = dq_pt.T.astype(jnp.bfloat16)
        for g in range(GROUP):
            column = (head * GROUP + g) * HEAD_DIM
            block = dq_t[:, g * rows : (g + 1) * rows]
            cdq_ref[:, column : column + HEAD_DIM] = block.T.astype(jnp.bfloat16)
            pdq_ref[:, column : column + HEAD_DIM] = dq_p[g * slots : (g + 1) * slots]


def pair_kernel(keep_ref, came_ref, sum_ref):
    sum_ref[...] = (keep_ref[...] + came_ref[...]).astype(jnp.bfloat16)


def total_kernel(terms_ref, dk_ref, dv_ref):
    width = dk_ref.shape[1]
    dk_ref[...] = jnp.sum(terms_ref[:, :, :width].astype(jnp.float32), axis=0).astype(jnp.bfloat16)
    dv_ref[...] = jnp.sum(terms_ref[:, :, width:].astype(jnp.float32), axis=0).astype(jnp.bfloat16)


def attend(prompt_length, comp_lengths, *arrays):
    slots = arrays[0].shape[0]
    rows = arrays[2].shape[0]
    half = CHIPS * slots
    width = KEY_VALUE_HEADS * HEAD_DIM
    smem = pl.BlockSpec(memory_space=pltpu.SMEM)
    vmem = pl.BlockSpec(memory_space=pltpu.VMEM)
    heads, lanes = KEY_VALUE_HEADS, GROUP * rows
    return pl.pallas_call(
        attend_kernel,
        out_shape=(
            jax.ShapeDtypeStruct((half, 2 * width), jnp.float32),
            jax.ShapeDtypeStruct((half, 2 * width), jnp.float32),
            jax.ShapeDtypeStruct((heads, rows, lanes), jnp.bfloat16),
            jax.ShapeDtypeStruct((heads, CORES * half + rows, lanes), jnp.bfloat16),
            jax.ShapeDtypeStruct((heads, CORES * half, GROUP * slots), jnp.bfloat16),
        ),
        in_specs=[smem, smem] + [vmem] * len(arrays),
        out_specs=(vmem,) * 5,
        compiler_params=pltpu.CompilerParams(vmem_limit_bytes=24 * 1024 * 1024),
        cost_estimate=pl.CostEstimate(
            flops=1_000_000_000, bytes_accessed=4_000_000, transcendentals=850_000
        ),
        name="attend",
    )(prompt_length, comp_lengths, *arrays)


def grads(slots, *arrays):
    rows, columns = arrays[0].shape
    width = KEY_VALUE_HEADS * HEAD_DIM
    vmem = pl.BlockSpec(memory_space=pltpu.VMEM)
    shapes = ((slots, columns), (rows, columns), (rows, width), (rows, width))
    return pl.pallas_call(
        grads_kernel,
        out_shape=tuple(jax.ShapeDtypeStruct(shape, jnp.bfloat16) for shape in shapes),
        in_specs=[vmem] * len(arrays),
        out_specs=(vmem,) * len(shapes),
        compiler_params=pltpu.CompilerParams(vmem_limit_bytes=16 * 1024 * 1024),
        cost_estimate=pl.CostEstimate(
            flops=350_000_000, bytes_accessed=4_000_000, transcendentals=0
        ),
        name="grads",
    )(*arrays)


def stage(keys, values, *rest):
    shapes = [(keys.shape[0], 2 * keys.shape[1])] + [a.shape for a in rest]
    return pl.pallas_call(
        stage_kernel,
        out_shape=tuple(jax.ShapeDtypeStruct(shape, keys.dtype) for shape in shapes),
        in_specs=[pl.BlockSpec(memory_space=pl.ANY)] * (2 + len(rest)),
        out_specs=(pl.BlockSpec(memory_space=pltpu.VMEM),) * len(shapes),
        scratch_shapes=[pltpu.SemaphoreType.DMA((2 + len(rest),))],
        compiler_params=pltpu.CompilerParams(vmem_limit_bytes=8 * 1024 * 1024),
        cost_estimate=pl.CostEstimate(flops=0, bytes_accessed=2_800_000, transcendentals=0),
        name="stage",
    )(*[pltpu.with_memory_space_constraint(a, pltpu.HBM) for a in (keys, values, *rest)])


def pair_sum(keep, came):
    vmem = pl.BlockSpec(memory_space=pltpu.VMEM)
    return pl.pallas_call(
        pair_kernel,
        out_shape=jax.ShapeDtypeStruct(keep.shape, jnp.bfloat16),
        in_specs=[vmem, vmem],
        out_specs=vmem,
        compiler_params=pltpu.CompilerParams(vmem_limit_bytes=8 * 1024 * 1024),
        cost_estimate=pl.CostEstimate(flops=140_000, bytes_accessed=1_300_000, transcendentals=0),
        name="pair_sum",
    )(keep, came)


def total(terms):
    _, slots, columns = terms.shape
    vmem = pl.BlockSpec(memory_space=pltpu.VMEM)
    shape = jax.ShapeDtypeStruct((slots, columns // 2), jnp.bfloat16)
    return pl.pallas_call(
        total_kernel,
        out_shape=(shape, shape),
        in_specs=[vmem],
        out_specs=(vmem, vmem),
        compiler_params=pltpu.CompilerParams(vmem_limit_bytes=4 * 1024 * 1024),
        cost_estimate=pl.CostEstimate(flops=600_000, bytes_accessed=560_000, transcendentals=0),
        name="total",
    )(terms)


def body(
    prompt_q,
    prompt_k,
    prompt_value_rows,
    prompt_dout,
    comp_q,
    completion_keys,
    completion_values,
    comp_dout,
    comp_lengths,
    prompt_length,
):
    own, *staged = stage(
        prompt_k,
        prompt_value_rows,
        prompt_q,
        prompt_dout,
        comp_q[0],
        comp_dout[0],
        completion_keys[0],
        completion_values[0],
    )
    pq, pdo, cq, cdo, ck, cv = staged
    swap = [(d, d ^ 1) for d in range(CHIPS * CORES)]
    same_core = [[y * CORES + c for y in range(CHIPS)] for c in range(CORES)]
    kv = lax.all_gather(own, "sample", axis=0, tiled=False)
    kv = kv.reshape(CHIPS, CORES, *own.shape)
    keep, send, soft, grad, prompt_grad = attend(
        prompt_length, comp_lengths, pq, pdo, cq, cdo, ck, cv, kv
    )
    came = lax.ppermute(send, "sample", swap)
    pdq, cdq, cdk, cdv = grads(pq.shape[0], cq, cdo, ck, kv, soft, grad, prompt_grad)
    partial = pair_sum(keep, came).reshape(CHIPS, *own.shape)
    terms = lax.all_to_all(
        partial, "sample", split_axis=0, concat_axis=0, axis_index_groups=same_core, tiled=True
    )
    pdk, pdv = total(terms)
    return (pdq, pdk, pdv, cdq[None], cdk[None], cdv[None])


def solution(mesh):
    rows = P(("prompt", "sample"), None)
    blocks = P(("prompt", "sample"), None, None)
    in_specs = (rows,) * 4 + (blocks,) * 4 + (P(("prompt", "sample")), P("prompt"))
    out_specs = (rows,) * 3 + (blocks,) * 3
    return jax.shard_map(body, mesh=mesh, in_specs=in_specs, out_specs=out_specs, check_vma=False)
```

```python
import functools

import jax
import jax.numpy as jnp
from jax import lax
from jax.experimental import pallas as pl
from jax.experimental.pallas import tpu as pltpu
from jax.sharding import PartitionSpec as P

QUERY_HEADS = 16
KEY_VALUE_HEADS = 4
HEAD_DIM = 128
GROUP = QUERY_HEADS // KEY_VALUE_HEADS
SCALE = HEAD_DIM ** (-0.5)
LOG2E = 1.4426950408889634
CHIPS = 8
CORES = 2
MASKED = -1e30


def dot(a, b, contract):
    return lax.dot_general(a, b, (contract, ((), ())), preferred_element_type=jnp.float32)


NT = ((1,), (1,))
NN = ((1,), (0,))


def head_columns(ref, head):
    parts = [
        ref[:, (head * GROUP + g) * HEAD_DIM : (head * GROUP + g + 1) * HEAD_DIM]
        for g in range(GROUP)
    ]
    return jnp.concatenate(parts, axis=0)


def prompt_head(kv_ref, core, lower):
    return jnp.concatenate(
        [
            kv_ref[:, lax.rem(core + other, CORES), :, lower : lower + HEAD_DIM].reshape(
                -1, HEAD_DIM
            )
            for other in range(CORES)
        ],
        axis=0,
    )


def softmax_terms(scores, valid):
    factor = SCALE * LOG2E
    peak = jnp.max(scores, axis=0, keepdims=True)
    terms = jnp.exp2(scores * factor - peak * factor)
    total = jnp.sum(terms, axis=0, keepdims=True)
    return terms * (valid / total)


def score_gradient(soft, soft_b, soft_grad):
    delta = jnp.sum(soft_b.astype(jnp.float32) * soft_grad, axis=0, keepdims=True)
    return (soft * (soft_grad - delta)).astype(jnp.bfloat16)


class Attention:
    def __init__(self, plen, clen, pq_ref, pdo_ref, cq_ref, cdo_ref, ck_ref, cv_ref, kv_ref):
        self.refs = pq_ref, pdo_ref, cq_ref, cdo_ref, ck_ref, cv_ref, kv_ref
        own = lax.axis_index("sample")
        core = self.core = lax.rem(own, CORES)
        slots = self.slots = pq_ref.shape[0]
        rows = self.rows = cq_ref.shape[0]
        half = self.half = CHIPS * slots
        safe = self.safe = half - slots

        def positions(first_row, count, lanes, other):
            row = lax.broadcasted_iota(jnp.int32, (count, lanes), 0) + first_row
            side = lax.rem(core + other, CORES)
            return row // slots * (CORES * slots) + side * slots + lax.rem(row, slots)

        lanes = GROUP * rows
        row_lane = lax.rem(lax.broadcasted_iota(jnp.int32, (1, lanes), 1), rows)
        self.comp_valid = jnp.where(row_lane < clen, 1.0, 0.0).astype(jnp.float32)
        self.near_ok = positions(safe, slots, lanes, 0) < plen
        self.far_ok = positions(safe, slots, lanes, 1) < plen
        self.own_ok = lax.broadcasted_iota(jnp.int32, (rows, lanes), 0) <= row_lane
        lanes = GROUP * slots
        global_row = lax.rem(lax.broadcasted_iota(jnp.int32, (1, lanes), 1), slots) + own * slots
        self.prompt_valid = jnp.where(global_row < plen, 1.0, 0.0).astype(jnp.float32)
        self.prompt_ok = jnp.concatenate(
            [positions(0, half, lanes, other) <= global_row for other in range(CORES)], axis=0
        )

    def products(self, head):
        pq_ref, pdo_ref, cq_ref, cdo_ref, ck_ref, cv_ref, kv_ref = self.refs
        lower = head * HEAD_DIM
        pk = prompt_head(kv_ref, self.core, lower)
        pv = prompt_head(kv_ref, self.core, KEY_VALUE_HEADS * HEAD_DIM + lower)
        keys = jnp.concatenate([pk, ck_ref[:, lower : lower + HEAD_DIM]], axis=0)
        values = jnp.concatenate([pv, cv_ref[:, lower : lower + HEAD_DIM]], axis=0)
        q, do = head_columns(cq_ref, head), head_columns(cdo_ref, head)
        q_p, do_p = head_columns(pq_ref, head), head_columns(pdo_ref, head)
        raw = dot(keys, q, NT), dot(values, do, NT), dot(pk, q_p, NT), dot(pv, do_p, NT)
        return raw, (q, do, q_p, do_p, keys)

    def weights(self, raw):
        scores, soft_grad, scores_p, soft_grad_p = raw
        half, safe = self.half, self.safe
        scores = jnp.concatenate(
            [
                scores[:safe],
                jnp.where(self.near_ok, scores[safe:half], MASKED),
                scores[half : half + safe],
                jnp.where(self.far_ok, scores[half + safe : CORES * half], MASKED),
                jnp.where(self.own_ok, scores[CORES * half :], MASKED),
            ],
            axis=0,
        )
        soft = softmax_terms(scores, self.comp_valid)
        soft_b = soft.astype(jnp.bfloat16)
        grad_b = score_gradient(soft, soft_b, soft_grad)
        soft_p = softmax_terms(jnp.where(self.prompt_ok, scores_p, MASKED), self.prompt_valid)
        soft_pb = soft_p.astype(jnp.bfloat16)
        grad_pb = score_gradient(soft_p, soft_pb, soft_grad_p)
        return soft_b, grad_b, soft_pb, grad_pb

    def heads(self):
        following = self.products(0)
        for head in range(KEY_VALUE_HEADS):
            raw, operands = following
            if head + 1 < KEY_VALUE_HEADS:
                following = self.products(head + 1)
            yield head, operands, self.weights(raw)


def stage_kernel(*refs):
    sources, targets, sems = refs[:8], refs[8:-1], refs[-1]
    key_target, value_target = (
        targets[0].at[:, : sources[0].shape[1]],
        targets[0].at[:, sources[0].shape[1] :],
    )
    copies = [
        pltpu.make_async_copy(source, target, sems.at[n])
        for n, (source, target) in enumerate(
            zip(sources, (key_target, value_target) + tuple(targets[1:]))
        )
    ]
    for copy in copies:
        copy.start()
    for copy in copies:
        copy.wait()


def attend_kernel(plen_ref, clen_ref, *refs):
    keep_ref, send_ref = refs[7:]
    attention = Attention(plen_ref[0], clen_ref[0], *refs[:7])
    half = attention.half
    for head, (q, do, q_p, do_p, _), weights in attention.heads():
        soft_b, grad_b, soft_pb, grad_pb = weights
        dv = dot(soft_b[: CORES * half], do, NN) + dot(soft_pb, do_p, NN)
        dk = (dot(grad_b[: CORES * half], q, NN) + dot(grad_pb, q_p, NN)) * SCALE
        for start, grad in ((head, dk), (KEY_VALUE_HEADS + head, dv)):
            columns = slice(start * HEAD_DIM, (start + 1) * HEAD_DIM)
            keep_ref[:, columns] = grad[:half]
            send_ref[:, columns] = grad[half:]


def grads_kernel(plen_ref, clen_ref, *refs):
    pdq_ref, cdq_ref, cdk_ref, cdv_ref = refs[8:]
    attention = Attention(plen_ref[0], clen_ref[0], *refs[:7])
    prompt_keys = CORES * attention.half
    slots, rows = attention.slots, attention.rows
    for head, (q, do, _, _, keys), weights in attention.heads():
        soft_b, grad_b, _, grad_pb = weights
        columns = slice(head * HEAD_DIM, (head + 1) * HEAD_DIM)
        own_dk = dot(grad_b[prompt_keys:], q, NN) * SCALE
        cdk_ref[:, columns] = own_dk.astype(jnp.bfloat16)
        cdv_ref[:, columns] = dot(soft_b[prompt_keys:], do, NN).astype(jnp.bfloat16)
        keys_t = keys.T
        dq_t = dot(keys_t, grad_b, NN) * SCALE
        dq_pt = dot(keys_t[:, :prompt_keys], grad_pb, NN) * SCALE
        dq_p = dq_pt.T.astype(jnp.bfloat16)
        for g in range(GROUP):
            column = (head * GROUP + g) * HEAD_DIM
            block = dq_t[:, g * rows : (g + 1) * rows]
            cdq_ref[:, column : column + HEAD_DIM] = block.T.astype(jnp.bfloat16)
            pdq_ref[:, column : column + HEAD_DIM] = dq_p[g * slots : (g + 1) * slots]


def pair_kernel(keep_ref, came_ref, sum_ref):
    core = lax.rem(lax.axis_index("sample"), CORES)
    for place in range(CHIPS):
        chip = lax.rem(place + core * (CHIPS // CORES), CHIPS)
        sum_ref[place] = (keep_ref[chip] + came_ref[chip]).astype(jnp.bfloat16)


def total_kernel(terms_ref, dk_ref, dv_ref):
    width = dk_ref.shape[1]
    dk_ref[...] = jnp.sum(terms_ref[:, :, :width].astype(jnp.float32), axis=0).astype(jnp.bfloat16)
    dv_ref[...] = jnp.sum(terms_ref[:, :, width:].astype(jnp.float32), axis=0).astype(jnp.bfloat16)


def attend(lengths, arrays):
    slots = arrays[0].shape[0]
    half = CHIPS * slots
    width = KEY_VALUE_HEADS * HEAD_DIM
    smem = pl.BlockSpec(memory_space=pltpu.SMEM)
    vmem = pl.BlockSpec(memory_space=pltpu.VMEM)
    return pl.pallas_call(
        attend_kernel,
        out_shape=(jax.ShapeDtypeStruct((half, 2 * width), jnp.float32),) * 2,
        in_specs=[smem, smem] + [vmem] * len(arrays),
        out_specs=(vmem,) * 2,
        compiler_params=pltpu.CompilerParams(vmem_limit_bytes=24 * 1024 * 1024),
        cost_estimate=pl.CostEstimate(
            flops=1_000_000_000, bytes_accessed=4_000_000, transcendentals=850_000
        ),
        name="attend",
    )(*lengths, *arrays)


def grads(lengths, arrays, after):
    slots, columns = arrays[0].shape
    rows = arrays[2].shape[0]
    width = KEY_VALUE_HEADS * HEAD_DIM
    smem = pl.BlockSpec(memory_space=pltpu.SMEM)
    vmem = pl.BlockSpec(memory_space=pltpu.VMEM)
    shapes = ((slots, columns), (rows, columns), (rows, width), (rows, width))
    return pl.pallas_call(
        grads_kernel,
        out_shape=tuple(jax.ShapeDtypeStruct(shape, jnp.bfloat16) for shape in shapes),
        in_specs=[smem, smem] + [vmem] * len(arrays) + [pl.BlockSpec(memory_space=pl.ANY)],
        out_specs=(vmem,) * len(shapes),
        compiler_params=pltpu.CompilerParams(vmem_limit_bytes=24 * 1024 * 1024),
        cost_estimate=pl.CostEstimate(
            flops=1_000_000_000, bytes_accessed=4_000_000, transcendentals=850_000
        ),
        name="grads",
    )(*lengths, *arrays, after)


def stage(keys, values, *rest):
    shapes = [(keys.shape[0], 2 * keys.shape[1])] + [a.shape for a in rest]
    return pl.pallas_call(
        stage_kernel,
        out_shape=tuple(jax.ShapeDtypeStruct(shape, keys.dtype) for shape in shapes),
        in_specs=[pl.BlockSpec(memory_space=pl.ANY)] * (2 + len(rest)),
        out_specs=(pl.BlockSpec(memory_space=pltpu.VMEM),) * len(shapes),
        scratch_shapes=[pltpu.SemaphoreType.DMA((2 + len(rest),))],
        compiler_params=pltpu.CompilerParams(vmem_limit_bytes=8 * 1024 * 1024),
        cost_estimate=pl.CostEstimate(flops=0, bytes_accessed=2_800_000, transcendentals=0),
        name="stage",
    )(*[pltpu.with_memory_space_constraint(a, pltpu.HBM) for a in (keys, values, *rest)])


def pair_sum(keep, came):
    vmem = pl.BlockSpec(memory_space=pltpu.VMEM)
    return pl.pallas_call(
        pair_kernel,
        out_shape=jax.ShapeDtypeStruct(keep.shape, jnp.bfloat16),
        in_specs=[vmem, vmem],
        out_specs=vmem,
        compiler_params=pltpu.CompilerParams(vmem_limit_bytes=8 * 1024 * 1024),
        cost_estimate=pl.CostEstimate(flops=140_000, bytes_accessed=1_300_000, transcendentals=0),
        name="pair_sum",
    )(keep, came)


def total(terms):
    _, slots, columns = terms.shape
    vmem = pl.BlockSpec(memory_space=pltpu.VMEM)
    shape = jax.ShapeDtypeStruct((slots, columns // 2), jnp.bfloat16)
    return pl.pallas_call(
        total_kernel,
        out_shape=(shape, shape),
        in_specs=[vmem],
        out_specs=(vmem, vmem),
        compiler_params=pltpu.CompilerParams(vmem_limit_bytes=4 * 1024 * 1024),
        cost_estimate=pl.CostEstimate(flops=600_000, bytes_accessed=560_000, transcendentals=0),
        name="total",
    )(terms)


def body(
    prompt_q,
    prompt_k,
    prompt_value_rows,
    prompt_dout,
    comp_q,
    completion_keys,
    completion_values,
    comp_dout,
    comp_lengths,
    prompt_length,
):
    own, *staged = stage(
        prompt_k,
        prompt_value_rows,
        prompt_q,
        prompt_dout,
        comp_q[0],
        comp_dout[0],
        completion_keys[0],
        completion_values[0],
    )
    lengths = prompt_length, comp_lengths
    kv = lax.all_gather(own, "sample", axis=0, tiled=False)
    arrays = (*staged, kv.reshape(CHIPS, CORES, *own.shape))
    keep, send = attend(lengths, arrays)
    swap = [(d, d ^ 1) for d in range(CHIPS * CORES)]
    came = lax.ppermute(send, "sample", swap)
    by_chip = (CHIPS, *own.shape)
    partial = pair_sum(keep.reshape(by_chip), came.reshape(by_chip))
    half_turn = CHIPS // CORES
    same_core = [
        [(y + c * half_turn) % CHIPS * CORES + c for y in range(CHIPS)] for c in range(CORES)
    ]
    terms = lax.all_to_all(
        partial, "sample", split_axis=0, concat_axis=0, axis_index_groups=same_core, tiled=True
    )
    pdq, cdq, cdk, cdv = grads(lengths, arrays, partial)
    pdk, pdv = total(terms)
    return (pdq, pdk, pdv, cdq[None], cdk[None], cdv[None])


def solution(mesh):
    rows = P(("prompt", "sample"), None)
    blocks = P(("prompt", "sample"), None, None)
    in_specs = (rows,) * 4 + (blocks,) * 4 + (P(("prompt", "sample")), P("prompt"))
    out_specs = (rows,) * 3 + (blocks,) * 3
    return jax.shard_map(body, mesh=mesh, in_specs=in_specs, out_specs=out_specs, check_vma=False)
```

```python
import jax
import jax.numpy as jnp
from jax import lax
from jax.experimental import pallas as pl
from jax.experimental.pallas import tpu as pltpu
from jax.sharding import PartitionSpec as P

QUERY_HEADS = 16
KEY_VALUE_HEADS = 4
HEAD_DIM = 128
GROUP = QUERY_HEADS // KEY_VALUE_HEADS
SCALE = HEAD_DIM ** (-0.5)
LOG2E = 1.4426950408889634
CHIPS = 8
CORES = 2
DEVICES = CHIPS * CORES
MASKED = -1e30

HALF_HEADS = KEY_VALUE_HEADS // CORES
HALF_WIDTH = HALF_HEADS * HEAD_DIM
HALF_COLUMNS = HALF_WIDTH * GROUP

SLOTS = 16
ROWS = 128
KEYS = DEVICES * SLOTS
LANES = GROUP * ROWS

Q_ROW = 0
DO_ROW = ROWS
PQ_ROW = 2 * ROWS
PDO_ROW = PQ_ROW + SLOTS
KV_ROW = PDO_ROW + SLOTS
LENGTH_ROW = KV_ROW + ROWS // 2
OPERAND_ROWS = LENGTH_ROW + SLOTS

DQ_ROW = 0
PDQ_ROW = ROWS
DKV_ROW = PDQ_ROW + SLOTS
RESULT_ROWS = DKV_ROW + ROWS // 2

ORDER = [
    chip % CHIPS * CORES + core
    for step in range(CHIPS)
    for core in range(CORES)
    for chip in [3 * step + core * (CHIPS // CORES)]
]
PLACE = [ORDER.index(device) for device in range(DEVICES)]

NT = ((1,), (1,))
NN = ((1,), (0,))
VMEM = pl.BlockSpec(memory_space=pltpu.VMEM)
SMEM = pl.BlockSpec(memory_space=pltpu.SMEM)
ANY = pl.BlockSpec(memory_space=pl.ANY)


def dot(a, b, contract):
    return lax.dot_general(a, b, (contract, ((), ())), preferred_element_type=jnp.float32)


def own_core():
    return lax.rem(lax.axis_index("sample"), CORES)


def columns_of(core, width):
    return pl.ds(pl.multiple_of(core * width, HEAD_DIM), width)


def run(copies):
    for copy in copies:
        copy.start()
    for copy in copies:
        copy.wait()


def stage_kernel(k_ref, v_ref, out_ref, kv_ref, sems):
    run(
        [
            pltpu.make_async_copy(
                source.at[:, core * HALF_WIDTH : (core + 1) * HALF_WIDTH],
                kv_ref.at[core, :, n * HALF_WIDTH : (n + 1) * HALF_WIDTH],
                sems.at[2 * core + n],
            )
            for core in range(CORES)
            for n, source in enumerate((k_ref, v_ref))
        ]
    )
    for core in range(CORES):
        rows = kv_ref[core]
        for chip in range(CHIPS):
            out_ref[PLACE[chip * CORES + core]] = rows


def packed(ref, first_row, n):
    return ref.at[first_row : first_row + ROWS // 2, n * HALF_WIDTH : (n + 1) * HALF_WIDTH]


def split_kernel(clen_ref, q_ref, do_ref, pq_ref, pdo_ref, ck_ref, cv_ref, _, mine, theirs, sems):
    core = own_core()
    copies = []
    for n, (target, half) in enumerate(((mine, core), (theirs, 1 - core))):
        wide, narrow = columns_of(half, HALF_COLUMNS), columns_of(half, HALF_WIDTH)
        pairs = [
            (q_ref.at[:, wide], target.at[Q_ROW : Q_ROW + ROWS]),
            (do_ref.at[:, wide], target.at[DO_ROW : DO_ROW + ROWS]),
            (pq_ref.at[:, wide], target.at[PQ_ROW : PQ_ROW + SLOTS]),
            (pdo_ref.at[:, wide], target.at[PDO_ROW : PDO_ROW + SLOTS]),
        ]
        for k, source in enumerate((ck_ref, cv_ref)):
            for part in range(2):
                rows = slice(part * ROWS // 2, (part + 1) * ROWS // 2)
                pairs.append((source.at[rows, narrow], packed(target, KV_ROW, 2 * k + part)))
        copies += [
            pltpu.make_async_copy(source, place, sems.at[n * len(pairs) + k])
            for k, (source, place) in enumerate(pairs)
        ]
    for copy in copies:
        copy.start()
    length = jnp.full((SLOTS, HALF_COLUMNS), clen_ref[0], jnp.int32).astype(jnp.float32)
    for target in (mine, theirs):
        target[LENGTH_ROW:OPERAND_ROWS] = length.astype(jnp.bfloat16)
    for copy in copies:
        copy.wait()


def head_columns(ref, first_row, count, head):
    parts = [
        ref[
            first_row : first_row + count,
            (head * GROUP + g) * HEAD_DIM : (head * GROUP + g + 1) * HEAD_DIM,
        ]
        for g in range(GROUP)
    ]
    return jnp.concatenate(parts, axis=0)


def own_rows(ref, head, first):
    parts = [
        packed(ref, KV_ROW, first + part)[:, head * HEAD_DIM : (head + 1) * HEAD_DIM]
        for part in range(2)
    ]
    return jnp.concatenate(parts, axis=0)


def softmax_terms(scores, valid):
    factor = SCALE * LOG2E
    peak = jnp.max(scores, axis=0, keepdims=True)
    terms = jnp.exp2(scores * factor - peak * factor)
    total = jnp.sum(terms, axis=0, keepdims=True)
    return terms * (valid / total)


def score_gradient(soft, soft_b, soft_grad):
    delta = jnp.sum(soft_b.astype(jnp.float32) * soft_grad, axis=0, keepdims=True)
    return (soft * (soft_grad - delta)).astype(jnp.bfloat16)


class Attention:
    def __init__(self, plen_ref, mine_ref, got_ref, kv_ref):
        self.sides = mine_ref, got_ref
        self.kv_ref = kv_ref
        plen = plen_ref[0]
        own = lax.axis_index("sample")
        other = own + 1 - 2 * own_core()
        row_lane = lax.rem(lax.broadcasted_iota(jnp.int32, (1, LANES), 1), ROWS)
        self.valid = []
        for ref in self.sides:
            length = ref[LENGTH_ROW:OPERAND_ROWS, :LANES].astype(jnp.float32)[0:1]
            live = row_lane.astype(jnp.float32) < length
            self.valid.append(jnp.where(live, 1.0, 0.0).astype(jnp.float32))
        self.safe = KEYS - 2 * SLOTS
        self.tail_ok = (
            lax.broadcasted_iota(jnp.int32, (2 * SLOTS, LANES), 0) + self.safe < plen
        )
        self.own_ok = lax.broadcasted_iota(jnp.int32, (ROWS, LANES), 0) <= row_lane
        lanes = CORES * GROUP * SLOTS
        lane = lax.broadcasted_iota(jnp.int32, (1, lanes), 1)
        device = jnp.where(lane < GROUP * SLOTS, own, other)
        global_row = device * SLOTS + lax.rem(lane, SLOTS)
        self.prompt_valid = jnp.where(global_row < plen, 1.0, 0.0).astype(jnp.float32)
        self.prompt_ok = lax.broadcasted_iota(jnp.int32, (KEYS, lanes), 0) <= global_row

    def prompt_rows(self, start):
        parts = [
            self.kv_ref[PLACE[device], :, start : start + HEAD_DIM] for device in range(DEVICES)
        ]
        return jnp.concatenate(parts, axis=0)

    def products(self, head, side):
        keys = self.prompt_rows(head * HEAD_DIM)
        values = self.prompt_rows(HALF_WIDTH + head * HEAD_DIM)
        if side < CORES:
            ref = self.sides[side]
            keys = jnp.concatenate([keys, own_rows(ref, head, 0)], axis=0)
            values = jnp.concatenate([values, own_rows(ref, head, 2)], axis=0)
            q = head_columns(ref, Q_ROW, ROWS, head)
            do = head_columns(ref, DO_ROW, ROWS, head)
        else:
            q, do = (
                jnp.concatenate(
                    [head_columns(ref, row, SLOTS, head) for ref in self.sides], axis=0
                )
                for row in (PQ_ROW, PDO_ROW)
            )
        return dot(keys, q, NT), dot(values, do, NT), (keys, q, do)

    def weights(self, side, scores, soft_grad):
        if side < CORES:
            scores = jnp.concatenate(
                [
                    scores[: self.safe],
                    jnp.where(self.tail_ok, scores[self.safe : KEYS], MASKED),
                    jnp.where(self.own_ok, scores[KEYS:], MASKED),
                ],
                axis=0,
            )
            valid = self.valid[side]
        else:
            scores = jnp.where(self.prompt_ok, scores, MASKED)
            valid = self.prompt_valid
        soft = softmax_terms(scores, valid)
        soft_b = soft.astype(jnp.bfloat16)
        return soft_b, score_gradient(soft, soft_b, soft_grad)

    def units(self):
        todo = [(head, side) for head in range(HALF_HEADS) for side in (0, 1, 2)]
        following = self.products(*todo[0])
        for n, (head, side) in enumerate(todo):
            scores, soft_grad, operands = following
            if n + 1 < len(todo):
                following = self.products(*todo[n + 1])
            yield head, side, operands, *self.weights(side, scores, soft_grad)


def attend_kernel(plen_ref, mine_ref, got_ref, kv_ref, part_ref):
    dk = dv = None
    for head, side, (_, q, do), soft_b, grad_b in Attention(
        plen_ref, mine_ref, got_ref, kv_ref
    ).units():
        more_dv = dot(soft_b[:KEYS], do, NN)
        more_dk = dot(grad_b[:KEYS], q, NN)
        dv = more_dv if side == 0 else dv + more_dv
        dk = more_dk if side == 0 else dk + more_dk
        if side == CORES:
            for start, grad in ((head, dk * SCALE), (HALF_HEADS + head, dv)):
                grad = grad.astype(jnp.bfloat16)
                for device in range(DEVICES):
                    part_ref[PLACE[device], :, start * HEAD_DIM : (start + 1) * HEAD_DIM] = grad[
                        device * SLOTS : (device + 1) * SLOTS
                    ]


def grads_kernel(plen_ref, mine_ref, got_ref, kv_ref, _, mine_out, theirs_out):
    outs = mine_out, theirs_out
    half = ROWS // 2
    for head, side, (keys, q, do), soft_b, grad_b in Attention(
        plen_ref, mine_ref, got_ref, kv_ref
    ).units():
        dq_t = dot(keys.T, grad_b, NN) * SCALE
        if side == CORES:
            dq = dq_t.T.astype(jnp.bfloat16)
            for n, out in enumerate(outs):
                for g in range(GROUP):
                    column = (head * GROUP + g) * HEAD_DIM
                    row = (n * GROUP + g) * SLOTS
                    out[PDQ_ROW : PDQ_ROW + SLOTS, column : column + HEAD_DIM] = dq[
                        row : row + SLOTS
                    ]
            continue
        out = outs[side]
        for g in range(GROUP):
            column = (head * GROUP + g) * HEAD_DIM
            block = dq_t[:, g * ROWS : (g + 1) * ROWS]
            out[DQ_ROW : DQ_ROW + ROWS, column : column + HEAD_DIM] = block.T.astype(jnp.bfloat16)
        own_dk = (dot(grad_b[KEYS:], q, NN) * SCALE).astype(jnp.bfloat16)
        own_dv = dot(soft_b[KEYS:], do, NN).astype(jnp.bfloat16)
        for n, grad in enumerate((own_dk, own_dv)):
            for part in range(2):
                column = (2 * n + part) * HALF_WIDTH + head * HEAD_DIM
                out[DKV_ROW:RESULT_ROWS, column : column + HEAD_DIM] = grad[
                    part * half : (part + 1) * half
                ]


def join_kernel(mine_ref, got_ref, pdq_ref, cdq_ref, cdk_ref, cdv_ref, sems):
    core = own_core()
    copies = []
    for n, (source, half) in enumerate(((mine_ref, core), (got_ref, 1 - core))):
        wide, narrow = columns_of(half, HALF_COLUMNS), columns_of(half, HALF_WIDTH)
        pairs = [
            (source.at[DQ_ROW : DQ_ROW + ROWS], cdq_ref.at[:, wide]),
            (source.at[PDQ_ROW : PDQ_ROW + SLOTS], pdq_ref.at[:, wide]),
        ]
        for k, target in enumerate((cdk_ref, cdv_ref)):
            for part in range(2):
                rows = slice(part * ROWS // 2, (part + 1) * ROWS // 2)
                pairs.append((packed(source, DKV_ROW, 2 * k + part), target.at[rows, narrow]))
        copies += [
            pltpu.make_async_copy(place, target, sems.at[n * len(pairs) + k])
            for k, (place, target) in enumerate(pairs)
        ]
    run(copies)


def total_kernel(terms_ref, dk_ref, dv_ref):
    for core in range(CORES):
        total = sum(
            terms_ref[PLACE[chip * CORES + core]].astype(jnp.float32) for chip in range(CHIPS)
        ).astype(jnp.bfloat16)
        columns = slice(core * HALF_WIDTH, (core + 1) * HALF_WIDTH)
        dk_ref[:, columns] = total[:, :HALF_WIDTH]
        dv_ref[:, columns] = total[:, HALF_WIDTH:]


def kernel(body, name, shapes, in_specs, out_specs, limit, cost, scratch=(), dtype=jnp.bfloat16):
    flops, moved, transcendentals = cost
    return pl.pallas_call(
        body,
        out_shape=tuple(jax.ShapeDtypeStruct(shape, dtype) for shape in shapes),
        in_specs=in_specs,
        out_specs=out_specs,
        scratch_shapes=list(scratch),
        compiler_params=pltpu.CompilerParams(vmem_limit_bytes=limit * 1024 * 1024),
        cost_estimate=pl.CostEstimate(
            flops=flops, bytes_accessed=moved, transcendentals=transcendentals
        ),
        name=name,
    )


def in_hbm(*arrays):
    return [pltpu.with_memory_space_constraint(a, pltpu.HBM) for a in arrays]


def body(
    prompt_q,
    prompt_k,
    prompt_value_rows,
    prompt_dout,
    comp_q,
    completion_keys,
    completion_values,
    comp_dout,
    comp_lengths,
    prompt_length,
):
    block = (DEVICES, SLOTS, 2 * HALF_WIDTH)
    operands = (OPERAND_ROWS, HALF_COLUMNS)
    results = (RESULT_ROWS, HALF_COLUMNS)
    swap = [(device, device ^ 1) for device in range(DEVICES)]

    def exchange(blocks):
        return lax.all_to_all(
            blocks, "sample", split_axis=0, concat_axis=0, axis_index_groups=[ORDER], tiled=True
        )

    (outgoing,) = kernel(
        stage_kernel,
        "stage",
        [block],
        [ANY] * 2,
        (VMEM,),
        4,
        (0, 300_000, 0),
        [
            pltpu.VMEM((CORES, SLOTS, 2 * HALF_WIDTH), jnp.bfloat16),
            pltpu.SemaphoreType.DMA((2 * CORES,)),
        ],
    )(*in_hbm(prompt_k, prompt_value_rows))
    kv = exchange(outgoing)
    mine, theirs = kernel(
        split_kernel,
        "split",
        [operands] * 2,
        [SMEM] + [ANY] * 7,
        (VMEM,) * 2,
        8,
        (0, 3_000_000, 0),
        [pltpu.SemaphoreType.DMA((16,))],
    )(
        comp_lengths,
        *in_hbm(
            comp_q[0],
            comp_dout[0],
            prompt_q,
            prompt_dout,
            completion_keys[0],
            completion_values[0],
        ),
        outgoing,
    )
    got = lax.ppermute(theirs, "sample", swap)
    scores_in = prompt_length, mine, got, kv
    cost = (1_000_000_000, 4_000_000, 850_000)
    (partial,) = kernel(
        attend_kernel, "attend", [block], [SMEM] + [VMEM] * 3, (VMEM,), 24, cost
    )(*scores_in)
    terms = exchange(partial)
    mine_out, theirs_out = kernel(
        grads_kernel, "grads", [results] * 2, [SMEM] + [VMEM] * 3 + [ANY], (VMEM,) * 2, 24, cost
    )(*scores_in, partial)
    got_out = lax.ppermute(theirs_out, "sample", swap)
    width = KEY_VALUE_HEADS * HEAD_DIM
    shapes = (
        (SLOTS, QUERY_HEADS * HEAD_DIM),
        (ROWS, QUERY_HEADS * HEAD_DIM),
        (ROWS, width),
        (ROWS, width),
    )
    pdq, cdq, cdk, cdv = kernel(
        join_kernel,
        "join",
        shapes,
        [VMEM] * 2,
        (ANY,) * 4,
        4,
        (0, 1_700_000, 0),
        [pltpu.SemaphoreType.DMA((12,))],
    )(mine_out, got_out)
    pdk, pdv = kernel(
        total_kernel, "total", [(SLOTS, width)] * 2, [VMEM], (VMEM,) * 2, 4, (130_000, 300_000, 0)
    )(terms)
    return (pdq, pdk, pdv, cdq[None], cdk[None], cdv[None])


def solution(mesh):
    rows = P(("prompt", "sample"), None)
    blocks = P(("prompt", "sample"), None, None)
    in_specs = (rows,) * 4 + (blocks,) * 4 + (P(("prompt", "sample")), P("prompt"))
    out_specs = (rows,) * 3 + (blocks,) * 3
    return jax.shard_map(body, mesh=mesh, in_specs=in_specs, out_specs=out_specs, check_vma=False)
```

```python
import jax
import jax.numpy as jnp
from jax import lax
from jax.experimental import pallas as pl
from jax.experimental.pallas import tpu as pltpu
from jax.sharding import PartitionSpec as P

QUERY_HEADS = 16
KEY_VALUE_HEADS = 4
HEAD_DIM = 128
GROUP = QUERY_HEADS // KEY_VALUE_HEADS
SCALE = HEAD_DIM ** (-0.5)
LOG2E = 1.4426950408889634
CHIPS = 8
CORES = 2
DEVICES = CHIPS * CORES
MASKED = -1e30

HALF_HEADS = KEY_VALUE_HEADS // CORES
HALF_WIDTH = HALF_HEADS * HEAD_DIM
HALF_COLUMNS = HALF_WIDTH * GROUP

SLOTS = 16
ROWS = 128
KEYS = DEVICES * SLOTS
LANES = GROUP * ROWS

Q_ROW = 0
DO_ROW = ROWS
PQ_ROW = 2 * ROWS
PDO_ROW = PQ_ROW + SLOTS
KV_ROW = PDO_ROW + SLOTS
LENGTH_ROW = KV_ROW + ROWS // 2
OPERAND_ROWS = LENGTH_ROW + SLOTS

DQ_ROW = 0
PDQ_ROW = ROWS
DKV_ROW = PDQ_ROW + SLOTS
RESULT_ROWS = DKV_ROW + ROWS // 2

ORDER = [
    chip % CHIPS * CORES + core
    for step in range(CHIPS)
    for core in range(CORES)
    for chip in [3 * step + core * (CHIPS // CORES)]
]
PLACE = [ORDER.index(device) for device in range(DEVICES)]

NT = ((1,), (1,))
NN = ((1,), (0,))
VMEM = pl.BlockSpec(memory_space=pltpu.VMEM)
SMEM = pl.BlockSpec(memory_space=pltpu.SMEM)
ANY = pl.BlockSpec(memory_space=pl.ANY)


def dot(a, b, contract):
    return lax.dot_general(a, b, (contract, ((), ())), preferred_element_type=jnp.float32)


def own_core():
    return lax.rem(lax.axis_index("sample"), CORES)


def columns_of(core, width):
    return pl.ds(pl.multiple_of(core * width, HEAD_DIM), width)


def run(copies):
    for copy in copies:
        copy.start()
    for copy in copies:
        copy.wait()


def stage_kernel(k_ref, v_ref, out_ref, kv_ref, sems):
    run(
        [
            pltpu.make_async_copy(source, kv_ref.at[n], sems.at[n])
            for n, source in enumerate((k_ref, v_ref))
        ]
    )
    for core in range(CORES):
        columns = slice(core * HALF_WIDTH, (core + 1) * HALF_WIDTH)
        rows = jnp.concatenate([kv_ref[0, :, columns], kv_ref[1, :, columns]], axis=1)
        for chip in range(CHIPS):
            out_ref[PLACE[chip * CORES + core]] = rows


def packed(ref, first_row, n):
    return ref.at[first_row : first_row + ROWS // 2, n * HALF_WIDTH : (n + 1) * HALF_WIDTH]


def split_kernel(clen_ref, q_ref, do_ref, pq_ref, pdo_ref, ck_ref, cv_ref, _, mine, theirs, sems):
    core = own_core()
    copies = []
    for n, (target, half) in enumerate(((mine, core), (theirs, 1 - core))):
        wide, narrow = columns_of(half, HALF_COLUMNS), columns_of(half, HALF_WIDTH)
        pairs = [
            (q_ref.at[:, wide], target.at[Q_ROW : Q_ROW + ROWS]),
            (do_ref.at[:, wide], target.at[DO_ROW : DO_ROW + ROWS]),
            (pq_ref.at[:, wide], target.at[PQ_ROW : PQ_ROW + SLOTS]),
            (pdo_ref.at[:, wide], target.at[PDO_ROW : PDO_ROW + SLOTS]),
        ]
        for k, source in enumerate((ck_ref, cv_ref)):
            for part in range(2):
                rows = slice(part * ROWS // 2, (part + 1) * ROWS // 2)
                pairs.append((source.at[rows, narrow], packed(target, KV_ROW, 2 * k + part)))
        copies += [
            pltpu.make_async_copy(source, place, sems.at[n * len(pairs) + k])
            for k, (source, place) in enumerate(pairs)
        ]
    for copy in copies:
        copy.start()
    length = jnp.full((SLOTS, HALF_COLUMNS), clen_ref[0], jnp.int32).astype(jnp.float32)
    for target in (mine, theirs):
        target[LENGTH_ROW:OPERAND_ROWS] = length.astype(jnp.bfloat16)
    for copy in copies:
        copy.wait()


def head_columns(ref, first_row, count, head):
    parts = [
        ref[
            first_row : first_row + count,
            (head * GROUP + g) * HEAD_DIM : (head * GROUP + g + 1) * HEAD_DIM,
        ]
        for g in range(GROUP)
    ]
    return jnp.concatenate(parts, axis=0)


def own_rows(ref, head, first):
    parts = [
        packed(ref, KV_ROW, first + part)[:, head * HEAD_DIM : (head + 1) * HEAD_DIM]
        for part in range(2)
    ]
    return jnp.concatenate(parts, axis=0)


def softmax_terms(scores, valid):
    factor = SCALE * LOG2E
    peak = jnp.max(scores, axis=0, keepdims=True)
    terms = jnp.exp2(scores * factor - peak * factor)
    total = jnp.sum(terms, axis=0, keepdims=True)
    return terms * (valid / total)


def score_gradient(soft, soft_b, soft_grad):
    delta = jnp.sum(soft_b.astype(jnp.float32) * soft_grad, axis=0, keepdims=True)
    return (soft * (soft_grad - delta)).astype(jnp.bfloat16)


def valid_kernel(mine_ref, got_ref, valid_ref):
    row = lax.rem(lax.broadcasted_iota(jnp.int32, (8, LANES), 1), ROWS).astype(jnp.float32)
    lengths = [
        ref[LENGTH_ROW:OPERAND_ROWS, :LANES].astype(jnp.float32)[0:1]
        for ref in (mine_ref, got_ref)
    ]
    first = lax.broadcasted_iota(jnp.int32, (8, LANES), 0) == 0
    valid_ref[...] = jnp.where(row < jnp.where(first, *lengths), 1.0, 0.0).astype(jnp.float32)


class Attention:
    def __init__(self, plen_ref, mine_ref, got_ref, valid_ref, kv_ref):
        self.sides = mine_ref, got_ref
        self.kv_ref = kv_ref
        plen = plen_ref[0]
        own = lax.axis_index("sample")
        other = own + 1 - 2 * own_core()
        row_lane = lax.rem(lax.broadcasted_iota(jnp.int32, (1, LANES), 1), ROWS)
        self.valid = [valid_ref[side : side + 1] for side in range(CORES)]
        self.safe = KEYS - 2 * SLOTS
        self.tail_ok = (
            lax.broadcasted_iota(jnp.int32, (2 * SLOTS, LANES), 0) + self.safe < plen
        )
        self.own_ok = lax.broadcasted_iota(jnp.int32, (ROWS, LANES), 0) <= row_lane
        lanes = CORES * GROUP * SLOTS
        lane = lax.broadcasted_iota(jnp.int32, (1, lanes), 1)
        device = jnp.where(lane < GROUP * SLOTS, own, other)
        global_row = device * SLOTS + lax.rem(lane, SLOTS)
        self.prompt_valid = jnp.where(global_row < plen, 1.0, 0.0).astype(jnp.float32)
        self.prompt_ok = lax.broadcasted_iota(jnp.int32, (KEYS, lanes), 0) <= global_row

    def prompt_rows(self, start):
        parts = [
            self.kv_ref[PLACE[device], :, start : start + HEAD_DIM] for device in range(DEVICES)
        ]
        return jnp.concatenate(parts, axis=0)

    def products(self, head, side):
        keys = self.prompt_rows(head * HEAD_DIM)
        values = self.prompt_rows(HALF_WIDTH + head * HEAD_DIM)
        if side < CORES:
            ref = self.sides[side]
            keys = jnp.concatenate([keys, own_rows(ref, head, 0)], axis=0)
            values = jnp.concatenate([values, own_rows(ref, head, 2)], axis=0)
            q = head_columns(ref, Q_ROW, ROWS, head)
            do = head_columns(ref, DO_ROW, ROWS, head)
        else:
            q, do = (
                jnp.concatenate(
                    [head_columns(ref, row, SLOTS, head) for ref in self.sides], axis=0
                )
                for row in (PQ_ROW, PDO_ROW)
            )
        return dot(keys, q, NT), dot(values, do, NT), (keys, q, do)

    def weights(self, side, scores, soft_grad):
        if side < CORES:
            scores = jnp.concatenate(
                [
                    scores[: self.safe],
                    jnp.where(self.tail_ok, scores[self.safe : KEYS], MASKED),
                    jnp.where(self.own_ok, scores[KEYS:], MASKED),
                ],
                axis=0,
            )
            valid = self.valid[side]
        else:
            scores = jnp.where(self.prompt_ok, scores, MASKED)
            valid = self.prompt_valid
        soft = softmax_terms(scores, valid)
        soft_b = soft.astype(jnp.bfloat16)
        return soft_b, score_gradient(soft, soft_b, soft_grad)

    def units(self):
        todo = [
            group for head in range(HALF_HEADS) for group in ([(head, 0)], [(head, 1), (head, 2)])
        ]
        following = [self.products(*unit) for unit in todo[0]]
        for n, group in enumerate(todo):
            ready = following
            if n + 1 < len(todo):
                following = [self.products(*unit) for unit in todo[n + 1]]
            for (head, side), (scores, soft_grad, operands) in zip(group, ready):
                yield head, side, operands, *self.weights(side, scores, soft_grad)


def attend_kernel(plen_ref, mine_ref, got_ref, valid_ref, kv_ref, part_ref):
    dk = dv = None
    for head, side, (_, q, do), soft_b, grad_b in Attention(
        plen_ref, mine_ref, got_ref, valid_ref, kv_ref
    ).units():
        more_dv = dot(soft_b[:KEYS], do, NN)
        more_dk = dot(grad_b[:KEYS], q, NN)
        dv = more_dv if side == 0 else dv + more_dv
        dk = more_dk if side == 0 else dk + more_dk
        if side == CORES:
            for start, grad in ((head, dk * SCALE), (HALF_HEADS + head, dv)):
                grad = grad.astype(jnp.bfloat16)
                for device in range(DEVICES):
                    part_ref[PLACE[device], :, start * HEAD_DIM : (start + 1) * HEAD_DIM] = grad[
                        device * SLOTS : (device + 1) * SLOTS
                    ]


def grads_kernel(plen_ref, mine_ref, got_ref, valid_ref, kv_ref, _, mine_out, theirs_out):
    outs = mine_out, theirs_out
    half = ROWS // 2
    for head, side, (keys, q, do), soft_b, grad_b in Attention(
        plen_ref, mine_ref, got_ref, valid_ref, kv_ref
    ).units():
        dq_t = dot(keys.T, grad_b, NN) * SCALE
        if side == CORES:
            dq = dq_t.T.astype(jnp.bfloat16)
            for n, out in enumerate(outs):
                for g in range(GROUP):
                    column = (head * GROUP + g) * HEAD_DIM
                    row = (n * GROUP + g) * SLOTS
                    out[PDQ_ROW : PDQ_ROW + SLOTS, column : column + HEAD_DIM] = dq[
                        row : row + SLOTS
                    ]
            continue
        out = outs[side]
        for g in range(GROUP):
            column = (head * GROUP + g) * HEAD_DIM
            block = dq_t[:, g * ROWS : (g + 1) * ROWS]
            out[DQ_ROW : DQ_ROW + ROWS, column : column + HEAD_DIM] = block.T.astype(jnp.bfloat16)
        own_dk = (dot(grad_b[KEYS:], q, NN) * SCALE).astype(jnp.bfloat16)
        own_dv = dot(soft_b[KEYS:], do, NN).astype(jnp.bfloat16)
        for n, grad in enumerate((own_dk, own_dv)):
            for part in range(2):
                column = (2 * n + part) * HALF_WIDTH + head * HEAD_DIM
                out[DKV_ROW:RESULT_ROWS, column : column + HEAD_DIM] = grad[
                    part * half : (part + 1) * half
                ]


def join_kernel(mine_ref, got_ref, pdq_ref, cdq_ref, cdk_ref, cdv_ref, sems):
    core = own_core()
    copies = []
    for n, (source, half) in enumerate(((mine_ref, core), (got_ref, 1 - core))):
        wide, narrow = columns_of(half, HALF_COLUMNS), columns_of(half, HALF_WIDTH)
        pairs = [
            (source.at[DQ_ROW : DQ_ROW + ROWS], cdq_ref.at[:, wide]),
            (source.at[PDQ_ROW : PDQ_ROW + SLOTS], pdq_ref.at[:, wide]),
        ]
        for k, target in enumerate((cdk_ref, cdv_ref)):
            for part in range(2):
                rows = slice(part * ROWS // 2, (part + 1) * ROWS // 2)
                pairs.append((packed(source, DKV_ROW, 2 * k + part), target.at[rows, narrow]))
        copies += [
            pltpu.make_async_copy(place, target, sems.at[n * len(pairs) + k])
            for k, (place, target) in enumerate(pairs)
        ]
    run(copies)


def total_kernel(terms_ref, dk_ref, dv_ref):
    for core in range(CORES):
        total = sum(
            terms_ref[PLACE[chip * CORES + core]].astype(jnp.float32) for chip in range(CHIPS)
        ).astype(jnp.bfloat16)
        columns = slice(core * HALF_WIDTH, (core + 1) * HALF_WIDTH)
        dk_ref[:, columns] = total[:, :HALF_WIDTH]
        dv_ref[:, columns] = total[:, HALF_WIDTH:]


def kernel(body, name, shapes, in_specs, out_specs, limit, cost, scratch=(), dtype=jnp.bfloat16):
    flops, moved, transcendentals = cost
    return pl.pallas_call(
        body,
        out_shape=tuple(jax.ShapeDtypeStruct(shape, dtype) for shape in shapes),
        in_specs=in_specs,
        out_specs=out_specs,
        scratch_shapes=list(scratch),
        compiler_params=pltpu.CompilerParams(vmem_limit_bytes=limit * 1024 * 1024),
        cost_estimate=pl.CostEstimate(
            flops=flops, bytes_accessed=moved, transcendentals=transcendentals
        ),
        name=name,
    )


def in_hbm(*arrays):
    return [pltpu.with_memory_space_constraint(a, pltpu.HBM) for a in arrays]


def body(
    prompt_q,
    prompt_k,
    prompt_value_rows,
    prompt_dout,
    comp_q,
    completion_keys,
    completion_values,
    comp_dout,
    comp_lengths,
    prompt_length,
):
    block = (DEVICES, SLOTS, 2 * HALF_WIDTH)
    operands = (OPERAND_ROWS, HALF_COLUMNS)
    results = (RESULT_ROWS, HALF_COLUMNS)
    swap = [(device, device ^ 1) for device in range(DEVICES)]

    def exchange(blocks):
        return lax.all_to_all(
            blocks, "sample", split_axis=0, concat_axis=0, axis_index_groups=[ORDER], tiled=True
        )

    (outgoing,) = kernel(
        stage_kernel,
        "stage",
        [block],
        [ANY] * 2,
        (VMEM,),
        4,
        (0, 300_000, 0),
        [
            pltpu.VMEM((2, SLOTS, KEY_VALUE_HEADS * HEAD_DIM), jnp.bfloat16),
            pltpu.SemaphoreType.DMA((2,)),
        ],
    )(*in_hbm(prompt_k, prompt_value_rows))
    kv = exchange(outgoing)
    mine, theirs = kernel(
        split_kernel,
        "split",
        [operands] * 2,
        [SMEM] + [ANY] * 7,
        (VMEM,) * 2,
        8,
        (0, 3_000_000, 0),
        [pltpu.SemaphoreType.DMA((16,))],
    )(
        comp_lengths,
        *in_hbm(
            comp_q[0],
            comp_dout[0],
            prompt_q,
            prompt_dout,
            completion_keys[0],
            completion_values[0],
        ),
        outgoing,
    )
    got = lax.ppermute(theirs, "sample", swap)
    valid = pl.pallas_call(
        valid_kernel,
        out_shape=jax.ShapeDtypeStruct((8, LANES), jnp.float32),
        in_specs=[VMEM] * 2,
        out_specs=VMEM,
        compiler_params=pltpu.CompilerParams(vmem_limit_bytes=4 * 1024 * 1024),
        cost_estimate=pl.CostEstimate(flops=10_000, bytes_accessed=1_700_000, transcendentals=0),
        name="valid",
    )(mine, got)
    scores_in = prompt_length, mine, got, valid, kv
    cost = (1_000_000_000, 4_000_000, 850_000)
    (partial,) = kernel(
        attend_kernel, "attend", [block], [SMEM] + [VMEM] * 4, (VMEM,), 24, cost
    )(*scores_in)
    terms = exchange(partial)
    mine_out, theirs_out = kernel(
        grads_kernel, "grads", [results] * 2, [SMEM] + [VMEM] * 4 + [ANY], (VMEM,) * 2, 24, cost
    )(*scores_in, partial)
    got_out = lax.ppermute(theirs_out, "sample", swap)
    width = KEY_VALUE_HEADS * HEAD_DIM
    shapes = (
        (SLOTS, QUERY_HEADS * HEAD_DIM),
        (ROWS, QUERY_HEADS * HEAD_DIM),
        (ROWS, width),
        (ROWS, width),
    )
    pdq, cdq, cdk, cdv = kernel(
        join_kernel,
        "join",
        shapes,
        [VMEM] * 2,
        (ANY,) * 4,
        4,
        (0, 1_700_000, 0),
        [pltpu.SemaphoreType.DMA((12,))],
    )(mine_out, got_out)
    pdk, pdv = kernel(
        total_kernel, "total", [(SLOTS, width)] * 2, [VMEM], (VMEM,) * 2, 4, (130_000, 300_000, 0)
    )(terms)
    return (pdq, pdk, pdv, cdq[None], cdk[None], cdv[None])


def solution(mesh):
    rows = P(("prompt", "sample"), None)
    blocks = P(("prompt", "sample"), None, None)
    in_specs = (rows,) * 4 + (blocks,) * 4 + (P(("prompt", "sample")), P("prompt"))
    out_specs = (rows,) * 3 + (blocks,) * 3
    return jax.shard_map(body, mesh=mesh, in_specs=in_specs, out_specs=out_specs, check_vma=False)
```

```python
import jax
import jax.numpy as jnp
from jax import lax
from jax.experimental import pallas as pl
from jax.experimental.pallas import tpu as pltpu
from jax.sharding import PartitionSpec as P

QUERY_HEADS = 16
KEY_VALUE_HEADS = 4
HEAD_DIM = 128
GROUP = QUERY_HEADS // KEY_VALUE_HEADS
SCALE = HEAD_DIM ** (-0.5)
LOG2E = 1.4426950408889634
CHIPS = 8
CORES = 2
DEVICES = CHIPS * CORES
MASKED = -1e30

HALF_HEADS = KEY_VALUE_HEADS // CORES
HALF_WIDTH = HALF_HEADS * HEAD_DIM
HALF_COLUMNS = HALF_WIDTH * GROUP

SLOTS = 16
ROWS = 128
KEYS = DEVICES * SLOTS
LANES = GROUP * ROWS

PROMPT_ROW = ROWS
EXTRA_ROW = ROWS + SLOTS
QUERY_BLOCK = EXTRA_ROW + SLOTS
OTHER_BLOCK = EXTRA_ROW + ROWS // 2

ORDER = [
    chip % CHIPS * CORES + core
    for step in range(CHIPS)
    for core in range(CORES)
    for chip in [3 * step + core * (CHIPS // CORES)]
]
PLACE = [ORDER.index(device) for device in range(DEVICES)]

NT = ((1,), (1,))
NN = ((1,), (0,))
VMEM = pl.BlockSpec(memory_space=pltpu.VMEM)
SMEM = pl.BlockSpec(memory_space=pltpu.SMEM)
ANY = pl.BlockSpec(memory_space=pl.ANY)


def dot(a, b, contract):
    return lax.dot_general(a, b, (contract, ((), ())), preferred_element_type=jnp.float32)


def own_core():
    return lax.rem(lax.axis_index("sample"), CORES)


def columns_of(core, width):
    return pl.ds(pl.multiple_of(core * width, HEAD_DIM), width)


def run(copies):
    for copy in copies:
        copy.start()
    for copy in copies:
        copy.wait()


def stage_kernel(k_ref, v_ref, out_ref, kv_ref, sems):
    run(
        [
            pltpu.make_async_copy(source, kv_ref.at[n], sems.at[n])
            for n, source in enumerate((k_ref, v_ref))
        ]
    )
    for core in range(CORES):
        columns = slice(core * HALF_WIDTH, (core + 1) * HALF_WIDTH)
        rows = jnp.concatenate([kv_ref[0, :, columns], kv_ref[1, :, columns]], axis=1)
        for chip in range(CHIPS):
            out_ref[PLACE[chip * CORES + core]] = rows


def packed(ref, n):
    return ref.at[EXTRA_ROW:OTHER_BLOCK, n * HALF_WIDTH : (n + 1) * HALF_WIDTH]


def split_kernel(clen_ref, q_ref, do_ref, pq_ref, pdo_ref, ck_ref, cv_ref, _, *refs):
    core = own_core()
    sems = refs[-1]
    copies = []
    for n, half in enumerate((core, 1 - core)):
        query_block, other_block = refs[2 * n : 2 * n + 2]
        wide, narrow = columns_of(half, HALF_COLUMNS), columns_of(half, HALF_WIDTH)
        pairs = [
            (q_ref.at[:, wide], query_block.at[:ROWS]),
            (pq_ref.at[:, wide], query_block.at[PROMPT_ROW:EXTRA_ROW]),
            (do_ref.at[:, wide], other_block.at[:ROWS]),
            (pdo_ref.at[:, wide], other_block.at[PROMPT_ROW:EXTRA_ROW]),
        ]
        for k, source in enumerate((ck_ref, cv_ref)):
            for part in range(2):
                rows = slice(part * ROWS // 2, (part + 1) * ROWS // 2)
                pairs.append((source.at[rows, narrow], packed(other_block, 2 * k + part)))
        copies += [
            pltpu.make_async_copy(source, place, sems.at[n * len(pairs) + k])
            for k, (source, place) in enumerate(pairs)
        ]
    for copy in copies:
        copy.start()
    length = jnp.full((SLOTS, HALF_COLUMNS), clen_ref[0], jnp.int32).astype(jnp.float32)
    for query_block in refs[0:4:2]:
        query_block[EXTRA_ROW:QUERY_BLOCK] = length.astype(jnp.bfloat16)
    for copy in copies:
        copy.wait()


def head_columns(ref, first_row, count, head):
    parts = [
        ref[
            first_row : first_row + count,
            (head * GROUP + g) * HEAD_DIM : (head * GROUP + g + 1) * HEAD_DIM,
        ]
        for g in range(GROUP)
    ]
    return jnp.concatenate(parts, axis=0)


def own_rows(ref, head, first):
    parts = [
        packed(ref, first + part)[:, head * HEAD_DIM : (head + 1) * HEAD_DIM]
        for part in range(2)
    ]
    return jnp.concatenate(parts, axis=0)


def softmax_terms(scores, valid):
    factor = SCALE * LOG2E
    peak = jnp.max(scores, axis=0, keepdims=True)
    terms = jnp.exp2(scores * factor - peak * factor)
    total = jnp.sum(terms, axis=0, keepdims=True)
    return terms * (valid / total)


def score_gradient(soft, soft_b, soft_grad):
    delta = jnp.sum(soft_b.astype(jnp.float32) * soft_grad, axis=0, keepdims=True)
    return (soft * (soft_grad - delta)).astype(jnp.bfloat16)


class Attention:
    def __init__(self, plen_ref, mine_q, mine_other, got_q, got_other, kv_ref):
        self.sides = (mine_q, mine_other), (got_q, got_other)
        self.kv_ref = kv_ref
        plen = plen_ref[0]
        own = lax.axis_index("sample")
        other = own + 1 - 2 * own_core()
        row_lane = lax.rem(lax.broadcasted_iota(jnp.int32, (1, LANES), 1), ROWS)
        self.valid = []
        for ref, _ in self.sides:
            length = ref[EXTRA_ROW:QUERY_BLOCK, :LANES].astype(jnp.float32)[0:1]
            live = row_lane.astype(jnp.float32) < length
            self.valid.append(jnp.where(live, 1.0, 0.0).astype(jnp.float32))
        self.safe = KEYS - 2 * SLOTS
        self.tail_ok = (
            lax.broadcasted_iota(jnp.int32, (2 * SLOTS, LANES), 0) + self.safe < plen
        )
        self.own_ok = lax.broadcasted_iota(jnp.int32, (ROWS, LANES), 0) <= row_lane
        lanes = CORES * GROUP * SLOTS
        lane = lax.broadcasted_iota(jnp.int32, (1, lanes), 1)
        device = jnp.where(lane < GROUP * SLOTS, own, other)
        global_row = device * SLOTS + lax.rem(lane, SLOTS)
        self.prompt_valid = jnp.where(global_row < plen, 1.0, 0.0).astype(jnp.float32)
        self.prompt_ok = lax.broadcasted_iota(jnp.int32, (KEYS, lanes), 0) <= global_row

    def prompt_rows(self, start):
        parts = [
            self.kv_ref[PLACE[device], :, start : start + HEAD_DIM] for device in range(DEVICES)
        ]
        return jnp.concatenate(parts, axis=0)

    def products(self, head, side):
        keys = self.prompt_rows(head * HEAD_DIM)
        values = self.prompt_rows(HALF_WIDTH + head * HEAD_DIM)
        if side < CORES:
            query_block, other_block = self.sides[side]
            keys = jnp.concatenate([keys, own_rows(other_block, head, 0)], axis=0)
            values = jnp.concatenate([values, own_rows(other_block, head, 2)], axis=0)
            q = head_columns(query_block, 0, ROWS, head)
            do = head_columns(other_block, 0, ROWS, head)
        else:
            q, do = (
                jnp.concatenate(
                    [head_columns(ref, PROMPT_ROW, SLOTS, head) for ref in blocks], axis=0
                )
                for blocks in zip(*self.sides)
            )
        return dot(keys, q, NT), dot(values, do, NT), (keys, q, do)

    def weights(self, side, scores, soft_grad):
        if side < CORES:
            scores = jnp.concatenate(
                [
                    scores[: self.safe],
                    jnp.where(self.tail_ok, scores[self.safe : KEYS], MASKED),
                    jnp.where(self.own_ok, scores[KEYS:], MASKED),
                ],
                axis=0,
            )
            valid = self.valid[side]
        else:
            scores = jnp.where(self.prompt_ok, scores, MASKED)
            valid = self.prompt_valid
        soft = softmax_terms(scores, valid)
        soft_b = soft.astype(jnp.bfloat16)
        return soft_b, score_gradient(soft, soft_b, soft_grad)

    def units(self):
        todo = [(head, side) for head in range(HALF_HEADS) for side in (0, 1, 2)]
        following = self.products(*todo[0])
        for n, (head, side) in enumerate(todo):
            scores, soft_grad, operands = following
            if n + 1 < len(todo):
                following = self.products(*todo[n + 1])
            yield head, side, operands, *self.weights(side, scores, soft_grad)


def attend_kernel(*refs):
    part_ref = refs[-1]
    dk = dv = None
    for head, side, (_, q, do), soft_b, grad_b in Attention(*refs[:6]).units():
        more_dv = dot(soft_b[:KEYS], do, NN)
        more_dk = dot(grad_b[:KEYS], q, NN)
        dv = more_dv if side == 0 else dv + more_dv
        dk = more_dk if side == 0 else dk + more_dk
        if side == CORES:
            for start, grad in ((head, dk * SCALE), (HALF_HEADS + head, dv)):
                grad = grad.astype(jnp.bfloat16)
                for device in range(DEVICES):
                    part_ref[PLACE[device], :, start * HEAD_DIM : (start + 1) * HEAD_DIM] = grad[
                        device * SLOTS : (device + 1) * SLOTS
                    ]


def grads_kernel(*refs):
    outs = refs[-2:]
    half = ROWS // 2
    for head, side, (keys, q, do), soft_b, grad_b in Attention(*refs[:6]).units():
        dq_t = dot(keys.T, grad_b, NN) * SCALE
        if side == CORES:
            dq = dq_t.T.astype(jnp.bfloat16)
            for n, out in enumerate(outs):
                for g in range(GROUP):
                    column = (head * GROUP + g) * HEAD_DIM
                    row = (n * GROUP + g) * SLOTS
                    out[PROMPT_ROW:EXTRA_ROW, column : column + HEAD_DIM] = dq[
                        row : row + SLOTS
                    ]
            continue
        out = outs[side]
        for g in range(GROUP):
            column = (head * GROUP + g) * HEAD_DIM
            block = dq_t[:, g * ROWS : (g + 1) * ROWS]
            out[:ROWS, column : column + HEAD_DIM] = block.T.astype(jnp.bfloat16)
        own_dk = (dot(grad_b[KEYS:], q, NN) * SCALE).astype(jnp.bfloat16)
        own_dv = dot(soft_b[KEYS:], do, NN).astype(jnp.bfloat16)
        for n, grad in enumerate((own_dk, own_dv)):
            for part in range(2):
                column = (2 * n + part) * HALF_WIDTH + head * HEAD_DIM
                out[EXTRA_ROW:OTHER_BLOCK, column : column + HEAD_DIM] = grad[
                    part * half : (part + 1) * half
                ]


def join_kernel(mine_ref, got_ref, pdq_ref, cdq_ref, cdk_ref, cdv_ref, sems):
    core = own_core()
    copies = []
    for n, (source, half) in enumerate(((mine_ref, core), (got_ref, 1 - core))):
        wide, narrow = columns_of(half, HALF_COLUMNS), columns_of(half, HALF_WIDTH)
        pairs = [
            (source.at[:ROWS], cdq_ref.at[:, wide]),
            (source.at[PROMPT_ROW:EXTRA_ROW], pdq_ref.at[:, wide]),
        ]
        for k, target in enumerate((cdk_ref, cdv_ref)):
            for part in range(2):
                rows = slice(part * ROWS // 2, (part + 1) * ROWS // 2)
                pairs.append((packed(source, 2 * k + part), target.at[rows, narrow]))
        copies += [
            pltpu.make_async_copy(place, target, sems.at[n * len(pairs) + k])
            for k, (place, target) in enumerate(pairs)
        ]
    run(copies)


def total_kernel(terms_ref, dk_ref, dv_ref):
    for core in range(CORES):
        total = sum(
            terms_ref[PLACE[chip * CORES + core]].astype(jnp.float32) for chip in range(CHIPS)
        ).astype(jnp.bfloat16)
        columns = slice(core * HALF_WIDTH, (core + 1) * HALF_WIDTH)
        dk_ref[:, columns] = total[:, :HALF_WIDTH]
        dv_ref[:, columns] = total[:, HALF_WIDTH:]


def kernel(body, name, shapes, in_specs, out_specs, limit, cost, scratch=(), to_vmem=False):
    flops, moved, transcendentals = cost
    shaped = pltpu.VMEM if to_vmem else jax.ShapeDtypeStruct
    return pl.pallas_call(
        body,
        out_shape=tuple(shaped(shape, jnp.bfloat16) for shape in shapes),
        in_specs=in_specs,
        out_specs=out_specs,
        scratch_shapes=list(scratch),
        compiler_params=pltpu.CompilerParams(vmem_limit_bytes=limit * 1024 * 1024),
        cost_estimate=pl.CostEstimate(
            flops=flops, bytes_accessed=moved, transcendentals=transcendentals
        ),
        name=name,
    )


def in_hbm(*arrays):
    return [pltpu.with_memory_space_constraint(a, pltpu.HBM) for a in arrays]


def body(
    prompt_q,
    prompt_k,
    prompt_value_rows,
    prompt_dout,
    comp_q,
    completion_keys,
    completion_values,
    comp_dout,
    comp_lengths,
    prompt_length,
):
    block = (DEVICES, SLOTS, 2 * HALF_WIDTH)
    queries = (QUERY_BLOCK, HALF_COLUMNS)
    others = (OTHER_BLOCK, HALF_COLUMNS)
    swap = [(device, device ^ 1) for device in range(DEVICES)]

    def exchange(blocks):
        return lax.all_to_all(
            blocks, "sample", split_axis=0, concat_axis=0, axis_index_groups=[ORDER], tiled=True
        )

    (outgoing,) = kernel(
        stage_kernel,
        "stage",
        [block],
        [ANY] * 2,
        (VMEM,),
        4,
        (0, 300_000, 0),
        [
            pltpu.VMEM((2, SLOTS, KEY_VALUE_HEADS * HEAD_DIM), jnp.bfloat16),
            pltpu.SemaphoreType.DMA((2,)),
        ],
        to_vmem=True,
    )(*in_hbm(prompt_k, prompt_value_rows))
    kv = exchange(outgoing)
    mine_q, mine_other, their_q, their_other = kernel(
        split_kernel,
        "split",
        [queries, others] * 2,
        [SMEM] + [ANY] * 7,
        (VMEM,) * 4,
        8,
        (0, 3_000_000, 0),
        [pltpu.SemaphoreType.DMA((16,))],
    )(
        comp_lengths,
        *in_hbm(
            comp_q[0],
            comp_dout[0],
            prompt_q,
            prompt_dout,
            completion_keys[0],
            completion_values[0],
        ),
        outgoing,
    )
    got_q = lax.ppermute(their_q, "sample", swap)
    got_other = lax.ppermute(their_other, "sample", swap)
    scores_in = prompt_length, mine_q, mine_other, got_q, got_other, kv
    cost = (1_000_000_000, 4_000_000, 850_000)
    (partial,) = kernel(
        attend_kernel, "attend", [block], [SMEM] + [VMEM] * 5, (VMEM,), 24, cost, to_vmem=True
    )(*scores_in)
    terms = exchange(partial)
    mine_out, theirs_out = kernel(
        grads_kernel, "grads", [others] * 2, [SMEM] + [VMEM] * 5 + [ANY], (VMEM,) * 2, 24, cost
    )(*scores_in, partial)
    got_out = lax.ppermute(theirs_out, "sample", swap)
    width = KEY_VALUE_HEADS * HEAD_DIM
    shapes = (
        (SLOTS, QUERY_HEADS * HEAD_DIM),
        (ROWS, QUERY_HEADS * HEAD_DIM),
        (ROWS, width),
        (ROWS, width),
    )
    pdq, cdq, cdk, cdv = kernel(
        join_kernel,
        "join",
        shapes,
        [VMEM] * 2,
        (ANY,) * 4,
        4,
        (0, 1_700_000, 0),
        [pltpu.SemaphoreType.DMA((12,))],
    )(mine_out, got_out)
    pdk, pdv = kernel(
        total_kernel, "total", [(SLOTS, width)] * 2, [VMEM], (VMEM,) * 2, 4, (130_000, 300_000, 0)
    )(terms)
    return (pdq, pdk, pdv, cdq[None], cdk[None], cdv[None])


def solution(mesh):
    rows = P(("prompt", "sample"), None)
    blocks = P(("prompt", "sample"), None, None)
    in_specs = (rows,) * 4 + (blocks,) * 4 + (P(("prompt", "sample")), P("prompt"))
    out_specs = (rows,) * 3 + (blocks,) * 3
    return jax.shard_map(body, mesh=mesh, in_specs=in_specs, out_specs=out_specs, check_vma=False)
```

```python
import jax
import jax.numpy as jnp
from jax import lax
from jax.experimental import pallas as pl
from jax.experimental.pallas import tpu as pltpu
from jax.sharding import PartitionSpec as P

QUERY_HEADS = 16
KEY_VALUE_HEADS = 4
HEAD_DIM = 128
GROUP = QUERY_HEADS // KEY_VALUE_HEADS
SCALE = HEAD_DIM ** (-0.5)
LOG2E = 1.4426950408889634
CHIPS = 8
CORES = 2
DEVICES = CHIPS * CORES
MASKED = -1e30

HALF_HEADS = KEY_VALUE_HEADS // CORES
HALF_WIDTH = HALF_HEADS * HEAD_DIM
HALF_COLUMNS = HALF_WIDTH * GROUP

SLOTS = 16
ROWS = 128
KEYS = DEVICES * SLOTS
LANES = GROUP * ROWS

PROMPT_ROW = ROWS
EXTRA_ROW = ROWS + SLOTS
QUERY_BLOCK = EXTRA_ROW + SLOTS
OTHER_BLOCK = EXTRA_ROW + ROWS // 2

GATHER_ORDER = [3 * step % CHIPS * CORES + core for core in range(CORES) for step in range(CHIPS)]
GATHER_PLACE = [GATHER_ORDER.index(device) for device in range(DEVICES)]
SUM_ORDER = [
    (chip + core * (CHIPS // CORES)) % CHIPS * CORES + core
    for chip in (0, 2, 1, 3, 4, 6, 5, 7)
    for core in range(CORES)
]
SUM_PLACE = [SUM_ORDER.index(device) for device in range(DEVICES)]

NT = ((1,), (1,))
NN = ((1,), (0,))
VMEM = pl.BlockSpec(memory_space=pltpu.VMEM)
SMEM = pl.BlockSpec(memory_space=pltpu.SMEM)
ANY = pl.BlockSpec(memory_space=pl.ANY)


def dot(a, b, contract):
    return lax.dot_general(a, b, (contract, ((), ())), preferred_element_type=jnp.float32)


def own_core():
    return lax.rem(lax.axis_index("sample"), CORES)


def columns_of(core, width):
    return pl.ds(pl.multiple_of(core * width, HEAD_DIM), width)


def run(copies):
    for copy in copies:
        copy.start()
    for copy in copies:
        copy.wait()


def stage_kernel(k_ref, v_ref, out_ref, sems):
    run(
        [
            pltpu.make_async_copy(
                source.at[:, device % CORES * HALF_WIDTH : (device % CORES + 1) * HALF_WIDTH],
                out_ref.at[place, :, n * HALF_WIDTH : (n + 1) * HALF_WIDTH],
                sems.at[2 * place + n],
            )
            for place, device in enumerate(GATHER_ORDER)
            for n, source in enumerate((k_ref, v_ref))
        ]
    )


def packed(ref, n):
    return ref.at[EXTRA_ROW:OTHER_BLOCK, n * HALF_WIDTH : (n + 1) * HALF_WIDTH]


def split_kernel(clen_ref, q_ref, do_ref, pq_ref, pdo_ref, ck_ref, cv_ref, _, *refs):
    core = own_core()
    sems = refs[-1]
    copies = []
    for n, half in enumerate((core, 1 - core)):
        query_block, other_block = refs[2 * n : 2 * n + 2]
        wide, narrow = columns_of(half, HALF_COLUMNS), columns_of(half, HALF_WIDTH)
        pairs = [
            (q_ref.at[:, wide], query_block.at[:ROWS]),
            (pq_ref.at[:, wide], query_block.at[PROMPT_ROW:EXTRA_ROW]),
            (do_ref.at[:, wide], other_block.at[:ROWS]),
            (pdo_ref.at[:, wide], other_block.at[PROMPT_ROW:EXTRA_ROW]),
        ]
        for k, source in enumerate((ck_ref, cv_ref)):
            for part in range(2):
                rows = slice(part * ROWS // 2, (part + 1) * ROWS // 2)
                pairs.append((source.at[rows, narrow], packed(other_block, 2 * k + part)))
        copies += [
            pltpu.make_async_copy(source, place, sems.at[n * len(pairs) + k])
            for k, (source, place) in enumerate(pairs)
        ]
    for copy in copies:
        copy.start()
    length = jnp.full((SLOTS, HALF_COLUMNS), clen_ref[0], jnp.int32).astype(jnp.float32)
    for query_block in refs[0:4:2]:
        query_block[EXTRA_ROW:QUERY_BLOCK] = length.astype(jnp.bfloat16)
    for copy in copies:
        copy.wait()


def head_columns(ref, first_row, count, head):
    parts = [
        ref[
            first_row : first_row + count,
            (head * GROUP + g) * HEAD_DIM : (head * GROUP + g + 1) * HEAD_DIM,
        ]
        for g in range(GROUP)
    ]
    return jnp.concatenate(parts, axis=0)


def own_rows(ref, head, first):
    parts = [
        packed(ref, first + part)[:, head * HEAD_DIM : (head + 1) * HEAD_DIM]
        for part in range(2)
    ]
    return jnp.concatenate(parts, axis=0)


def softmax_terms(scores, valid):
    factor = SCALE * LOG2E
    peak = jnp.max(scores, axis=0, keepdims=True)
    terms = jnp.exp2(scores * factor - peak * factor)
    total = jnp.sum(terms, axis=0, keepdims=True)
    return terms * (valid / total)


def score_gradient(soft, soft_b, soft_grad):
    delta = jnp.sum(soft_b.astype(jnp.float32) * soft_grad, axis=0, keepdims=True)
    return (soft * (soft_grad - delta)).astype(jnp.bfloat16)


class Attention:
    def __init__(self, plen_ref, mine_q, mine_other, got_q, got_other, kv_ref):
        self.sides = (mine_q, mine_other), (got_q, got_other)
        self.kv_ref = kv_ref
        plen = plen_ref[0]
        own = lax.axis_index("sample")
        other = own + 1 - 2 * own_core()
        row_lane = lax.rem(lax.broadcasted_iota(jnp.int32, (1, LANES), 1), ROWS)
        self.valid = []
        for ref, _ in self.sides:
            length = ref[EXTRA_ROW:QUERY_BLOCK, :LANES].astype(jnp.float32)[0:1]
            live = row_lane.astype(jnp.float32) < length
            self.valid.append(jnp.where(live, 1.0, 0.0).astype(jnp.float32))
        self.safe = KEYS - 2 * SLOTS
        self.tail_ok = (
            lax.broadcasted_iota(jnp.int32, (2 * SLOTS, LANES), 0) + self.safe < plen
        )
        self.own_ok = lax.broadcasted_iota(jnp.int32, (ROWS, LANES), 0) <= row_lane
        lanes = CORES * GROUP * SLOTS
        lane = lax.broadcasted_iota(jnp.int32, (1, lanes), 1)
        device = jnp.where(lane < GROUP * SLOTS, own, other)
        global_row = device * SLOTS + lax.rem(lane, SLOTS)
        self.prompt_valid = jnp.where(global_row < plen, 1.0, 0.0).astype(jnp.float32)
        self.prompt_ok = lax.broadcasted_iota(jnp.int32, (KEYS, lanes), 0) <= global_row

    def prompt_rows(self, start):
        parts = [
            self.kv_ref[GATHER_PLACE[device], :, start : start + HEAD_DIM] for device in range(DEVICES)
        ]
        return jnp.concatenate(parts, axis=0)

    def products(self, head, side):
        keys = self.prompt_rows(head * HEAD_DIM)
        values = self.prompt_rows(HALF_WIDTH + head * HEAD_DIM)
        if side < CORES:
            query_block, other_block = self.sides[side]
            keys = jnp.concatenate([keys, own_rows(other_block, head, 0)], axis=0)
            values = jnp.concatenate([values, own_rows(other_block, head, 2)], axis=0)
            q = head_columns(query_block, 0, ROWS, head)
            do = head_columns(other_block, 0, ROWS, head)
        else:
            q, do = (
                jnp.concatenate(
                    [head_columns(ref, PROMPT_ROW, SLOTS, head) for ref in blocks], axis=0
                )
                for blocks in zip(*self.sides)
            )
        return dot(keys, q, NT), dot(values, do, NT), (keys, q, do)

    def weights(self, side, scores, soft_grad):
        if side < CORES:
            scores = jnp.concatenate(
                [
                    scores[: self.safe],
                    jnp.where(self.tail_ok, scores[self.safe : KEYS], MASKED),
                    jnp.where(self.own_ok, scores[KEYS:], MASKED),
                ],
                axis=0,
            )
            valid = self.valid[side]
        else:
            scores = jnp.where(self.prompt_ok, scores, MASKED)
            valid = self.prompt_valid
        soft = softmax_terms(scores, valid)
        soft_b = soft.astype(jnp.bfloat16)
        return soft_b, score_gradient(soft, soft_b, soft_grad)

    def units(self):
        todo = [(head, side) for head in range(HALF_HEADS) for side in (0, 1, 2)]
        following = self.products(*todo[0])
        for n, (head, side) in enumerate(todo):
            scores, soft_grad, operands = following
            if n + 1 < len(todo):
                following = self.products(*todo[n + 1])
            yield head, side, operands, *self.weights(side, scores, soft_grad)


def attend_kernel(*refs):
    part_ref = refs[-1]
    dk = dv = None
    for head, side, (_, q, do), soft_b, grad_b in Attention(*refs[:6]).units():
        more_dv = dot(soft_b[:KEYS], do, NN)
        more_dk = dot(grad_b[:KEYS], q, NN)
        dv = more_dv if side == 0 else dv + more_dv
        dk = more_dk if side == 0 else dk + more_dk
        if side == CORES:
            for start, grad in ((head, dk * SCALE), (HALF_HEADS + head, dv)):
                grad = grad.astype(jnp.bfloat16)
                for device in range(DEVICES):
                    part_ref[SUM_PLACE[device], :, start * HEAD_DIM : (start + 1) * HEAD_DIM] = grad[
                        device * SLOTS : (device + 1) * SLOTS
                    ]


def grads_kernel(*refs):
    outs = refs[-2:]
    half = ROWS // 2
    for head, side, (keys, q, do), soft_b, grad_b in Attention(*refs[:6]).units():
        dq_t = dot(keys.T, grad_b, NN) * SCALE
        if side == CORES:
            dq = dq_t.T.astype(jnp.bfloat16)
            for n, out in enumerate(outs):
                for g in range(GROUP):
                    column = (head * GROUP + g) * HEAD_DIM
                    row = (n * GROUP + g) * SLOTS
                    out[PROMPT_ROW:EXTRA_ROW, column : column + HEAD_DIM] = dq[
                        row : row + SLOTS
                    ]
            continue
        out = outs[side]
        for g in range(GROUP):
            column = (head * GROUP + g) * HEAD_DIM
            block = dq_t[:, g * ROWS : (g + 1) * ROWS]
            out[:ROWS, column : column + HEAD_DIM] = block.T.astype(jnp.bfloat16)
        own_dk = (dot(grad_b[KEYS:], q, NN) * SCALE).astype(jnp.bfloat16)
        own_dv = dot(soft_b[KEYS:], do, NN).astype(jnp.bfloat16)
        for n, grad in enumerate((own_dk, own_dv)):
            for part in range(2):
                column = (2 * n + part) * HALF_WIDTH + head * HEAD_DIM
                out[EXTRA_ROW:OTHER_BLOCK, column : column + HEAD_DIM] = grad[
                    part * half : (part + 1) * half
                ]


def join_kernel(mine_ref, got_ref, pdq_ref, cdq_ref, cdk_ref, cdv_ref, sems):
    core = own_core()
    copies = []
    for n, (source, half) in enumerate(((mine_ref, core), (got_ref, 1 - core))):
        wide, narrow = columns_of(half, HALF_COLUMNS), columns_of(half, HALF_WIDTH)
        pairs = [
            (source.at[:ROWS], cdq_ref.at[:, wide]),
            (source.at[PROMPT_ROW:EXTRA_ROW], pdq_ref.at[:, wide]),
        ]
        for k, target in enumerate((cdk_ref, cdv_ref)):
            for part in range(2):
                rows = slice(part * ROWS // 2, (part + 1) * ROWS // 2)
                pairs.append((packed(source, 2 * k + part), target.at[rows, narrow]))
        copies += [
            pltpu.make_async_copy(place, target, sems.at[n * len(pairs) + k])
            for k, (place, target) in enumerate(pairs)
        ]
    run(copies)


def total_kernel(terms_ref, dk_ref, dv_ref):
    for core in range(CORES):
        total = sum(
            terms_ref[SUM_PLACE[chip * CORES + core]].astype(jnp.float32) for chip in range(CHIPS)
        ).astype(jnp.bfloat16)
        columns = slice(core * HALF_WIDTH, (core + 1) * HALF_WIDTH)
        dk_ref[:, columns] = total[:, :HALF_WIDTH]
        dv_ref[:, columns] = total[:, HALF_WIDTH:]


def kernel(body, name, shapes, in_specs, out_specs, limit, cost, scratch=()):
    flops, moved, transcendentals = cost
    return pl.pallas_call(
        body,
        out_shape=tuple(jax.ShapeDtypeStruct(shape, jnp.bfloat16) for shape in shapes),
        in_specs=in_specs,
        out_specs=out_specs,
        scratch_shapes=list(scratch),
        compiler_params=pltpu.CompilerParams(vmem_limit_bytes=limit * 1024 * 1024),
        cost_estimate=pl.CostEstimate(
            flops=flops, bytes_accessed=moved, transcendentals=transcendentals
        ),
        name=name,
    )


def in_hbm(*arrays):
    return [pltpu.with_memory_space_constraint(a, pltpu.HBM) for a in arrays]


def body(
    prompt_q,
    prompt_k,
    prompt_value_rows,
    prompt_dout,
    comp_q,
    completion_keys,
    completion_values,
    comp_dout,
    comp_lengths,
    prompt_length,
):
    block = (DEVICES, SLOTS, 2 * HALF_WIDTH)
    queries = (QUERY_BLOCK, HALF_COLUMNS)
    others = (OTHER_BLOCK, HALF_COLUMNS)
    swap = [(device, device ^ 1) for device in range(DEVICES)]

    def exchange(blocks, order):
        return lax.all_to_all(
            blocks, "sample", split_axis=0, concat_axis=0, axis_index_groups=[order], tiled=True
        )

    (outgoing,) = kernel(
        stage_kernel,
        "stage",
        [block],
        [ANY] * 2,
        (ANY,),
        4,
        (0, 500_000, 0),
        [pltpu.SemaphoreType.DMA((2 * DEVICES,))],
    )(*in_hbm(prompt_k, prompt_value_rows))
    kv = exchange(outgoing, GATHER_ORDER)
    mine_q, mine_other, their_q, their_other = kernel(
        split_kernel,
        "split",
        [queries, others] * 2,
        [SMEM] + [ANY] * 7,
        (VMEM,) * 4,
        8,
        (0, 3_000_000, 0),
        [pltpu.SemaphoreType.DMA((16,))],
    )(
        comp_lengths,
        *in_hbm(
            comp_q[0],
            comp_dout[0],
            prompt_q,
            prompt_dout,
            completion_keys[0],
            completion_values[0],
        ),
        outgoing,
    )
    got_q = lax.ppermute(their_q, "sample", swap)
    got_other = lax.ppermute(their_other, "sample", swap)
    scores_in = prompt_length, mine_q, mine_other, got_q, got_other, kv
    cost = (1_000_000_000, 4_000_000, 850_000)
    (partial,) = kernel(
        attend_kernel, "attend", [block], [SMEM] + [VMEM] * 5, (VMEM,), 24, cost
    )(*scores_in)
    terms = exchange(partial, SUM_ORDER)
    mine_out, theirs_out = kernel(
        grads_kernel, "grads", [others] * 2, [SMEM] + [VMEM] * 5 + [ANY], (VMEM,) * 2, 24, cost
    )(*scores_in, partial)
    got_out = lax.ppermute(theirs_out, "sample", swap)
    width = KEY_VALUE_HEADS * HEAD_DIM
    shapes = (
        (SLOTS, QUERY_HEADS * HEAD_DIM),
        (ROWS, QUERY_HEADS * HEAD_DIM),
        (ROWS, width),
        (ROWS, width),
    )
    pdq, cdq, cdk, cdv = kernel(
        join_kernel,
        "join",
        shapes,
        [VMEM] * 2,
        (ANY,) * 4,
        4,
        (0, 1_700_000, 0),
        [pltpu.SemaphoreType.DMA((12,))],
    )(mine_out, got_out)
    pdk, pdv = kernel(
        total_kernel, "total", [(SLOTS, width)] * 2, [VMEM], (VMEM,) * 2, 4, (130_000, 300_000, 0)
    )(terms)
    return (pdq, pdk, pdv, cdq[None], cdk[None], cdv[None])


def solution(mesh):
    rows = P(("prompt", "sample"), None)
    blocks = P(("prompt", "sample"), None, None)
    in_specs = (rows,) * 4 + (blocks,) * 4 + (P(("prompt", "sample")), P("prompt"))
    out_specs = (rows,) * 3 + (blocks,) * 3
    return jax.shard_map(body, mesh=mesh, in_specs=in_specs, out_specs=out_specs, check_vma=False)
```

```python
import jax
import jax.numpy as jnp
from jax import lax
from jax.experimental import pallas as pl
from jax.experimental.pallas import tpu as pltpu
from jax.sharding import PartitionSpec as P

QUERY_HEADS = 16
KEY_VALUE_HEADS = 4
HEAD_DIM = 128
GROUP = QUERY_HEADS // KEY_VALUE_HEADS
SCALE = HEAD_DIM ** (-0.5)
LOG2E = 1.4426950408889634
CHIPS = 8
CORES = 2
DEVICES = CHIPS * CORES
MASKED = -1e30

HALF_HEADS = KEY_VALUE_HEADS // CORES
HALF_WIDTH = HALF_HEADS * HEAD_DIM
HALF_COLUMNS = HALF_WIDTH * GROUP

SLOTS = 16
ROWS = 128
KEYS = DEVICES * SLOTS

PROMPT_ROW = ROWS
EXTRA_ROW = ROWS + SLOTS
QUERY_BLOCK = EXTRA_ROW + SLOTS
OTHER_BLOCK = EXTRA_ROW + ROWS // 2

ORDER = [
    chip % CHIPS * CORES + core
    for step in range(CHIPS)
    for core in range(CORES)
    for chip in [3 * step + core * (CHIPS // CORES)]
]
PLACE = [ORDER.index(device) for device in range(DEVICES)]

NT = ((1,), (1,))
NN = ((1,), (0,))
VMEM = pl.BlockSpec(memory_space=pltpu.VMEM)
SMEM = pl.BlockSpec(memory_space=pltpu.SMEM)
ANY = pl.BlockSpec(memory_space=pl.ANY)


def dot(a, b, contract):
    return lax.dot_general(a, b, (contract, ((), ())), preferred_element_type=jnp.float32)


def own_core():
    return lax.rem(lax.axis_index("sample"), CORES)


def columns_of(core, width):
    return pl.ds(pl.multiple_of(core * width, HEAD_DIM), width)


def run(copies):
    for copy in copies:
        copy.start()
    for copy in copies:
        copy.wait()


def stage_kernel(k_ref, v_ref, out_ref, kv_ref, sems):
    run(
        [
            pltpu.make_async_copy(source, kv_ref.at[n], sems.at[n])
            for n, source in enumerate((k_ref, v_ref))
        ]
    )
    for core in range(CORES):
        columns = slice(core * HALF_WIDTH, (core + 1) * HALF_WIDTH)
        rows = jnp.concatenate([kv_ref[0, :, columns], kv_ref[1, :, columns]], axis=1)
        for chip in range(CHIPS):
            out_ref[PLACE[chip * CORES + core]] = rows


def packed(ref, n):
    return ref.at[EXTRA_ROW:OTHER_BLOCK, n * HALF_WIDTH : (n + 1) * HALF_WIDTH]


def split_kernel(clen_ref, q_ref, do_ref, pq_ref, pdo_ref, ck_ref, cv_ref, _, *refs):
    core = own_core()
    sems = refs[-1]
    copies = []
    for n, half in enumerate((core, 1 - core)):
        query_block, other_block = refs[2 * n : 2 * n + 2]
        wide, narrow = columns_of(half, HALF_COLUMNS), columns_of(half, HALF_WIDTH)
        pairs = [
            (q_ref.at[:, wide], query_block.at[:ROWS]),
            (pq_ref.at[:, wide], query_block.at[PROMPT_ROW:EXTRA_ROW]),
            (do_ref.at[:, wide], other_block.at[:ROWS]),
            (pdo_ref.at[:, wide], other_block.at[PROMPT_ROW:EXTRA_ROW]),
        ]
        for k, source in enumerate((ck_ref, cv_ref)):
            for part in range(2):
                rows = slice(part * ROWS // 2, (part + 1) * ROWS // 2)
                pairs.append((source.at[rows, narrow], packed(other_block, 2 * k + part)))
        copies += [
            pltpu.make_async_copy(source, place, sems.at[n * len(pairs) + k])
            for k, (source, place) in enumerate(pairs)
        ]
    for copy in copies:
        copy.start()
    length = jnp.full((SLOTS, HALF_COLUMNS), clen_ref[0], jnp.int32).astype(jnp.float32)
    for query_block in refs[0:4:2]:
        query_block[EXTRA_ROW:QUERY_BLOCK] = length.astype(jnp.bfloat16)
    for copy in copies:
        copy.wait()


def head_columns(ref, first_row, count, head):
    parts = [
        ref[
            first_row : first_row + count,
            (head * GROUP + g) * HEAD_DIM : (head * GROUP + g + 1) * HEAD_DIM,
        ]
        for g in range(GROUP)
    ]
    return jnp.concatenate(parts, axis=0)


def own_rows(ref, head, first):
    parts = [
        packed(ref, first + part)[:, head * HEAD_DIM : (head + 1) * HEAD_DIM]
        for part in range(2)
    ]
    return jnp.concatenate(parts, axis=0)


def softmax_terms(scores, valid):
    factor = SCALE * LOG2E
    peak = jnp.max(scores, axis=0, keepdims=True)
    terms = jnp.exp2(scores * factor - peak * factor)
    total = jnp.sum(terms, axis=0, keepdims=True)
    return terms * (valid / total)


def score_gradient(soft, soft_b, soft_grad):
    delta = jnp.sum(soft_b.astype(jnp.float32) * soft_grad, axis=0, keepdims=True)
    return (soft * (soft_grad - delta)).astype(jnp.bfloat16)


class Attention:
    def __init__(self, plen_ref, mine_q, mine_other, got_q, got_other, kv_ref):
        self.sides = (mine_q, mine_other), (got_q, got_other)
        self.kv_ref = kv_ref
        plen = plen_ref[0]
        own = lax.axis_index("sample")
        other = own + 1 - 2 * own_core()
        row_lane = lax.broadcasted_iota(jnp.int32, (1, ROWS), 1)
        self.valid = []
        for ref, _ in self.sides:
            length = ref[EXTRA_ROW:QUERY_BLOCK, :ROWS].astype(jnp.float32)[0:1]
            live = row_lane.astype(jnp.float32) < length
            self.valid.append(jnp.where(live, 1.0, 0.0).astype(jnp.float32))
        self.safe = KEYS - 2 * SLOTS
        self.tail_ok = (
            lax.broadcasted_iota(jnp.int32, (2 * SLOTS, ROWS), 0) + self.safe < plen
        )
        self.own_ok = lax.broadcasted_iota(jnp.int32, (ROWS, ROWS), 0) <= row_lane
        lanes = CORES * GROUP * SLOTS
        lane = lax.broadcasted_iota(jnp.int32, (1, lanes), 1)
        device = jnp.where(lane < GROUP * SLOTS, own, other)
        global_row = device * SLOTS + lax.rem(lane, SLOTS)
        self.prompt_valid = jnp.where(global_row < plen, 1.0, 0.0).astype(jnp.float32)
        self.prompt_ok = lax.broadcasted_iota(jnp.int32, (KEYS, lanes), 0) <= global_row

    def prompt_rows(self, start):
        parts = [
            self.kv_ref[PLACE[device], :, start : start + HEAD_DIM] for device in range(DEVICES)
        ]
        return jnp.concatenate(parts, axis=0)

    def products(self, head, side):
        keys = self.prompt_rows(head * HEAD_DIM)
        values = self.prompt_rows(HALF_WIDTH + head * HEAD_DIM)
        if side < CORES:
            query_block, other_block = self.sides[side]
            keys = jnp.concatenate([keys, own_rows(other_block, head, 0)], axis=0)
            values = jnp.concatenate([values, own_rows(other_block, head, 2)], axis=0)
            q = head_columns(query_block, 0, ROWS, head)
            do = head_columns(other_block, 0, ROWS, head)
        else:
            q, do = (
                jnp.concatenate(
                    [head_columns(ref, PROMPT_ROW, SLOTS, head) for ref in blocks], axis=0
                )
                for blocks in zip(*self.sides)
            )
        return dot(keys, q, NT), dot(values, do, NT), (keys, q, do)

    def weights(self, side, scores, soft_grad):
        pieces = []
        for start in range(0, scores.shape[1], ROWS):
            lanes = slice(start, start + ROWS)
            piece = scores[:, lanes]
            if side < CORES:
                piece = jnp.concatenate(
                    [
                        piece[: self.safe],
                        jnp.where(self.tail_ok, piece[self.safe : KEYS], MASKED),
                        jnp.where(self.own_ok, piece[KEYS:], MASKED),
                    ],
                    axis=0,
                )
                valid = self.valid[side]
            else:
                piece = jnp.where(self.prompt_ok, piece, MASKED)
                valid = self.prompt_valid
            soft = softmax_terms(piece, valid)
            soft_b = soft.astype(jnp.bfloat16)
            pieces.append((soft_b, score_gradient(soft, soft_b, soft_grad[:, lanes])))
        return [jnp.concatenate(part, axis=1) for part in zip(*pieces)]

    def units(self):
        todo = [(head, side) for head in range(HALF_HEADS) for side in (0, 1, 2)]
        following = self.products(*todo[0])
        for n, (head, side) in enumerate(todo):
            scores, soft_grad, operands = following
            if n + 1 < len(todo):
                following = self.products(*todo[n + 1])
            yield head, side, operands, *self.weights(side, scores, soft_grad)


def attend_kernel(*refs):
    part_ref = refs[-1]
    dk = dv = None
    for head, side, (_, q, do), soft_b, grad_b in Attention(*refs[:6]).units():
        more_dv = dot(soft_b[:KEYS], do, NN)
        more_dk = dot(grad_b[:KEYS], q, NN)
        dv = more_dv if side == 0 else dv + more_dv
        dk = more_dk if side == 0 else dk + more_dk
        if side == CORES:
            for start, grad in ((head, dk * SCALE), (HALF_HEADS + head, dv)):
                grad = grad.astype(jnp.bfloat16)
                for device in range(DEVICES):
                    part_ref[PLACE[device], :, start * HEAD_DIM : (start + 1) * HEAD_DIM] = grad[
                        device * SLOTS : (device + 1) * SLOTS
                    ]


def grads_kernel(*refs):
    outs = refs[-2:]
    half = ROWS // 2
    for head, side, (keys, q, do), soft_b, grad_b in Attention(*refs[:6]).units():
        dq_t = dot(keys.T, grad_b, NN) * SCALE
        if side == CORES:
            dq = dq_t.T.astype(jnp.bfloat16)
            for n, out in enumerate(outs):
                for g in range(GROUP):
                    column = (head * GROUP + g) * HEAD_DIM
                    row = (n * GROUP + g) * SLOTS
                    out[PROMPT_ROW:EXTRA_ROW, column : column + HEAD_DIM] = dq[
                        row : row + SLOTS
                    ]
            continue
        out = outs[side]
        for g in range(GROUP):
            column = (head * GROUP + g) * HEAD_DIM
            block = dq_t[:, g * ROWS : (g + 1) * ROWS]
            out[:ROWS, column : column + HEAD_DIM] = block.T.astype(jnp.bfloat16)
        own_dk = (dot(grad_b[KEYS:], q, NN) * SCALE).astype(jnp.bfloat16)
        own_dv = dot(soft_b[KEYS:], do, NN).astype(jnp.bfloat16)
        for n, grad in enumerate((own_dk, own_dv)):
            for part in range(2):
                column = (2 * n + part) * HALF_WIDTH + head * HEAD_DIM
                out[EXTRA_ROW:OTHER_BLOCK, column : column + HEAD_DIM] = grad[
                    part * half : (part + 1) * half
                ]


def join_kernel(mine_ref, got_ref, pdq_ref, cdq_ref, cdk_ref, cdv_ref, sems):
    core = own_core()
    copies = []
    for n, (source, half) in enumerate(((mine_ref, core), (got_ref, 1 - core))):
        wide, narrow = columns_of(half, HALF_COLUMNS), columns_of(half, HALF_WIDTH)
        pairs = [
            (source.at[:ROWS], cdq_ref.at[:, wide]),
            (source.at[PROMPT_ROW:EXTRA_ROW], pdq_ref.at[:, wide]),
        ]
        for k, target in enumerate((cdk_ref, cdv_ref)):
            for part in range(2):
                rows = slice(part * ROWS // 2, (part + 1) * ROWS // 2)
                pairs.append((packed(source, 2 * k + part), target.at[rows, narrow]))
        copies += [
            pltpu.make_async_copy(place, target, sems.at[n * len(pairs) + k])
            for k, (place, target) in enumerate(pairs)
        ]
    run(copies)


def total_kernel(terms_ref, dk_ref, dv_ref):
    for core in range(CORES):
        total = sum(
            terms_ref[PLACE[chip * CORES + core]].astype(jnp.float32) for chip in range(CHIPS)
        ).astype(jnp.bfloat16)
        columns = slice(core * HALF_WIDTH, (core + 1) * HALF_WIDTH)
        dk_ref[:, columns] = total[:, :HALF_WIDTH]
        dv_ref[:, columns] = total[:, HALF_WIDTH:]


def kernel(body, name, shapes, in_specs, out_specs, limit, cost, scratch=()):
    flops, moved, transcendentals = cost
    return pl.pallas_call(
        body,
        out_shape=tuple(jax.ShapeDtypeStruct(shape, jnp.bfloat16) for shape in shapes),
        in_specs=in_specs,
        out_specs=out_specs,
        scratch_shapes=list(scratch),
        compiler_params=pltpu.CompilerParams(vmem_limit_bytes=limit * 1024 * 1024),
        cost_estimate=pl.CostEstimate(
            flops=flops, bytes_accessed=moved, transcendentals=transcendentals
        ),
        name=name,
    )


def in_hbm(*arrays):
    return [pltpu.with_memory_space_constraint(a, pltpu.HBM) for a in arrays]


def body(
    prompt_q,
    prompt_k,
    prompt_value_rows,
    prompt_dout,
    comp_q,
    completion_keys,
    completion_values,
    comp_dout,
    comp_lengths,
    prompt_length,
):
    block = (DEVICES, SLOTS, 2 * HALF_WIDTH)
    queries = (QUERY_BLOCK, HALF_COLUMNS)
    others = (OTHER_BLOCK, HALF_COLUMNS)
    swap = [(device, device ^ 1) for device in range(DEVICES)]

    def exchange(blocks):
        return lax.all_to_all(
            blocks, "sample", split_axis=0, concat_axis=0, axis_index_groups=[ORDER], tiled=True
        )

    (outgoing,) = kernel(
        stage_kernel,
        "stage",
        [block],
        [ANY] * 2,
        (VMEM,),
        4,
        (0, 300_000, 0),
        [
            pltpu.VMEM((2, SLOTS, KEY_VALUE_HEADS * HEAD_DIM), jnp.bfloat16),
            pltpu.SemaphoreType.DMA((2,)),
        ],
    )(*in_hbm(prompt_k, prompt_value_rows))
    kv = exchange(outgoing)
    mine_q, mine_other, their_q, their_other = kernel(
        split_kernel,
        "split",
        [queries, others] * 2,
        [SMEM] + [ANY] * 7,
        (VMEM,) * 4,
        8,
        (0, 3_000_000, 0),
        [pltpu.SemaphoreType.DMA((16,))],
    )(
        comp_lengths,
        *in_hbm(
            comp_q[0],
            comp_dout[0],
            prompt_q,
            prompt_dout,
            completion_keys[0],
            completion_values[0],
        ),
        outgoing,
    )
    got_q = lax.ppermute(their_q, "sample", swap)
    got_other = lax.ppermute(their_other, "sample", swap)
    scores_in = prompt_length, mine_q, mine_other, got_q, got_other, kv
    cost = (1_000_000_000, 4_000_000, 850_000)
    (partial,) = kernel(
        attend_kernel, "attend", [block], [SMEM] + [VMEM] * 5, (VMEM,), 24, cost
    )(*scores_in)
    terms = exchange(partial)
    mine_out, theirs_out = kernel(
        grads_kernel, "grads", [others] * 2, [SMEM] + [VMEM] * 5 + [ANY], (VMEM,) * 2, 24, cost
    )(*scores_in, partial)
    got_out = lax.ppermute(theirs_out, "sample", swap)
    width = KEY_VALUE_HEADS * HEAD_DIM
    shapes = (
        (SLOTS, QUERY_HEADS * HEAD_DIM),
        (ROWS, QUERY_HEADS * HEAD_DIM),
        (ROWS, width),
        (ROWS, width),
    )
    pdq, cdq, cdk, cdv = kernel(
        join_kernel,
        "join",
        shapes,
        [VMEM] * 2,
        (ANY,) * 4,
        4,
        (0, 1_700_000, 0),
        [pltpu.SemaphoreType.DMA((12,))],
    )(mine_out, got_out)
    pdk, pdv = kernel(
        total_kernel, "total", [(SLOTS, width)] * 2, [VMEM], (VMEM,) * 2, 4, (130_000, 300_000, 0)
    )(terms)
    return (pdq, pdk, pdv, cdq[None], cdk[None], cdv[None])


def solution(mesh):
    rows = P(("prompt", "sample"), None)
    blocks = P(("prompt", "sample"), None, None)
    in_specs = (rows,) * 4 + (blocks,) * 4 + (P(("prompt", "sample")), P("prompt"))
    out_specs = (rows,) * 3 + (blocks,) * 3
    return jax.shard_map(body, mesh=mesh, in_specs=in_specs, out_specs=out_specs, check_vma=False)
```

```python
import jax
import jax.numpy as jnp
from jax import lax
from jax.experimental import pallas as pl
from jax.experimental.pallas import tpu as pltpu
from jax.sharding import PartitionSpec as P

QUERY_HEADS = 16
KEY_VALUE_HEADS = 4
HEAD_DIM = 128
GROUP = QUERY_HEADS // KEY_VALUE_HEADS
SCALE = HEAD_DIM ** (-0.5)
LOG2E = 1.4426950408889634
CHIPS = 8
CORES = 2
DEVICES = CHIPS * CORES
MASKED = -1e30

HALF_HEADS = KEY_VALUE_HEADS // CORES
HALF_WIDTH = HALF_HEADS * HEAD_DIM
HALF_COLUMNS = HALF_WIDTH * GROUP

SLOTS = 16
ROWS = 128
KEYS = DEVICES * SLOTS

PROMPT_ROW = ROWS
EXTRA_ROW = ROWS + SLOTS
QUERY_BLOCK = EXTRA_ROW + SLOTS
OTHER_BLOCK = EXTRA_ROW + ROWS // 2

ORDER = [
    chip % CHIPS * CORES + core
    for step in range(CHIPS)
    for core in range(CORES)
    for chip in [3 * step + core * (CHIPS // CORES)]
]
PLACE = [ORDER.index(device) for device in range(DEVICES)]

NT = ((1,), (1,))
NN = ((1,), (0,))
VMEM = pl.BlockSpec(memory_space=pltpu.VMEM)
SMEM = pl.BlockSpec(memory_space=pltpu.SMEM)
ANY = pl.BlockSpec(memory_space=pl.ANY)


def dot(a, b, contract):
    return lax.dot_general(a, b, (contract, ((), ())), preferred_element_type=jnp.float32)


def own_core():
    return lax.rem(lax.axis_index("sample"), CORES)


def columns_of(core, width):
    return pl.ds(pl.multiple_of(core * width, HEAD_DIM), width)


def run(copies):
    for copy in copies:
        copy.start()
    for copy in copies:
        copy.wait()


def stage_kernel(k_ref, v_ref, out_ref, kv_ref, sems):
    run(
        [
            pltpu.make_async_copy(source, kv_ref.at[n], sems.at[n])
            for n, source in enumerate((k_ref, v_ref))
        ]
    )
    for core in range(CORES):
        columns = slice(core * HALF_WIDTH, (core + 1) * HALF_WIDTH)
        rows = jnp.concatenate([kv_ref[0, :, columns], kv_ref[1, :, columns]], axis=1)
        for chip in range(CHIPS):
            out_ref[PLACE[chip * CORES + core]] = rows


def packed(ref, n):
    return ref.at[EXTRA_ROW:OTHER_BLOCK, n * HALF_WIDTH : (n + 1) * HALF_WIDTH]


def split_kernel(clen_ref, q_ref, do_ref, pq_ref, pdo_ref, ck_ref, cv_ref, _, *refs):
    core = own_core()
    sems = refs[-1]
    copies = []
    for n, half in enumerate((core, 1 - core)):
        query_block, other_block = refs[2 * n : 2 * n + 2]
        wide, narrow = columns_of(half, HALF_COLUMNS), columns_of(half, HALF_WIDTH)
        pairs = [
            (q_ref.at[:, wide], query_block.at[:ROWS]),
            (pq_ref.at[:, wide], query_block.at[PROMPT_ROW:EXTRA_ROW]),
            (do_ref.at[:, wide], other_block.at[:ROWS]),
            (pdo_ref.at[:, wide], other_block.at[PROMPT_ROW:EXTRA_ROW]),
        ]
        for k, source in enumerate((ck_ref, cv_ref)):
            for part in range(2):
                rows = slice(part * ROWS // 2, (part + 1) * ROWS // 2)
                pairs.append((source.at[rows, narrow], packed(other_block, 2 * k + part)))
        copies += [
            pltpu.make_async_copy(source, place, sems.at[n * len(pairs) + k])
            for k, (source, place) in enumerate(pairs)
        ]
    for copy in copies:
        copy.start()
    length = jnp.full((SLOTS, HALF_COLUMNS), clen_ref[0], jnp.int32).astype(jnp.float32)
    for query_block in refs[0:4:2]:
        query_block[EXTRA_ROW:QUERY_BLOCK] = length.astype(jnp.bfloat16)
    for copy in copies:
        copy.wait()


def head_columns(ref, first_row, count, head):
    parts = [
        ref[
            first_row : first_row + count,
            (head * GROUP + g) * HEAD_DIM : (head * GROUP + g + 1) * HEAD_DIM,
        ]
        for g in range(GROUP)
    ]
    return jnp.concatenate(parts, axis=0)


def own_rows(ref, head, first):
    parts = [
        packed(ref, first + part)[:, head * HEAD_DIM : (head + 1) * HEAD_DIM]
        for part in range(2)
    ]
    return jnp.concatenate(parts, axis=0)


FACTOR = SCALE * LOG2E


def exponentials(scores, peak):
    return jnp.exp2(scores * FACTOR - peak * FACTOR)


def top(scores):
    return jnp.max(scores, axis=0, keepdims=True)


def column_sum(values):
    return jnp.sum(values, axis=0, keepdims=True)


def own_allowed():
    key = lax.broadcasted_iota(jnp.int32, (ROWS, ROWS), 0)
    return key <= lax.broadcasted_iota(jnp.int32, (ROWS, ROWS), 1)


def own_kernel(mine_q, mine_other, got_q, got_other, share_ref):
    allowed = own_allowed()
    for side, (query_block, other_block) in enumerate(
        ((mine_q, mine_other), (got_q, got_other))
    ):
        for head in range(HALF_HEADS):
            q = head_columns(query_block, 0, ROWS, head)
            do = head_columns(other_block, 0, ROWS, head)
            scores = dot(own_rows(other_block, head, 0), q, NT)
            soft_grad = dot(own_rows(other_block, head, 2), do, NT)
            for start in range(0, GROUP * ROWS, ROWS):
                lanes = slice(start, start + ROWS)
                piece = jnp.where(allowed, scores[:, lanes], MASKED)
                peak = top(piece)
                terms = exponentials(piece, peak)
                unit = CORES * head + side
                share_ref[unit, 0:1, lanes] = peak
                share_ref[unit, 1:2, lanes] = column_sum(terms)
                share_ref[unit, 2:3, lanes] = column_sum(terms * soft_grad[:, lanes])


class Attention:
    def __init__(self, plen_ref, mine_q, mine_other, got_q, got_other, kv_ref, share_ref=None):
        self.share_ref = share_ref
        self.sides = (mine_q, mine_other), (got_q, got_other)
        self.kv_ref = kv_ref
        plen = plen_ref[0]
        own = lax.axis_index("sample")
        other = own + 1 - 2 * own_core()
        row_lane = lax.broadcasted_iota(jnp.int32, (1, ROWS), 1)
        self.valid = []
        for ref, _ in self.sides:
            length = ref[EXTRA_ROW:QUERY_BLOCK, :ROWS].astype(jnp.float32)[0:1]
            live = row_lane.astype(jnp.float32) < length
            self.valid.append(jnp.where(live, 1.0, 0.0).astype(jnp.float32))
        self.safe = KEYS - 2 * SLOTS
        self.tail_ok = (
            lax.broadcasted_iota(jnp.int32, (2 * SLOTS, ROWS), 0) + self.safe < plen
        )
        self.own_ok = own_allowed()
        lanes = CORES * GROUP * SLOTS
        lane = lax.broadcasted_iota(jnp.int32, (1, lanes), 1)
        device = jnp.where(lane < GROUP * SLOTS, own, other)
        global_row = device * SLOTS + lax.rem(lane, SLOTS)
        self.prompt_valid = jnp.where(global_row < plen, 1.0, 0.0).astype(jnp.float32)
        self.prompt_ok = lax.broadcasted_iota(jnp.int32, (KEYS, lanes), 0) <= global_row

    def prompt_rows(self, start):
        parts = [
            self.kv_ref[PLACE[device], :, start : start + HEAD_DIM] for device in range(DEVICES)
        ]
        return jnp.concatenate(parts, axis=0)

    def products(self, head, side):
        keys = self.prompt_rows(head * HEAD_DIM)
        values = self.prompt_rows(HALF_WIDTH + head * HEAD_DIM)
        if side < CORES:
            query_block, other_block = self.sides[side]
            if self.share_ref is None:
                keys = jnp.concatenate([keys, own_rows(other_block, head, 0)], axis=0)
                values = jnp.concatenate([values, own_rows(other_block, head, 2)], axis=0)
            q = head_columns(query_block, 0, ROWS, head)
            do = head_columns(other_block, 0, ROWS, head)
        else:
            q, do = (
                jnp.concatenate(
                    [head_columns(ref, PROMPT_ROW, SLOTS, head) for ref in blocks], axis=0
                )
                for blocks in zip(*self.sides)
            )
        return dot(keys, q, NT), dot(values, do, NT), (keys, q, do)

    def weights(self, head, side, scores, soft_grad):
        pieces = []
        for start in range(0, scores.shape[1], ROWS):
            lanes = slice(start, start + ROWS)
            piece, piece_grad = scores[:, lanes], soft_grad[:, lanes]
            if side < CORES:
                parts = [piece[: self.safe], jnp.where(self.tail_ok, piece[self.safe : KEYS], MASKED)]
                if self.share_ref is None:
                    parts.append(jnp.where(self.own_ok, piece[KEYS:], MASKED))
                piece = jnp.concatenate(parts, axis=0)
                valid = self.valid[side]
            else:
                piece = jnp.where(self.prompt_ok, piece, MASKED)
                valid = self.prompt_valid
            peak = top(piece)
            own_total = own_delta = 0.0
            if side < CORES and self.share_ref is not None:
                unit = CORES * head + side
                own_peak, own_total, own_delta = (
                    self.share_ref[unit, n : n + 1, lanes] for n in range(3)
                )
                peak = jnp.maximum(peak, own_peak)
                weight = exponentials(own_peak, peak)
                own_total, own_delta = own_total * weight, own_delta * weight
            terms = exponentials(piece, peak)
            scale = valid / (column_sum(terms) + own_total)
            soft = terms * scale
            soft_b = soft.astype(jnp.bfloat16)
            delta = column_sum(soft_b.astype(jnp.float32) * piece_grad) + own_delta * scale
            pieces.append((soft_b, (soft * (piece_grad - delta)).astype(jnp.bfloat16)))
        return [jnp.concatenate(part, axis=1) for part in zip(*pieces)]

    def units(self):
        todo = [(head, side) for head in range(HALF_HEADS) for side in (0, 1, 2)]
        following = self.products(*todo[0])
        for n, (head, side) in enumerate(todo):
            scores, soft_grad, operands = following
            if n + 1 < len(todo):
                following = self.products(*todo[n + 1])
            yield head, side, operands, *self.weights(head, side, scores, soft_grad)


def attend_kernel(*refs):
    part_ref = refs[-1]
    dk = dv = None
    for head, side, (_, q, do), soft_b, grad_b in Attention(*refs[:7]).units():
        more_dv = dot(soft_b, do, NN)
        more_dk = dot(grad_b, q, NN)
        dv = more_dv if side == 0 else dv + more_dv
        dk = more_dk if side == 0 else dk + more_dk
        if side == CORES:
            for start, grad in ((head, dk * SCALE), (HALF_HEADS + head, dv)):
                grad = grad.astype(jnp.bfloat16)
                for device in range(DEVICES):
                    part_ref[PLACE[device], :, start * HEAD_DIM : (start + 1) * HEAD_DIM] = grad[
                        device * SLOTS : (device + 1) * SLOTS
                    ]


def grads_kernel(*refs):
    outs = refs[-2:]
    half = ROWS // 2
    for head, side, (keys, q, do), soft_b, grad_b in Attention(*refs[:6]).units():
        dq_t = dot(keys.T, grad_b, NN) * SCALE
        if side == CORES:
            dq = dq_t.T.astype(jnp.bfloat16)
            for n, out in enumerate(outs):
                for g in range(GROUP):
                    column = (head * GROUP + g) * HEAD_DIM
                    row = (n * GROUP + g) * SLOTS
                    out[PROMPT_ROW:EXTRA_ROW, column : column + HEAD_DIM] = dq[
                        row : row + SLOTS
                    ]
            continue
        out = outs[side]
        for g in range(GROUP):
            column = (head * GROUP + g) * HEAD_DIM
            block = dq_t[:, g * ROWS : (g + 1) * ROWS]
            out[:ROWS, column : column + HEAD_DIM] = block.T.astype(jnp.bfloat16)
        own_dk = (dot(grad_b[KEYS:], q, NN) * SCALE).astype(jnp.bfloat16)
        own_dv = dot(soft_b[KEYS:], do, NN).astype(jnp.bfloat16)
        for n, grad in enumerate((own_dk, own_dv)):
            for part in range(2):
                column = (2 * n + part) * HALF_WIDTH + head * HEAD_DIM
                out[EXTRA_ROW:OTHER_BLOCK, column : column + HEAD_DIM] = grad[
                    part * half : (part + 1) * half
                ]


def join_kernel(mine_ref, got_ref, pdq_ref, cdq_ref, cdk_ref, cdv_ref, sems):
    core = own_core()
    copies = []
    for n, (source, half) in enumerate(((mine_ref, core), (got_ref, 1 - core))):
        wide, narrow = columns_of(half, HALF_COLUMNS), columns_of(half, HALF_WIDTH)
        pairs = [
            (source.at[:ROWS], cdq_ref.at[:, wide]),
            (source.at[PROMPT_ROW:EXTRA_ROW], pdq_ref.at[:, wide]),
        ]
        for k, target in enumerate((cdk_ref, cdv_ref)):
            for part in range(2):
                rows = slice(part * ROWS // 2, (part + 1) * ROWS // 2)
                pairs.append((packed(source, 2 * k + part), target.at[rows, narrow]))
        copies += [
            pltpu.make_async_copy(place, target, sems.at[n * len(pairs) + k])
            for k, (place, target) in enumerate(pairs)
        ]
    run(copies)


def total_kernel(terms_ref, dk_ref, dv_ref):
    for core in range(CORES):
        total = sum(
            terms_ref[PLACE[chip * CORES + core]].astype(jnp.float32) for chip in range(CHIPS)
        ).astype(jnp.bfloat16)
        columns = slice(core * HALF_WIDTH, (core + 1) * HALF_WIDTH)
        dk_ref[:, columns] = total[:, :HALF_WIDTH]
        dv_ref[:, columns] = total[:, HALF_WIDTH:]


def kernel(body, name, shapes, in_specs, out_specs, limit, cost, scratch=()):
    flops, moved, transcendentals = cost
    return pl.pallas_call(
        body,
        out_shape=tuple(jax.ShapeDtypeStruct(shape, jnp.bfloat16) for shape in shapes),
        in_specs=in_specs,
        out_specs=out_specs,
        scratch_shapes=list(scratch),
        compiler_params=pltpu.CompilerParams(vmem_limit_bytes=limit * 1024 * 1024),
        cost_estimate=pl.CostEstimate(
            flops=flops, bytes_accessed=moved, transcendentals=transcendentals
        ),
        name=name,
    )


def in_hbm(*arrays):
    return [pltpu.with_memory_space_constraint(a, pltpu.HBM) for a in arrays]


def body(
    prompt_q,
    prompt_k,
    prompt_value_rows,
    prompt_dout,
    comp_q,
    completion_keys,
    completion_values,
    comp_dout,
    comp_lengths,
    prompt_length,
):
    block = (DEVICES, SLOTS, 2 * HALF_WIDTH)
    queries = (QUERY_BLOCK, HALF_COLUMNS)
    others = (OTHER_BLOCK, HALF_COLUMNS)
    swap = [(device, device ^ 1) for device in range(DEVICES)]

    def exchange(blocks):
        return lax.all_to_all(
            blocks, "sample", split_axis=0, concat_axis=0, axis_index_groups=[ORDER], tiled=True
        )

    (outgoing,) = kernel(
        stage_kernel,
        "stage",
        [block],
        [ANY] * 2,
        (VMEM,),
        4,
        (0, 300_000, 0),
        [
            pltpu.VMEM((2, SLOTS, KEY_VALUE_HEADS * HEAD_DIM), jnp.bfloat16),
            pltpu.SemaphoreType.DMA((2,)),
        ],
    )(*in_hbm(prompt_k, prompt_value_rows))
    kv = exchange(outgoing)
    mine_q, mine_other, their_q, their_other = kernel(
        split_kernel,
        "split",
        [queries, others] * 2,
        [SMEM] + [ANY] * 7,
        (VMEM,) * 4,
        8,
        (0, 3_000_000, 0),
        [pltpu.SemaphoreType.DMA((16,))],
    )(
        comp_lengths,
        *in_hbm(
            comp_q[0],
            comp_dout[0],
            prompt_q,
            prompt_dout,
            completion_keys[0],
            completion_values[0],
        ),
        outgoing,
    )
    got_q = lax.ppermute(their_q, "sample", swap)
    got_other = lax.ppermute(their_other, "sample", swap)
    scores_in = prompt_length, mine_q, mine_other, got_q, got_other, kv
    share = pl.pallas_call(
        own_kernel,
        out_shape=jax.ShapeDtypeStruct((KEY_VALUE_HEADS, 8, GROUP * ROWS), jnp.float32),
        in_specs=[VMEM] * 4,
        out_specs=VMEM,
        compiler_params=pltpu.CompilerParams(vmem_limit_bytes=16 * 1024 * 1024),
        cost_estimate=pl.CostEstimate(flops=1_000_000, bytes_accessed=300_000, transcendentals=0),
        name="own",
    )(mine_q, mine_other, got_q, got_other)
    cost = (1_000_000_000, 4_000_000, 850_000)
    (partial,) = kernel(
        attend_kernel, "attend", [block], [SMEM] + [VMEM] * 6, (VMEM,), 24, cost
    )(*scores_in, share)
    terms = exchange(partial)
    mine_out, theirs_out = kernel(
        grads_kernel, "grads", [others] * 2, [SMEM] + [VMEM] * 5 + [ANY], (VMEM,) * 2, 24, cost
    )(*scores_in, partial)
    got_out = lax.ppermute(theirs_out, "sample", swap)
    width = KEY_VALUE_HEADS * HEAD_DIM
    shapes = (
        (SLOTS, QUERY_HEADS * HEAD_DIM),
        (ROWS, QUERY_HEADS * HEAD_DIM),
        (ROWS, width),
        (ROWS, width),
    )
    pdq, cdq, cdk, cdv = kernel(
        join_kernel,
        "join",
        shapes,
        [VMEM] * 2,
        (ANY,) * 4,
        4,
        (0, 1_700_000, 0),
        [pltpu.SemaphoreType.DMA((12,))],
    )(mine_out, got_out)
    pdk, pdv = kernel(
        total_kernel, "total", [(SLOTS, width)] * 2, [VMEM], (VMEM,) * 2, 4, (130_000, 300_000, 0)
    )(terms)
    return (pdq, pdk, pdv, cdq[None], cdk[None], cdv[None])


def solution(mesh):
    rows = P(("prompt", "sample"), None)
    blocks = P(("prompt", "sample"), None, None)
    in_specs = (rows,) * 4 + (blocks,) * 4 + (P(("prompt", "sample")), P("prompt"))
    out_specs = (rows,) * 3 + (blocks,) * 3
    return jax.shard_map(body, mesh=mesh, in_specs=in_specs, out_specs=out_specs, check_vma=False)
```

```python
import jax
import jax.numpy as jnp
from jax import lax
from jax.experimental import pallas as pl
from jax.experimental.pallas import tpu as pltpu
from jax.sharding import PartitionSpec as P

QUERY_HEADS = 16
KEY_VALUE_HEADS = 4
HEAD_DIM = 128
GROUP = QUERY_HEADS // KEY_VALUE_HEADS
SCALE = HEAD_DIM ** (-0.5)
LOG2E = 1.4426950408889634
CHIPS = 8
CORES = 2
DEVICES = CHIPS * CORES
MASKED = -1e30

HALF_HEADS = KEY_VALUE_HEADS // CORES
HALF_WIDTH = HALF_HEADS * HEAD_DIM
HALF_COLUMNS = HALF_WIDTH * GROUP

SLOTS = 16
ROWS = 128
KEYS = DEVICES * SLOTS

PROMPT_ROW = ROWS
EXTRA_ROW = ROWS + SLOTS
QUERY_BLOCK = EXTRA_ROW + SLOTS
OTHER_BLOCK = EXTRA_ROW + ROWS // 2

ORDER = [
    chip % CHIPS * CORES + core
    for step in range(CHIPS)
    for core in range(CORES)
    for chip in [3 * step + core * (CHIPS // CORES)]
]
PLACE = [ORDER.index(device) for device in range(DEVICES)]

NT = ((1,), (1,))
NN = ((1,), (0,))
VMEM = pl.BlockSpec(memory_space=pltpu.VMEM)
SMEM = pl.BlockSpec(memory_space=pltpu.SMEM)
ANY = pl.BlockSpec(memory_space=pl.ANY)


def dot(a, b, contract):
    return lax.dot_general(a, b, (contract, ((), ())), preferred_element_type=jnp.float32)


def own_core():
    return lax.rem(lax.axis_index("sample"), CORES)


def columns_of(core, width):
    return pl.ds(pl.multiple_of(core * width, HEAD_DIM), width)


def run(copies):
    for copy in copies:
        copy.start()
    for copy in copies:
        copy.wait()


def stage_kernel(k_ref, v_ref, out_ref, kv_ref, sems):
    run(
        [
            pltpu.make_async_copy(source, kv_ref.at[n], sems.at[n])
            for n, source in enumerate((k_ref, v_ref))
        ]
    )
    for core in range(CORES):
        columns = slice(core * HALF_WIDTH, (core + 1) * HALF_WIDTH)
        rows = jnp.concatenate([kv_ref[0, :, columns], kv_ref[1, :, columns]], axis=1)
        for chip in range(CHIPS):
            out_ref[PLACE[chip * CORES + core]] = rows


def packed(ref, n):
    return ref.at[EXTRA_ROW:OTHER_BLOCK, n * HALF_WIDTH : (n + 1) * HALF_WIDTH]


def split_kernel(clen_ref, q_ref, do_ref, pq_ref, pdo_ref, ck_ref, cv_ref, _, *refs):
    core = own_core()
    sems = refs[-1]
    copies = []
    for n, half in enumerate((core, 1 - core)):
        query_block, other_block = refs[2 * n : 2 * n + 2]
        wide, narrow = columns_of(half, HALF_COLUMNS), columns_of(half, HALF_WIDTH)
        pairs = [
            (q_ref.at[:, wide], query_block.at[:ROWS]),
            (pq_ref.at[:, wide], query_block.at[PROMPT_ROW:EXTRA_ROW]),
            (do_ref.at[:, wide], other_block.at[:ROWS]),
            (pdo_ref.at[:, wide], other_block.at[PROMPT_ROW:EXTRA_ROW]),
        ]
        for k, source in enumerate((ck_ref, cv_ref)):
            for part in range(2):
                rows = slice(part * ROWS // 2, (part + 1) * ROWS // 2)
                pairs.append((source.at[rows, narrow], packed(other_block, 2 * k + part)))
        copies += [
            pltpu.make_async_copy(source, place, sems.at[n * len(pairs) + k])
            for k, (source, place) in enumerate(pairs)
        ]
    for copy in copies:
        copy.start()
    length = jnp.full((SLOTS, HALF_COLUMNS), clen_ref[0], jnp.int32).astype(jnp.float32)
    for query_block in refs[0:4:2]:
        query_block[EXTRA_ROW:QUERY_BLOCK] = length.astype(jnp.bfloat16)
    for copy in copies:
        copy.wait()


def head_columns(ref, first_row, count, head):
    parts = [
        ref[
            first_row : first_row + count,
            (head * GROUP + g) * HEAD_DIM : (head * GROUP + g + 1) * HEAD_DIM,
        ]
        for g in range(GROUP)
    ]
    return jnp.concatenate(parts, axis=0)


def own_rows(ref, head, first):
    parts = [
        packed(ref, first + part)[:, head * HEAD_DIM : (head + 1) * HEAD_DIM]
        for part in range(2)
    ]
    return jnp.concatenate(parts, axis=0)


FACTOR = SCALE * LOG2E


def exponentials(scores, peak):
    return jnp.exp2(scores * FACTOR - peak * FACTOR)


def top(scores):
    return jnp.max(scores, axis=0, keepdims=True)


def column_sum(values):
    return jnp.sum(values, axis=0, keepdims=True)


def own_allowed():
    key = lax.broadcasted_iota(jnp.int32, (ROWS, ROWS), 0)
    return key <= lax.broadcasted_iota(jnp.int32, (ROWS, ROWS), 1)


def own_kernel(query_block, other_block, share_ref):
    allowed = own_allowed()
    for head in range(HALF_HEADS):
        q = head_columns(query_block, 0, ROWS, head)
        do = head_columns(other_block, 0, ROWS, head)
        scores = dot(own_rows(other_block, head, 0), q, NT)
        soft_grad = dot(own_rows(other_block, head, 2), do, NT)
        for start in range(0, GROUP * ROWS, ROWS):
            lanes = slice(start, start + ROWS)
            piece = jnp.where(allowed, scores[:, lanes], MASKED)
            peak = top(piece)
            terms = exponentials(piece, peak)
            share_ref[head, 0:1, lanes] = peak
            share_ref[head, 1:2, lanes] = column_sum(terms)
            share_ref[head, 2:3, lanes] = column_sum(terms * soft_grad[:, lanes])


class Attention:
    def __init__(self, plen_ref, mine_q, mine_other, got_q, got_other, kv_ref, *shares):
        self.shares = shares
        self.sides = (mine_q, mine_other), (got_q, got_other)
        self.kv_ref = kv_ref
        plen = plen_ref[0]
        own = lax.axis_index("sample")
        other = own + 1 - 2 * own_core()
        row_lane = lax.broadcasted_iota(jnp.int32, (1, ROWS), 1)
        self.valid = []
        for ref, _ in self.sides:
            length = ref[EXTRA_ROW:QUERY_BLOCK, :ROWS].astype(jnp.float32)[0:1]
            live = row_lane.astype(jnp.float32) < length
            self.valid.append(jnp.where(live, 1.0, 0.0).astype(jnp.float32))
        self.safe = KEYS - 2 * SLOTS
        self.tail_ok = (
            lax.broadcasted_iota(jnp.int32, (2 * SLOTS, ROWS), 0) + self.safe < plen
        )
        self.own_ok = own_allowed()
        lanes = CORES * GROUP * SLOTS
        lane = lax.broadcasted_iota(jnp.int32, (1, lanes), 1)
        device = jnp.where(lane < GROUP * SLOTS, own, other)
        global_row = device * SLOTS + lax.rem(lane, SLOTS)
        self.prompt_valid = jnp.where(global_row < plen, 1.0, 0.0).astype(jnp.float32)
        self.prompt_ok = lax.broadcasted_iota(jnp.int32, (KEYS, lanes), 0) <= global_row

    def prompt_rows(self, start):
        parts = [
            self.kv_ref[PLACE[device], :, start : start + HEAD_DIM] for device in range(DEVICES)
        ]
        return jnp.concatenate(parts, axis=0)

    def products(self, head, side):
        keys = self.prompt_rows(head * HEAD_DIM)
        values = self.prompt_rows(HALF_WIDTH + head * HEAD_DIM)
        if side < CORES:
            query_block, other_block = self.sides[side]
            if not self.shares:
                keys = jnp.concatenate([keys, own_rows(other_block, head, 0)], axis=0)
                values = jnp.concatenate([values, own_rows(other_block, head, 2)], axis=0)
            q = head_columns(query_block, 0, ROWS, head)
            do = head_columns(other_block, 0, ROWS, head)
        else:
            q, do = (
                jnp.concatenate(
                    [head_columns(ref, PROMPT_ROW, SLOTS, head) for ref in blocks], axis=0
                )
                for blocks in zip(*self.sides)
            )
        return dot(keys, q, NT), dot(values, do, NT), (keys, q, do)

    def weights(self, head, side, scores, soft_grad):
        pieces = []
        for start in range(0, scores.shape[1], ROWS):
            lanes = slice(start, start + ROWS)
            piece, piece_grad = scores[:, lanes], soft_grad[:, lanes]
            if side < CORES:
                parts = [piece[: self.safe], jnp.where(self.tail_ok, piece[self.safe : KEYS], MASKED)]
                if not self.shares:
                    parts.append(jnp.where(self.own_ok, piece[KEYS:], MASKED))
                piece = jnp.concatenate(parts, axis=0)
                valid = self.valid[side]
            else:
                piece = jnp.where(self.prompt_ok, piece, MASKED)
                valid = self.prompt_valid
            peak = top(piece)
            own_total = own_delta = 0.0
            if side < CORES and self.shares:
                own_peak, own_total, own_delta = (
                    self.shares[side][head, n : n + 1, lanes] for n in range(3)
                )
                peak = jnp.maximum(peak, own_peak)
                weight = exponentials(own_peak, peak)
                own_total, own_delta = own_total * weight, own_delta * weight
            terms = exponentials(piece, peak)
            scale = valid / (column_sum(terms) + own_total)
            soft = terms * scale
            soft_b = soft.astype(jnp.bfloat16)
            delta = column_sum(soft_b.astype(jnp.float32) * piece_grad) + own_delta * scale
            pieces.append((soft_b, (soft * (piece_grad - delta)).astype(jnp.bfloat16)))
        return [jnp.concatenate(part, axis=1) for part in zip(*pieces)]

    def units(self):
        todo = [(head, side) for head in range(HALF_HEADS) for side in (0, 1, 2)]
        following = self.products(*todo[0])
        for n, (head, side) in enumerate(todo):
            scores, soft_grad, operands = following
            if n + 1 < len(todo):
                following = self.products(*todo[n + 1])
            yield head, side, operands, *self.weights(head, side, scores, soft_grad)


def attend_kernel(*refs):
    part_ref = refs[-1]
    dk = dv = None
    for head, side, (_, q, do), soft_b, grad_b in Attention(*refs[:8]).units():
        more_dv = dot(soft_b, do, NN)
        more_dk = dot(grad_b, q, NN)
        dv = more_dv if side == 0 else dv + more_dv
        dk = more_dk if side == 0 else dk + more_dk
        if side == CORES:
            for start, grad in ((head, dk * SCALE), (HALF_HEADS + head, dv)):
                grad = grad.astype(jnp.bfloat16)
                for device in range(DEVICES):
                    part_ref[PLACE[device], :, start * HEAD_DIM : (start + 1) * HEAD_DIM] = grad[
                        device * SLOTS : (device + 1) * SLOTS
                    ]


def grads_kernel(*refs):
    outs = refs[-2:]
    half = ROWS // 2
    for head, side, (keys, q, do), soft_b, grad_b in Attention(*refs[:6]).units():
        dq_t = dot(keys.T, grad_b, NN) * SCALE
        if side == CORES:
            dq = dq_t.T.astype(jnp.bfloat16)
            for n, out in enumerate(outs):
                for g in range(GROUP):
                    column = (head * GROUP + g) * HEAD_DIM
                    row = (n * GROUP + g) * SLOTS
                    out[PROMPT_ROW:EXTRA_ROW, column : column + HEAD_DIM] = dq[
                        row : row + SLOTS
                    ]
            continue
        out = outs[side]
        for g in range(GROUP):
            column = (head * GROUP + g) * HEAD_DIM
            block = dq_t[:, g * ROWS : (g + 1) * ROWS]
            out[:ROWS, column : column + HEAD_DIM] = block.T.astype(jnp.bfloat16)
        own_dk = (dot(grad_b[KEYS:], q, NN) * SCALE).astype(jnp.bfloat16)
        own_dv = dot(soft_b[KEYS:], do, NN).astype(jnp.bfloat16)
        for n, grad in enumerate((own_dk, own_dv)):
            for part in range(2):
                column = (2 * n + part) * HALF_WIDTH + head * HEAD_DIM
                out[EXTRA_ROW:OTHER_BLOCK, column : column + HEAD_DIM] = grad[
                    part * half : (part + 1) * half
                ]


def join_kernel(mine_ref, got_ref, pdq_ref, cdq_ref, cdk_ref, cdv_ref, sems):
    core = own_core()
    copies = []
    for n, (source, half) in enumerate(((mine_ref, core), (got_ref, 1 - core))):
        wide, narrow = columns_of(half, HALF_COLUMNS), columns_of(half, HALF_WIDTH)
        pairs = [
            (source.at[:ROWS], cdq_ref.at[:, wide]),
            (source.at[PROMPT_ROW:EXTRA_ROW], pdq_ref.at[:, wide]),
        ]
        for k, target in enumerate((cdk_ref, cdv_ref)):
            for part in range(2):
                rows = slice(part * ROWS // 2, (part + 1) * ROWS // 2)
                pairs.append((packed(source, 2 * k + part), target.at[rows, narrow]))
        copies += [
            pltpu.make_async_copy(place, target, sems.at[n * len(pairs) + k])
            for k, (place, target) in enumerate(pairs)
        ]
    run(copies)


def total_kernel(terms_ref, dk_ref, dv_ref):
    for core in range(CORES):
        total = sum(
            terms_ref[PLACE[chip * CORES + core]].astype(jnp.float32) for chip in range(CHIPS)
        ).astype(jnp.bfloat16)
        columns = slice(core * HALF_WIDTH, (core + 1) * HALF_WIDTH)
        dk_ref[:, columns] = total[:, :HALF_WIDTH]
        dv_ref[:, columns] = total[:, HALF_WIDTH:]


def kernel(body, name, shapes, in_specs, out_specs, limit, cost, scratch=()):
    flops, moved, transcendentals = cost
    return pl.pallas_call(
        body,
        out_shape=tuple(jax.ShapeDtypeStruct(shape, jnp.bfloat16) for shape in shapes),
        in_specs=in_specs,
        out_specs=out_specs,
        scratch_shapes=list(scratch),
        compiler_params=pltpu.CompilerParams(vmem_limit_bytes=limit * 1024 * 1024),
        cost_estimate=pl.CostEstimate(
            flops=flops, bytes_accessed=moved, transcendentals=transcendentals
        ),
        name=name,
    )


def in_hbm(*arrays):
    return [pltpu.with_memory_space_constraint(a, pltpu.HBM) for a in arrays]


def body(
    prompt_q,
    prompt_k,
    prompt_value_rows,
    prompt_dout,
    comp_q,
    completion_keys,
    completion_values,
    comp_dout,
    comp_lengths,
    prompt_length,
):
    block = (DEVICES, SLOTS, 2 * HALF_WIDTH)
    queries = (QUERY_BLOCK, HALF_COLUMNS)
    others = (OTHER_BLOCK, HALF_COLUMNS)
    swap = [(device, device ^ 1) for device in range(DEVICES)]

    def exchange(blocks):
        return lax.all_to_all(
            blocks, "sample", split_axis=0, concat_axis=0, axis_index_groups=[ORDER], tiled=True
        )

    (outgoing,) = kernel(
        stage_kernel,
        "stage",
        [block],
        [ANY] * 2,
        (VMEM,),
        4,
        (0, 300_000, 0),
        [
            pltpu.VMEM((2, SLOTS, KEY_VALUE_HEADS * HEAD_DIM), jnp.bfloat16),
            pltpu.SemaphoreType.DMA((2,)),
        ],
    )(*in_hbm(prompt_k, prompt_value_rows))
    kv = exchange(outgoing)
    mine_q, mine_other, their_q, their_other = kernel(
        split_kernel,
        "split",
        [queries, others] * 2,
        [SMEM] + [ANY] * 7,
        (VMEM,) * 4,
        8,
        (0, 3_000_000, 0),
        [pltpu.SemaphoreType.DMA((16,))],
    )(
        comp_lengths,
        *in_hbm(
            comp_q[0],
            comp_dout[0],
            prompt_q,
            prompt_dout,
            completion_keys[0],
            completion_values[0],
        ),
        outgoing,
    )
    got_q = lax.ppermute(their_q, "sample", swap)
    got_other = lax.ppermute(their_other, "sample", swap)
    scores_in = prompt_length, mine_q, mine_other, got_q, got_other, kv
    shares = [
        pl.pallas_call(
            own_kernel,
            out_shape=jax.ShapeDtypeStruct((HALF_HEADS, 8, GROUP * ROWS), jnp.float32),
            in_specs=[VMEM] * 2,
            out_specs=VMEM,
            compiler_params=pltpu.CompilerParams(vmem_limit_bytes=16 * 1024 * 1024),
            cost_estimate=pl.CostEstimate(
                flops=1_000_000, bytes_accessed=300_000, transcendentals=0
            ),
            name="own",
        )(*blocks)
        for blocks in ((mine_q, mine_other), (got_q, got_other))
    ]
    cost = (1_000_000_000, 4_000_000, 850_000)
    (partial,) = kernel(
        attend_kernel, "attend", [block], [SMEM] + [VMEM] * 7, (VMEM,), 24, cost
    )(*scores_in, *shares)
    terms = exchange(partial)
    mine_out, theirs_out = kernel(
        grads_kernel, "grads", [others] * 2, [SMEM] + [VMEM] * 5 + [ANY], (VMEM,) * 2, 24, cost
    )(*scores_in, partial)
    got_out = lax.ppermute(theirs_out, "sample", swap)
    width = KEY_VALUE_HEADS * HEAD_DIM
    shapes = (
        (SLOTS, QUERY_HEADS * HEAD_DIM),
        (ROWS, QUERY_HEADS * HEAD_DIM),
        (ROWS, width),
        (ROWS, width),
    )
    pdq, cdq, cdk, cdv = kernel(
        join_kernel,
        "join",
        shapes,
        [VMEM] * 2,
        (ANY,) * 4,
        4,
        (0, 1_700_000, 0),
        [pltpu.SemaphoreType.DMA((12,))],
    )(mine_out, got_out)
    pdk, pdv = kernel(
        total_kernel, "total", [(SLOTS, width)] * 2, [VMEM], (VMEM,) * 2, 4, (130_000, 300_000, 0)
    )(terms)
    return (pdq, pdk, pdv, cdq[None], cdk[None], cdv[None])


def solution(mesh):
    rows = P(("prompt", "sample"), None)
    blocks = P(("prompt", "sample"), None, None)
    in_specs = (rows,) * 4 + (blocks,) * 4 + (P(("prompt", "sample")), P("prompt"))
    out_specs = (rows,) * 3 + (blocks,) * 3
    return jax.shard_map(body, mesh=mesh, in_specs=in_specs, out_specs=out_specs, check_vma=False)
```

```python
import jax
import jax.numpy as jnp
from jax import lax
from jax.experimental import pallas as pl
from jax.experimental.pallas import tpu as pltpu
from jax.sharding import PartitionSpec as P

QUERY_HEADS = 16
KEY_VALUE_HEADS = 4
HEAD_DIM = 128
GROUP = QUERY_HEADS // KEY_VALUE_HEADS
SCALE = HEAD_DIM ** (-0.5)
LOG2E = 1.4426950408889634
CHIPS = 8
CORES = 2
DEVICES = CHIPS * CORES
MASKED = -1e30

HALF_HEADS = KEY_VALUE_HEADS // CORES
HALF_WIDTH = HALF_HEADS * HEAD_DIM
HALF_COLUMNS = HALF_WIDTH * GROUP

SLOTS = 16
ROWS = 128
KEYS = DEVICES * SLOTS

PROMPT_ROW = ROWS
EXTRA_ROW = ROWS + SLOTS
QUERY_BLOCK = EXTRA_ROW + SLOTS
OTHER_BLOCK = EXTRA_ROW + ROWS // 2

ORDER = [
    chip % CHIPS * CORES + core
    for step in range(CHIPS)
    for core in range(CORES)
    for chip in [5 * step + core * (CHIPS // CORES)]
]
PLACE = [ORDER.index(device) for device in range(DEVICES)]

NT = ((1,), (1,))
NN = ((1,), (0,))
VMEM = pl.BlockSpec(memory_space=pltpu.VMEM)
SMEM = pl.BlockSpec(memory_space=pltpu.SMEM)
ANY = pl.BlockSpec(memory_space=pl.ANY)


def dot(a, b, contract):
    return lax.dot_general(a, b, (contract, ((), ())), preferred_element_type=jnp.float32)


def own_core():
    return lax.rem(lax.axis_index("sample"), CORES)


def columns_of(core, width):
    return pl.ds(pl.multiple_of(core * width, HEAD_DIM), width)


def run(copies):
    for copy in copies:
        copy.start()
    for copy in copies:
        copy.wait()


def stage_kernel(k_ref, v_ref, out_ref, kv_ref, sems):
    run(
        [
            pltpu.make_async_copy(source, kv_ref.at[n], sems.at[n])
            for n, source in enumerate((k_ref, v_ref))
        ]
    )
    for core in range(CORES):
        columns = slice(core * HALF_WIDTH, (core + 1) * HALF_WIDTH)
        rows = jnp.concatenate([kv_ref[0, :, columns], kv_ref[1, :, columns]], axis=1)
        for chip in range(CHIPS):
            out_ref[PLACE[chip * CORES + core]] = rows


def packed(ref, n):
    return ref.at[EXTRA_ROW:OTHER_BLOCK, n * HALF_WIDTH : (n + 1) * HALF_WIDTH]


def split_kernel(clen_ref, q_ref, do_ref, pq_ref, pdo_ref, ck_ref, cv_ref, _, *refs):
    core = own_core()
    sems = refs[-1]
    copies = []
    for n, half in enumerate((core, 1 - core)):
        query_block, other_block = refs[2 * n : 2 * n + 2]
        wide, narrow = columns_of(half, HALF_COLUMNS), columns_of(half, HALF_WIDTH)
        pairs = [
            (q_ref.at[:, wide], query_block.at[:ROWS]),
            (pq_ref.at[:, wide], query_block.at[PROMPT_ROW:EXTRA_ROW]),
            (do_ref.at[:, wide], other_block.at[:ROWS]),
            (pdo_ref.at[:, wide], other_block.at[PROMPT_ROW:EXTRA_ROW]),
        ]
        for k, source in enumerate((ck_ref, cv_ref)):
            for part in range(2):
                rows = slice(part * ROWS // 2, (part + 1) * ROWS // 2)
                pairs.append((source.at[rows, narrow], packed(other_block, 2 * k + part)))
        copies += [
            pltpu.make_async_copy(source, place, sems.at[n * len(pairs) + k])
            for k, (source, place) in enumerate(pairs)
        ]
    for copy in copies:
        copy.start()
    length = jnp.full((SLOTS, HALF_COLUMNS), clen_ref[0], jnp.int32).astype(jnp.float32)
    for query_block in refs[0:4:2]:
        query_block[EXTRA_ROW:QUERY_BLOCK] = length.astype(jnp.bfloat16)
    for copy in copies:
        copy.wait()


def head_columns(ref, first_row, count, head):
    parts = [
        ref[
            first_row : first_row + count,
            (head * GROUP + g) * HEAD_DIM : (head * GROUP + g + 1) * HEAD_DIM,
        ]
        for g in range(GROUP)
    ]
    return jnp.concatenate(parts, axis=0)


def own_rows(ref, head, first):
    parts = [
        packed(ref, first + part)[:, head * HEAD_DIM : (head + 1) * HEAD_DIM]
        for part in range(2)
    ]
    return jnp.concatenate(parts, axis=0)


FACTOR = SCALE * LOG2E


def exponentials(scores, peak):
    return jnp.exp2(scores * FACTOR - peak * FACTOR)


def top(scores):
    return jnp.max(scores, axis=0, keepdims=True)


def column_sum(values):
    return jnp.sum(values, axis=0, keepdims=True)


def own_allowed():
    key = lax.broadcasted_iota(jnp.int32, (ROWS, ROWS), 0)
    return key <= lax.broadcasted_iota(jnp.int32, (ROWS, ROWS), 1)


def own_kernel(query_block, other_block, share_ref):
    allowed = own_allowed()
    for head in range(HALF_HEADS):
        q = head_columns(query_block, 0, ROWS, head)
        do = head_columns(other_block, 0, ROWS, head)
        scores = dot(own_rows(other_block, head, 0), q, NT)
        soft_grad = dot(own_rows(other_block, head, 2), do, NT)
        for start in range(0, GROUP * ROWS, ROWS):
            lanes = slice(start, start + ROWS)
            piece = jnp.where(allowed, scores[:, lanes], MASKED)
            peak = top(piece)
            terms = exponentials(piece, peak)
            share_ref[head, 0:1, lanes] = peak
            share_ref[head, 1:2, lanes] = column_sum(terms)
            share_ref[head, 2:3, lanes] = column_sum(terms * soft_grad[:, lanes])


class Attention:
    def __init__(self, plen_ref, mine_q, mine_other, got_q, got_other, kv_ref, *shares):
        self.shares = shares
        self.sides = (mine_q, mine_other), (got_q, got_other)
        self.kv_ref = kv_ref
        plen = plen_ref[0]
        own = lax.axis_index("sample")
        other = own + 1 - 2 * own_core()
        row_lane = lax.broadcasted_iota(jnp.int32, (1, ROWS), 1)
        self.valid = []
        for ref, _ in self.sides:
            length = ref[EXTRA_ROW:QUERY_BLOCK, :ROWS].astype(jnp.float32)[0:1]
            live = row_lane.astype(jnp.float32) < length
            self.valid.append(jnp.where(live, 1.0, 0.0).astype(jnp.float32))
        self.safe = KEYS - 2 * SLOTS
        self.tail_ok = (
            lax.broadcasted_iota(jnp.int32, (2 * SLOTS, ROWS), 0) + self.safe < plen
        )
        self.own_ok = own_allowed()
        lanes = CORES * GROUP * SLOTS
        lane = lax.broadcasted_iota(jnp.int32, (1, lanes), 1)
        device = jnp.where(lane < GROUP * SLOTS, own, other)
        global_row = device * SLOTS + lax.rem(lane, SLOTS)
        self.prompt_valid = jnp.where(global_row < plen, 1.0, 0.0).astype(jnp.float32)
        self.prompt_ok = lax.broadcasted_iota(jnp.int32, (KEYS, lanes), 0) <= global_row

    def prompt_rows(self, start):
        parts = [
            self.kv_ref[PLACE[device], :, start : start + HEAD_DIM] for device in range(DEVICES)
        ]
        return jnp.concatenate(parts, axis=0)

    def products(self, head, side):
        keys = self.prompt_rows(head * HEAD_DIM)
        values = self.prompt_rows(HALF_WIDTH + head * HEAD_DIM)
        if side < CORES:
            query_block, other_block = self.sides[side]
            if not self.shares:
                keys = jnp.concatenate([keys, own_rows(other_block, head, 0)], axis=0)
                values = jnp.concatenate([values, own_rows(other_block, head, 2)], axis=0)
            q = head_columns(query_block, 0, ROWS, head)
            do = head_columns(other_block, 0, ROWS, head)
        else:
            q, do = (
                jnp.concatenate(
                    [head_columns(ref, PROMPT_ROW, SLOTS, head) for ref in blocks], axis=0
                )
                for blocks in zip(*self.sides)
            )
        return dot(keys, q, NT), dot(values, do, NT), (keys, q, do)

    def weights(self, head, side, scores, soft_grad):
        pieces = []
        for start in range(0, scores.shape[1], ROWS):
            lanes = slice(start, start + ROWS)
            piece, piece_grad = scores[:, lanes], soft_grad[:, lanes]
            if side < CORES:
                parts = [piece[: self.safe], jnp.where(self.tail_ok, piece[self.safe : KEYS], MASKED)]
                if not self.shares:
                    parts.append(jnp.where(self.own_ok, piece[KEYS:], MASKED))
                piece = jnp.concatenate(parts, axis=0)
                valid = self.valid[side]
            else:
                piece = jnp.where(self.prompt_ok, piece, MASKED)
                valid = self.prompt_valid
            peak = top(piece)
            own_total = own_delta = 0.0
            if side < CORES and self.shares:
                own_peak, own_total, own_delta = (
                    self.shares[side][head, n : n + 1, lanes] for n in range(3)
                )
                peak = jnp.maximum(peak, own_peak)
                weight = exponentials(own_peak, peak)
                own_total, own_delta = own_total * weight, own_delta * weight
            terms = exponentials(piece, peak)
            scale = valid / (column_sum(terms) + own_total)
            soft = terms * scale
            soft_b = soft.astype(jnp.bfloat16)
            delta = column_sum(soft_b.astype(jnp.float32) * piece_grad) + own_delta * scale
            pieces.append((soft_b, (soft * (piece_grad - delta)).astype(jnp.bfloat16)))
        return [jnp.concatenate(part, axis=1) for part in zip(*pieces)]

    def units(self):
        todo = [(head, side) for head in range(HALF_HEADS) for side in (0, 1, 2)]
        following = self.products(*todo[0])
        for n, (head, side) in enumerate(todo):
            scores, soft_grad, operands = following
            if n + 1 < len(todo):
                following = self.products(*todo[n + 1])
            yield head, side, operands, *self.weights(head, side, scores, soft_grad)


def attend_kernel(*refs):
    part_ref = refs[-1]
    dk = dv = None
    for head, side, (_, q, do), soft_b, grad_b in Attention(*refs[:8]).units():
        more_dv = dot(soft_b, do, NN)
        more_dk = dot(grad_b, q, NN)
        dv = more_dv if side == 0 else dv + more_dv
        dk = more_dk if side == 0 else dk + more_dk
        if side == CORES:
            for start, grad in ((head, dk * SCALE), (HALF_HEADS + head, dv)):
                grad = grad.astype(jnp.bfloat16)
                for device in range(DEVICES):
                    part_ref[PLACE[device], :, start * HEAD_DIM : (start + 1) * HEAD_DIM] = grad[
                        device * SLOTS : (device + 1) * SLOTS
                    ]


def grads_kernel(*refs):
    outs = refs[-2:]
    half = ROWS // 2
    for head, side, (keys, q, do), soft_b, grad_b in Attention(*refs[:6]).units():
        dq_t = dot(keys.T, grad_b, NN) * SCALE
        if side == CORES:
            dq = dq_t.T.astype(jnp.bfloat16)
            for n, out in enumerate(outs):
                for g in range(GROUP):
                    column = (head * GROUP + g) * HEAD_DIM
                    row = (n * GROUP + g) * SLOTS
                    out[PROMPT_ROW:EXTRA_ROW, column : column + HEAD_DIM] = dq[
                        row : row + SLOTS
                    ]
            continue
        out = outs[side]
        for g in range(GROUP):
            column = (head * GROUP + g) * HEAD_DIM
            block = dq_t[:, g * ROWS : (g + 1) * ROWS]
            out[:ROWS, column : column + HEAD_DIM] = block.T.astype(jnp.bfloat16)
        own_dk = (dot(grad_b[KEYS:], q, NN) * SCALE).astype(jnp.bfloat16)
        own_dv = dot(soft_b[KEYS:], do, NN).astype(jnp.bfloat16)
        for n, grad in enumerate((own_dk, own_dv)):
            for part in range(2):
                column = (2 * n + part) * HALF_WIDTH + head * HEAD_DIM
                out[EXTRA_ROW:OTHER_BLOCK, column : column + HEAD_DIM] = grad[
                    part * half : (part + 1) * half
                ]


def join_kernel(mine_ref, got_ref, pdq_ref, cdq_ref, cdk_ref, cdv_ref, sems):
    core = own_core()
    copies = []
    for n, (source, half) in enumerate(((mine_ref, core), (got_ref, 1 - core))):
        wide, narrow = columns_of(half, HALF_COLUMNS), columns_of(half, HALF_WIDTH)
        pairs = [
            (source.at[:ROWS], cdq_ref.at[:, wide]),
            (source.at[PROMPT_ROW:EXTRA_ROW], pdq_ref.at[:, wide]),
        ]
        for k, target in enumerate((cdk_ref, cdv_ref)):
            for part in range(2):
                rows = slice(part * ROWS // 2, (part + 1) * ROWS // 2)
                pairs.append((packed(source, 2 * k + part), target.at[rows, narrow]))
        copies += [
            pltpu.make_async_copy(place, target, sems.at[n * len(pairs) + k])
            for k, (place, target) in enumerate(pairs)
        ]
    run(copies)


def total_kernel(terms_ref, dk_ref, dv_ref):
    for core in range(CORES):
        total = sum(
            terms_ref[PLACE[chip * CORES + core]].astype(jnp.float32) for chip in range(CHIPS)
        ).astype(jnp.bfloat16)
        columns = slice(core * HALF_WIDTH, (core + 1) * HALF_WIDTH)
        dk_ref[:, columns] = total[:, :HALF_WIDTH]
        dv_ref[:, columns] = total[:, HALF_WIDTH:]


def kernel(body, name, shapes, in_specs, out_specs, limit, cost, scratch=()):
    flops, moved, transcendentals = cost
    return pl.pallas_call(
        body,
        out_shape=tuple(jax.ShapeDtypeStruct(shape, jnp.bfloat16) for shape in shapes),
        in_specs=in_specs,
        out_specs=out_specs,
        scratch_shapes=list(scratch),
        compiler_params=pltpu.CompilerParams(vmem_limit_bytes=limit * 1024 * 1024),
        cost_estimate=pl.CostEstimate(
            flops=flops, bytes_accessed=moved, transcendentals=transcendentals
        ),
        name=name,
    )


def in_hbm(*arrays):
    return [pltpu.with_memory_space_constraint(a, pltpu.HBM) for a in arrays]


def body(
    prompt_q,
    prompt_k,
    prompt_value_rows,
    prompt_dout,
    comp_q,
    completion_keys,
    completion_values,
    comp_dout,
    comp_lengths,
    prompt_length,
):
    block = (DEVICES, SLOTS, 2 * HALF_WIDTH)
    queries = (QUERY_BLOCK, HALF_COLUMNS)
    others = (OTHER_BLOCK, HALF_COLUMNS)
    swap = [(device, device ^ 1) for device in range(DEVICES)]

    def exchange(blocks):
        return lax.all_to_all(
            blocks, "sample", split_axis=0, concat_axis=0, axis_index_groups=[ORDER], tiled=True
        )

    (outgoing,) = kernel(
        stage_kernel,
        "stage",
        [block],
        [ANY] * 2,
        (VMEM,),
        4,
        (0, 300_000, 0),
        [
            pltpu.VMEM((2, SLOTS, KEY_VALUE_HEADS * HEAD_DIM), jnp.bfloat16),
            pltpu.SemaphoreType.DMA((2,)),
        ],
    )(*in_hbm(prompt_k, prompt_value_rows))
    kv = exchange(outgoing)
    mine_q, mine_other, their_q, their_other = kernel(
        split_kernel,
        "split",
        [queries, others] * 2,
        [SMEM] + [ANY] * 7,
        (VMEM,) * 4,
        8,
        (0, 3_000_000, 0),
        [pltpu.SemaphoreType.DMA((16,))],
    )(
        comp_lengths,
        *in_hbm(
            comp_q[0],
            comp_dout[0],
            prompt_q,
            prompt_dout,
            completion_keys[0],
            completion_values[0],
        ),
        outgoing,
    )
    got_q = lax.ppermute(their_q, "sample", swap)
    got_other = lax.ppermute(their_other, "sample", swap)
    scores_in = prompt_length, mine_q, mine_other, got_q, got_other, kv
    shares = [
        pl.pallas_call(
            own_kernel,
            out_shape=jax.ShapeDtypeStruct((HALF_HEADS, 8, GROUP * ROWS), jnp.float32),
            in_specs=[VMEM] * 2,
            out_specs=VMEM,
            compiler_params=pltpu.CompilerParams(vmem_limit_bytes=16 * 1024 * 1024),
            cost_estimate=pl.CostEstimate(
                flops=1_000_000, bytes_accessed=300_000, transcendentals=0
            ),
            name="own",
        )(*blocks)
        for blocks in ((mine_q, mine_other), (got_q, got_other))
    ]
    cost = (1_000_000_000, 4_000_000, 850_000)
    (partial,) = kernel(
        attend_kernel, "attend", [block], [SMEM] + [VMEM] * 7, (VMEM,), 24, cost
    )(*scores_in, *shares)
    terms = exchange(partial)
    mine_out, theirs_out = kernel(
        grads_kernel, "grads", [others] * 2, [SMEM] + [VMEM] * 5 + [ANY], (VMEM,) * 2, 24, cost
    )(*scores_in, partial)
    got_out = lax.ppermute(theirs_out, "sample", swap)
    width = KEY_VALUE_HEADS * HEAD_DIM
    shapes = (
        (SLOTS, QUERY_HEADS * HEAD_DIM),
        (ROWS, QUERY_HEADS * HEAD_DIM),
        (ROWS, width),
        (ROWS, width),
    )
    pdq, cdq, cdk, cdv = kernel(
        join_kernel,
        "join",
        shapes,
        [VMEM] * 2,
        (ANY,) * 4,
        4,
        (0, 1_700_000, 0),
        [pltpu.SemaphoreType.DMA((12,))],
    )(mine_out, got_out)
    pdk, pdv = kernel(
        total_kernel, "total", [(SLOTS, width)] * 2, [VMEM], (VMEM,) * 2, 4, (130_000, 300_000, 0)
    )(terms)
    return (pdq, pdk, pdv, cdq[None], cdk[None], cdv[None])


def solution(mesh):
    rows = P(("prompt", "sample"), None)
    blocks = P(("prompt", "sample"), None, None)
    in_specs = (rows,) * 4 + (blocks,) * 4 + (P(("prompt", "sample")), P("prompt"))
    out_specs = (rows,) * 3 + (blocks,) * 3
    return jax.shard_map(body, mesh=mesh, in_specs=in_specs, out_specs=out_specs, check_vma=False)
```

```python
import jax
import jax.numpy as jnp
from jax import lax
from jax.experimental import pallas as pl
from jax.experimental.pallas import tpu as pltpu
from jax.sharding import PartitionSpec as P

QUERY_HEADS = 16
KEY_VALUE_HEADS = 4
HEAD_DIM = 128
GROUP = QUERY_HEADS // KEY_VALUE_HEADS
SCALE = HEAD_DIM ** (-0.5)
LOG2E = 1.4426950408889634
CHIPS = 8
CORES = 2
DEVICES = CHIPS * CORES
MASKED = -1e30

HALF_HEADS = KEY_VALUE_HEADS // CORES
HALF_WIDTH = HALF_HEADS * HEAD_DIM
HALF_COLUMNS = HALF_WIDTH * GROUP

SLOTS = 16
ROWS = 128
KEYS = DEVICES * SLOTS

PROMPT_ROW = ROWS
EXTRA_ROW = ROWS + SLOTS
QUERY_BLOCK = EXTRA_ROW + SLOTS
OTHER_BLOCK = EXTRA_ROW + ROWS // 2

ORDER = [
    chip % CHIPS * CORES + core
    for step in range(CHIPS)
    for core in range(CORES)
    for chip in [3 * step + core * (CHIPS // CORES)]
]
PLACE = [ORDER.index(device) for device in range(DEVICES)]

NT = ((1,), (1,))
NN = ((1,), (0,))
VMEM = pl.BlockSpec(memory_space=pltpu.VMEM)
SMEM = pl.BlockSpec(memory_space=pltpu.SMEM)
ANY = pl.BlockSpec(memory_space=pl.ANY)


def dot(a, b, contract):
    return lax.dot_general(a, b, (contract, ((), ())), preferred_element_type=jnp.float32)


def own_core():
    return lax.rem(lax.axis_index("sample"), CORES)


def columns_of(core, width):
    return pl.ds(pl.multiple_of(core * width, HEAD_DIM), width)


def window(start):
    if not isinstance(start, int):
        start = pl.multiple_of(start, HEAD_DIM)
    return pl.ds(start, HEAD_DIM)


def run(copies):
    for copy in copies:
        copy.start()
    for copy in copies:
        copy.wait()


def stage_kernel(k_ref, v_ref, out_ref, kv_ref, sems):
    run(
        [
            pltpu.make_async_copy(source, kv_ref.at[n], sems.at[n])
            for n, source in enumerate((k_ref, v_ref))
        ]
    )
    for core in range(CORES):
        columns = slice(core * HALF_WIDTH, (core + 1) * HALF_WIDTH)
        rows = jnp.concatenate([kv_ref[0, :, columns], kv_ref[1, :, columns]], axis=1)
        for chip in range(CHIPS):
            out_ref[PLACE[chip * CORES + core]] = rows


def packed(ref, n):
    return ref.at[EXTRA_ROW:OTHER_BLOCK, n * HALF_WIDTH : (n + 1) * HALF_WIDTH]


def split_kernel(clen_ref, q_ref, do_ref, pq_ref, pdo_ref, ck_ref, cv_ref, _, *refs):
    core = own_core()
    sems = refs[-1]
    copies = []
    for n, half in enumerate((core, 1 - core)):
        query_block, other_block = refs[2 * n : 2 * n + 2]
        wide, narrow = columns_of(half, HALF_COLUMNS), columns_of(half, HALF_WIDTH)
        pairs = [
            (q_ref.at[:, wide], query_block.at[:ROWS]),
            (pq_ref.at[:, wide], query_block.at[PROMPT_ROW:EXTRA_ROW]),
            (do_ref.at[:, wide], other_block.at[:ROWS]),
            (pdo_ref.at[:, wide], other_block.at[PROMPT_ROW:EXTRA_ROW]),
        ]
        for k, source in enumerate((ck_ref, cv_ref)):
            for part in range(2):
                rows = slice(part * ROWS // 2, (part + 1) * ROWS // 2)
                pairs.append((source.at[rows, narrow], packed(other_block, 2 * k + part)))
        copies += [
            pltpu.make_async_copy(source, place, sems.at[n * len(pairs) + k])
            for k, (source, place) in enumerate(pairs)
        ]
    for copy in copies:
        copy.start()
    length = jnp.full((SLOTS, HALF_COLUMNS), clen_ref[0], jnp.int32).astype(jnp.float32)
    for query_block in refs[0:4:2]:
        query_block[EXTRA_ROW:QUERY_BLOCK] = length.astype(jnp.bfloat16)
    for copy in copies:
        copy.wait()


def head_columns(ref, first_row, count, head):
    parts = [
        ref[
            first_row : first_row + count,
            window((head * GROUP + g) * HEAD_DIM),
        ]
        for g in range(GROUP)
    ]
    return jnp.concatenate(parts, axis=0)


def own_rows(ref, head, first):
    parts = [
        ref[EXTRA_ROW:OTHER_BLOCK, window((first + part) * HALF_WIDTH + head * HEAD_DIM)]
        for part in range(2)
    ]
    return jnp.concatenate(parts, axis=0)


FACTOR = SCALE * LOG2E


def exponentials(scores, peak):
    return jnp.exp2(scores * FACTOR - peak * FACTOR)


def top(scores):
    return jnp.max(scores, axis=0, keepdims=True)


def column_sum(values):
    return jnp.sum(values, axis=0, keepdims=True)


def own_allowed():
    key = lax.broadcasted_iota(jnp.int32, (ROWS, ROWS), 0)
    return key <= lax.broadcasted_iota(jnp.int32, (ROWS, ROWS), 1)


def own_kernel(query_block, other_block, share_ref):
    allowed = own_allowed()
    for head in range(HALF_HEADS):
        q = head_columns(query_block, 0, ROWS, head)
        do = head_columns(other_block, 0, ROWS, head)
        scores = dot(own_rows(other_block, head, 0), q, NT)
        soft_grad = dot(own_rows(other_block, head, 2), do, NT)
        for start in range(0, GROUP * ROWS, ROWS):
            lanes = slice(start, start + ROWS)
            piece = jnp.where(allowed, scores[:, lanes], MASKED)
            peak = top(piece)
            terms = exponentials(piece, peak)
            share_ref[head, 0:1, lanes] = peak
            share_ref[head, 1:2, lanes] = column_sum(terms)
            share_ref[head, 2:3, lanes] = column_sum(terms * soft_grad[:, lanes])


class Attention:
    def __init__(self, plen_ref, mine_q, mine_other, got_q, got_other, kv_ref, *shares):
        self.shares = shares
        self.sides = (mine_q, mine_other), (got_q, got_other)
        self.kv_ref = kv_ref
        plen = plen_ref[0]
        own = lax.axis_index("sample")
        other = own + 1 - 2 * own_core()
        row_lane = lax.broadcasted_iota(jnp.int32, (1, ROWS), 1)
        self.valid = []
        for ref, _ in self.sides:
            length = ref[EXTRA_ROW:QUERY_BLOCK, :ROWS].astype(jnp.float32)[0:1]
            live = row_lane.astype(jnp.float32) < length
            self.valid.append(jnp.where(live, 1.0, 0.0).astype(jnp.float32))
        self.safe = KEYS - 2 * SLOTS
        self.tail_ok = (
            lax.broadcasted_iota(jnp.int32, (2 * SLOTS, ROWS), 0) + self.safe < plen
        )
        self.own_ok = own_allowed()
        lanes = CORES * GROUP * SLOTS
        lane = lax.broadcasted_iota(jnp.int32, (1, lanes), 1)
        device = jnp.where(lane < GROUP * SLOTS, own, other)
        global_row = device * SLOTS + lax.rem(lane, SLOTS)
        self.prompt_valid = jnp.where(global_row < plen, 1.0, 0.0).astype(jnp.float32)
        self.prompt_ok = lax.broadcasted_iota(jnp.int32, (KEYS, lanes), 0) <= global_row

    def prompt_rows(self, start):
        parts = [
            self.kv_ref[PLACE[device], :, window(start)] for device in range(DEVICES)
        ]
        return jnp.concatenate(parts, axis=0)

    def products(self, head, side):
        keys = self.prompt_rows(head * HEAD_DIM)
        values = self.prompt_rows(HALF_WIDTH + head * HEAD_DIM)
        if side < CORES:
            query_block, other_block = self.sides[side]
            if not self.shares:
                keys = jnp.concatenate([keys, own_rows(other_block, head, 0)], axis=0)
                values = jnp.concatenate([values, own_rows(other_block, head, 2)], axis=0)
            q = head_columns(query_block, 0, ROWS, head)
            do = head_columns(other_block, 0, ROWS, head)
        else:
            q, do = (
                jnp.concatenate(
                    [head_columns(ref, PROMPT_ROW, SLOTS, head) for ref in blocks], axis=0
                )
                for blocks in zip(*self.sides)
            )
        return dot(keys, q, NT), dot(values, do, NT), (keys, q, do)

    def weights(self, head, side, scores, soft_grad):
        pieces = []
        for start in range(0, scores.shape[1], ROWS):
            lanes = slice(start, start + ROWS)
            piece, piece_grad = scores[:, lanes], soft_grad[:, lanes]
            if side < CORES:
                parts = [piece[: self.safe], jnp.where(self.tail_ok, piece[self.safe : KEYS], MASKED)]
                if not self.shares:
                    parts.append(jnp.where(self.own_ok, piece[KEYS:], MASKED))
                piece = jnp.concatenate(parts, axis=0)
                valid = self.valid[side]
            else:
                piece = jnp.where(self.prompt_ok, piece, MASKED)
                valid = self.prompt_valid
            peak = top(piece)
            own_total = own_delta = 0.0
            if side < CORES and self.shares:
                own_peak, own_total, own_delta = (
                    self.shares[side][head, n : n + 1, lanes] for n in range(3)
                )
                peak = jnp.maximum(peak, own_peak)
                weight = exponentials(own_peak, peak)
                own_total, own_delta = own_total * weight, own_delta * weight
            terms = exponentials(piece, peak)
            scale = valid / (column_sum(terms) + own_total)
            soft = terms * scale
            soft_b = soft.astype(jnp.bfloat16)
            delta = column_sum(soft_b.astype(jnp.float32) * piece_grad) + own_delta * scale
            pieces.append((soft_b, (soft * (piece_grad - delta)).astype(jnp.bfloat16)))
        return [jnp.concatenate(part, axis=1) for part in zip(*pieces)]

    def units(self, *heads):
        todo = [(head, side) for head in heads for side in (0, 1, 2)]
        following = self.products(*todo[0])
        for n, (head, side) in enumerate(todo):
            scores, soft_grad, operands = following
            if n + 1 < len(todo):
                following = self.products(*todo[n + 1])
            yield head, side, operands, *self.weights(head, side, scores, soft_grad)


def attend_kernel(*refs):
    part_ref = refs[-1]
    attention = Attention(*refs[:8])

    @pl.loop(0, HALF_HEADS)
    def _(head):
        dk = dv = None
        for _, side, (_, q, do), soft_b, grad_b in attention.units(head):
            more_dv = dot(soft_b, do, NN)
            more_dk = dot(grad_b, q, NN)
            dv = more_dv if side == 0 else dv + more_dv
            dk = more_dk if side == 0 else dk + more_dk
        for start, grad in ((head, dk * SCALE), (HALF_HEADS + head, dv)):
            grad = grad.astype(jnp.bfloat16)
            for device in range(DEVICES):
                part_ref[PLACE[device], :, window(start * HEAD_DIM)] = grad[
                    device * SLOTS : (device + 1) * SLOTS
                ]


def grads_kernel(*refs):
    outs = refs[-2:]
    half = ROWS // 2
    for head, side, (keys, q, do), soft_b, grad_b in Attention(*refs[:6]).units(
        *range(HALF_HEADS)
    ):
        dq_t = dot(keys.T, grad_b, NN) * SCALE
        if side == CORES:
            dq = dq_t.T.astype(jnp.bfloat16)
            for n, out in enumerate(outs):
                for g in range(GROUP):
                    column = (head * GROUP + g) * HEAD_DIM
                    row = (n * GROUP + g) * SLOTS
                    out[PROMPT_ROW:EXTRA_ROW, column : column + HEAD_DIM] = dq[
                        row : row + SLOTS
                    ]
            continue
        out = outs[side]
        for g in range(GROUP):
            column = (head * GROUP + g) * HEAD_DIM
            block = dq_t[:, g * ROWS : (g + 1) * ROWS]
            out[:ROWS, column : column + HEAD_DIM] = block.T.astype(jnp.bfloat16)
        own_dk = (dot(grad_b[KEYS:], q, NN) * SCALE).astype(jnp.bfloat16)
        own_dv = dot(soft_b[KEYS:], do, NN).astype(jnp.bfloat16)
        for n, grad in enumerate((own_dk, own_dv)):
            for part in range(2):
                column = (2 * n + part) * HALF_WIDTH + head * HEAD_DIM
                out[EXTRA_ROW:OTHER_BLOCK, column : column + HEAD_DIM] = grad[
                    part * half : (part + 1) * half
                ]


def join_kernel(mine_ref, got_ref, pdq_ref, cdq_ref, cdk_ref, cdv_ref, sems):
    core = own_core()
    copies = []
    for n, (source, half) in enumerate(((mine_ref, core), (got_ref, 1 - core))):
        wide, narrow = columns_of(half, HALF_COLUMNS), columns_of(half, HALF_WIDTH)
        pairs = [
            (source.at[:ROWS], cdq_ref.at[:, wide]),
            (source.at[PROMPT_ROW:EXTRA_ROW], pdq_ref.at[:, wide]),
        ]
        for k, target in enumerate((cdk_ref, cdv_ref)):
            for part in range(2):
                rows = slice(part * ROWS // 2, (part + 1) * ROWS // 2)
                pairs.append((packed(source, 2 * k + part), target.at[rows, narrow]))
        copies += [
            pltpu.make_async_copy(place, target, sems.at[n * len(pairs) + k])
            for k, (place, target) in enumerate(pairs)
        ]
    run(copies)


def total_kernel(terms_ref, dk_ref, dv_ref):
    for core in range(CORES):
        total = sum(
            terms_ref[PLACE[chip * CORES + core]].astype(jnp.float32) for chip in range(CHIPS)
        ).astype(jnp.bfloat16)
        columns = slice(core * HALF_WIDTH, (core + 1) * HALF_WIDTH)
        dk_ref[:, columns] = total[:, :HALF_WIDTH]
        dv_ref[:, columns] = total[:, HALF_WIDTH:]


def kernel(body, name, shapes, in_specs, out_specs, limit, cost, scratch=()):
    flops, moved, transcendentals = cost
    return pl.pallas_call(
        body,
        out_shape=tuple(jax.ShapeDtypeStruct(shape, jnp.bfloat16) for shape in shapes),
        in_specs=in_specs,
        out_specs=out_specs,
        scratch_shapes=list(scratch),
        compiler_params=pltpu.CompilerParams(vmem_limit_bytes=limit * 1024 * 1024),
        cost_estimate=pl.CostEstimate(
            flops=flops, bytes_accessed=moved, transcendentals=transcendentals
        ),
        name=name,
    )


def in_hbm(*arrays):
    return [pltpu.with_memory_space_constraint(a, pltpu.HBM) for a in arrays]


def body(
    prompt_q,
    prompt_k,
    prompt_value_rows,
    prompt_dout,
    comp_q,
    completion_keys,
    completion_values,
    comp_dout,
    comp_lengths,
    prompt_length,
):
    block = (DEVICES, SLOTS, 2 * HALF_WIDTH)
    queries = (QUERY_BLOCK, HALF_COLUMNS)
    others = (OTHER_BLOCK, HALF_COLUMNS)
    swap = [(device, device ^ 1) for device in range(DEVICES)]

    def exchange(blocks):
        return lax.all_to_all(
            blocks, "sample", split_axis=0, concat_axis=0, axis_index_groups=[ORDER], tiled=True
        )

    (outgoing,) = kernel(
        stage_kernel,
        "stage",
        [block],
        [ANY] * 2,
        (VMEM,),
        4,
        (0, 300_000, 0),
        [
            pltpu.VMEM((2, SLOTS, KEY_VALUE_HEADS * HEAD_DIM), jnp.bfloat16),
            pltpu.SemaphoreType.DMA((2,)),
        ],
    )(*in_hbm(prompt_k, prompt_value_rows))
    kv = exchange(outgoing)
    mine_q, mine_other, their_q, their_other = kernel(
        split_kernel,
        "split",
        [queries, others] * 2,
        [SMEM] + [ANY] * 7,
        (VMEM,) * 4,
        8,
        (0, 3_000_000, 0),
        [pltpu.SemaphoreType.DMA((16,))],
    )(
        comp_lengths,
        *in_hbm(
            comp_q[0],
            comp_dout[0],
            prompt_q,
            prompt_dout,
            completion_keys[0],
            completion_values[0],
        ),
        outgoing,
    )
    got_q = lax.ppermute(their_q, "sample", swap)
    got_other = lax.ppermute(their_other, "sample", swap)
    scores_in = prompt_length, mine_q, mine_other, got_q, got_other, kv
    shares = [
        pl.pallas_call(
            own_kernel,
            out_shape=jax.ShapeDtypeStruct((HALF_HEADS, 8, GROUP * ROWS), jnp.float32),
            in_specs=[VMEM] * 2,
            out_specs=VMEM,
            compiler_params=pltpu.CompilerParams(vmem_limit_bytes=16 * 1024 * 1024),
            cost_estimate=pl.CostEstimate(
                flops=1_000_000, bytes_accessed=300_000, transcendentals=0
            ),
            name="own",
        )(*blocks)
        for blocks in ((mine_q, mine_other), (got_q, got_other))
    ]
    cost = (1_000_000_000, 4_000_000, 850_000)
    (partial,) = kernel(
        attend_kernel, "attend", [block], [SMEM] + [VMEM] * 7, (VMEM,), 24, cost
    )(*scores_in, *shares)
    terms = exchange(partial)
    mine_out, theirs_out = kernel(
        grads_kernel, "grads", [others] * 2, [SMEM] + [VMEM] * 5 + [ANY], (VMEM,) * 2, 24, cost
    )(*scores_in, partial)
    got_out = lax.ppermute(theirs_out, "sample", swap)
    width = KEY_VALUE_HEADS * HEAD_DIM
    shapes = (
        (SLOTS, QUERY_HEADS * HEAD_DIM),
        (ROWS, QUERY_HEADS * HEAD_DIM),
        (ROWS, width),
        (ROWS, width),
    )
    pdq, cdq, cdk, cdv = kernel(
        join_kernel,
        "join",
        shapes,
        [VMEM] * 2,
        (ANY,) * 4,
        4,
        (0, 1_700_000, 0),
        [pltpu.SemaphoreType.DMA((12,))],
    )(mine_out, got_out)
    pdk, pdv = kernel(
        total_kernel, "total", [(SLOTS, width)] * 2, [VMEM], (VMEM,) * 2, 4, (130_000, 300_000, 0)
    )(terms)
    return (pdq, pdk, pdv, cdq[None], cdk[None], cdv[None])


def solution(mesh):
    rows = P(("prompt", "sample"), None)
    blocks = P(("prompt", "sample"), None, None)
    in_specs = (rows,) * 4 + (blocks,) * 4 + (P(("prompt", "sample")), P("prompt"))
    out_specs = (rows,) * 3 + (blocks,) * 3
    return jax.shard_map(body, mesh=mesh, in_specs=in_specs, out_specs=out_specs, check_vma=False)
```

```python
import jax
import jax.numpy as jnp
from jax import lax
from jax.experimental import pallas as pl
from jax.experimental.pallas import tpu as pltpu
from jax.sharding import PartitionSpec as P

QUERY_HEADS = 16
KEY_VALUE_HEADS = 4
HEAD_DIM = 128
GROUP = QUERY_HEADS // KEY_VALUE_HEADS
SCALE = HEAD_DIM ** (-0.5)
LOG2E = 1.4426950408889634
CHIPS = 8
CORES = 2
DEVICES = CHIPS * CORES
MASKED = -1e30

HALF_HEADS = KEY_VALUE_HEADS // CORES
HALF_WIDTH = HALF_HEADS * HEAD_DIM
HALF_COLUMNS = HALF_WIDTH * GROUP

SLOTS = 16
ROWS = 128
KEYS = DEVICES * SLOTS

PROMPT_ROW = ROWS
EXTRA_ROW = ROWS + SLOTS
QUERY_BLOCK = EXTRA_ROW + SLOTS
OTHER_BLOCK = EXTRA_ROW + ROWS // 2

ORDER = [
    chip % CHIPS * CORES + core
    for step in range(CHIPS)
    for core in range(CORES)
    for chip in [3 * step + core * (CHIPS // CORES)]
]
PLACE = [ORDER.index(device) for device in range(DEVICES)]

NT = ((1,), (1,))
NN = ((1,), (0,))
VMEM = pl.BlockSpec(memory_space=pltpu.VMEM)
SMEM = pl.BlockSpec(memory_space=pltpu.SMEM)
ANY = pl.BlockSpec(memory_space=pl.ANY)


def dot(a, b, contract):
    return lax.dot_general(a, b, (contract, ((), ())), preferred_element_type=jnp.float32)


def own_core():
    return lax.rem(lax.axis_index("sample"), CORES)


def columns_of(core, width):
    return pl.ds(pl.multiple_of(core * width, HEAD_DIM), width)


def run(copies):
    for copy in copies:
        copy.start()
    for copy in copies:
        copy.wait()


def stage_kernel(k_ref, v_ref, out_ref, kv_ref, sems):
    run(
        [
            pltpu.make_async_copy(source, kv_ref.at[n], sems.at[n])
            for n, source in enumerate((k_ref, v_ref))
        ]
    )
    for core in range(CORES):
        columns = slice(core * HALF_WIDTH, (core + 1) * HALF_WIDTH)
        rows = jnp.concatenate([kv_ref[0, :, columns], kv_ref[1, :, columns]], axis=1)
        for chip in range(CHIPS):
            out_ref[PLACE[chip * CORES + core]] = rows


def packed(ref, n):
    return ref.at[EXTRA_ROW:OTHER_BLOCK, n * HALF_WIDTH : (n + 1) * HALF_WIDTH]


def split_kernel(clen_ref, q_ref, do_ref, pq_ref, pdo_ref, ck_ref, cv_ref, _, *refs):
    core = own_core()
    sems = refs[-1]
    copies = []
    for n, half in enumerate((core, 1 - core)):
        query_block, other_block = refs[2 * n : 2 * n + 2]
        wide, narrow = columns_of(half, HALF_COLUMNS), columns_of(half, HALF_WIDTH)
        pairs = [
            (q_ref.at[:, wide], query_block.at[:ROWS]),
            (pq_ref.at[:, wide], query_block.at[PROMPT_ROW:EXTRA_ROW]),
            (do_ref.at[:, wide], other_block.at[:ROWS]),
            (pdo_ref.at[:, wide], other_block.at[PROMPT_ROW:EXTRA_ROW]),
        ]
        for k, source in enumerate((ck_ref, cv_ref)):
            for part in range(2):
                rows = slice(part * ROWS // 2, (part + 1) * ROWS // 2)
                pairs.append((source.at[rows, narrow], packed(other_block, 2 * k + part)))
        copies += [
            pltpu.make_async_copy(source, place, sems.at[n * len(pairs) + k])
            for k, (source, place) in enumerate(pairs)
        ]
    for copy in copies:
        copy.start()
    length = jnp.full((SLOTS, HALF_COLUMNS), clen_ref[0], jnp.int32).astype(jnp.float32)
    for query_block in refs[0:4:2]:
        query_block[EXTRA_ROW:QUERY_BLOCK] = length.astype(jnp.bfloat16)
    for copy in copies:
        copy.wait()


def head_columns(ref, first_row, count, head):
    parts = [
        ref[
            first_row : first_row + count,
            (head * GROUP + g) * HEAD_DIM : (head * GROUP + g + 1) * HEAD_DIM,
        ]
        for g in range(GROUP)
    ]
    return jnp.concatenate(parts, axis=0)


def own_rows(ref, head, first):
    parts = [
        packed(ref, first + part)[:, head * HEAD_DIM : (head + 1) * HEAD_DIM]
        for part in range(2)
    ]
    return jnp.concatenate(parts, axis=0)


FACTOR = SCALE * LOG2E


def exponentials(scores, peak):
    return jnp.exp2(scores * FACTOR - peak * FACTOR)


def top(scores):
    return jnp.max(scores, axis=0, keepdims=True)


def column_sum(values):
    return jnp.sum(values, axis=0, keepdims=True)


def own_allowed():
    key = lax.broadcasted_iota(jnp.int32, (ROWS, ROWS), 0)
    return key <= lax.broadcasted_iota(jnp.int32, (ROWS, ROWS), 1)


def own_kernel(query_block, other_block, share_ref):
    allowed = own_allowed()
    for head in range(HALF_HEADS):
        q = head_columns(query_block, 0, ROWS, head)
        do = head_columns(other_block, 0, ROWS, head)
        scores = dot(own_rows(other_block, head, 0), q, NT)
        soft_grad = dot(own_rows(other_block, head, 2), do, NT)
        for start in range(0, GROUP * ROWS, ROWS):
            lanes = slice(start, start + ROWS)
            piece = jnp.where(allowed, scores[:, lanes], MASKED)
            peak = top(piece)
            terms = exponentials(piece, peak)
            share_ref[head, 0:1, lanes] = peak
            share_ref[head, 1:2, lanes] = column_sum(terms)
            share_ref[head, 2:3, lanes] = column_sum(terms * soft_grad[:, lanes])


class Attention:
    def __init__(self, plen_ref, mine_q, mine_other, got_q, got_other, kv_ref, *shares):
        self.shares = shares
        self.sides = (mine_q, mine_other), (got_q, got_other)
        self.kv_ref = kv_ref
        plen = plen_ref[0]
        own = lax.axis_index("sample")
        other = own + 1 - 2 * own_core()
        row_lane = lax.broadcasted_iota(jnp.int32, (1, ROWS), 1)
        self.valid = []
        for ref, _ in self.sides:
            length = ref[EXTRA_ROW:QUERY_BLOCK, :ROWS].astype(jnp.float32)[0:1]
            live = row_lane.astype(jnp.float32) < length
            self.valid.append(jnp.where(live, 1.0, 0.0).astype(jnp.float32))
        self.safe = KEYS - 2 * SLOTS
        self.tail_ok = (
            lax.broadcasted_iota(jnp.int32, (2 * SLOTS, ROWS), 0) + self.safe < plen
        )
        self.own_ok = own_allowed()
        lanes = CORES * GROUP * SLOTS
        lane = lax.broadcasted_iota(jnp.int32, (1, lanes), 1)
        device = jnp.where(lane < GROUP * SLOTS, own, other)
        global_row = device * SLOTS + lax.rem(lane, SLOTS)
        self.prompt_valid = jnp.where(global_row < plen, 1.0, 0.0).astype(jnp.float32)
        self.prompt_ok = lax.broadcasted_iota(jnp.int32, (KEYS, lanes), 0) <= global_row

    def prompt_rows(self, start):
        parts = [
            self.kv_ref[PLACE[device], :, start : start + HEAD_DIM] for device in range(DEVICES)
        ]
        return jnp.concatenate(parts, axis=0)

    def products(self, head, side):
        keys = self.prompt_rows(head * HEAD_DIM)
        values = self.prompt_rows(HALF_WIDTH + head * HEAD_DIM)
        if side < CORES:
            query_block, other_block = self.sides[side]
            if not self.shares:
                keys = jnp.concatenate([keys, own_rows(other_block, head, 0)], axis=0)
                values = jnp.concatenate([values, own_rows(other_block, head, 2)], axis=0)
            q = head_columns(query_block, 0, ROWS, head)
            do = head_columns(other_block, 0, ROWS, head)
        else:
            q, do = (
                jnp.concatenate(
                    [head_columns(ref, PROMPT_ROW, SLOTS, head) for ref in blocks], axis=0
                )
                for blocks in zip(*self.sides)
            )
        return dot(keys, q, NT), dot(values, do, NT), (keys, q, do)

    def weights(self, head, side, scores, soft_grad):
        pieces = []
        for start in range(0, scores.shape[1], ROWS):
            lanes = slice(start, start + ROWS)
            piece, piece_grad = scores[:, lanes], soft_grad[:, lanes]
            if side < CORES:
                parts = [piece[: self.safe], jnp.where(self.tail_ok, piece[self.safe : KEYS], MASKED)]
                if not self.shares:
                    parts.append(jnp.where(self.own_ok, piece[KEYS:], MASKED))
                piece = jnp.concatenate(parts, axis=0)
                valid = self.valid[side]
            else:
                piece = jnp.where(self.prompt_ok, piece, MASKED)
                valid = self.prompt_valid
            peak = top(piece)
            own_total = own_delta = 0.0
            if side < CORES and self.shares:
                own_peak, own_total, own_delta = (
                    self.shares[side][head, n : n + 1, lanes] for n in range(3)
                )
                peak = jnp.maximum(peak, own_peak)
                weight = exponentials(own_peak, peak)
                own_total, own_delta = own_total * weight, own_delta * weight
            terms = exponentials(piece, peak)
            scale = valid / (column_sum(terms) + own_total)
            soft = terms * scale
            soft_b = soft.astype(jnp.bfloat16)
            delta = column_sum(soft_b.astype(jnp.float32) * piece_grad) + own_delta * scale
            pieces.append((soft_b, (soft * (piece_grad - delta)).astype(jnp.bfloat16)))
        return [jnp.concatenate(part, axis=1) for part in zip(*pieces)]

    def units(self):
        todo = [(0, CORES)]
        todo += [(head, side) for head in range(HALF_HEADS) for side in range(CORES)]
        todo += [(head, CORES) for head in range(1, HALF_HEADS)]
        ready = [self.products(*unit) for unit in todo[:2]]
        for n, (head, side) in enumerate(todo):
            scores, soft_grad, operands = ready.pop(0)
            weights = self.weights(head, side, scores, soft_grad)
            if n + 2 < len(todo):
                ready.append(self.products(*todo[n + 2]))
            yield head, side, operands, *weights


def attend_kernel(*refs):
    part_ref = refs[-1]
    terms = {}
    for head, _, (_, q, do), soft_b, grad_b in Attention(*refs[:8]).units():
        terms.setdefault(head, []).append((dot(grad_b, q, NN), dot(soft_b, do, NN)))
        if len(terms[head]) <= CORES:
            continue
        dk, dv = (sum(parts) for parts in zip(*terms[head]))
        for start, grad in ((head, dk * SCALE), (HALF_HEADS + head, dv)):
            grad = grad.astype(jnp.bfloat16)
            for device in range(DEVICES):
                part_ref[PLACE[device], :, start * HEAD_DIM : (start + 1) * HEAD_DIM] = grad[
                    device * SLOTS : (device + 1) * SLOTS
                ]


def grads_kernel(*refs):
    outs = refs[-2:]
    half = ROWS // 2
    for head, side, (keys, q, do), soft_b, grad_b in Attention(*refs[:6]).units():
        dq_t = dot(keys.T, grad_b, NN) * SCALE
        if side == CORES:
            dq = dq_t.T.astype(jnp.bfloat16)
            for n, out in enumerate(outs):
                for g in range(GROUP):
                    column = (head * GROUP + g) * HEAD_DIM
                    row = (n * GROUP + g) * SLOTS
                    out[PROMPT_ROW:EXTRA_ROW, column : column + HEAD_DIM] = dq[
                        row : row + SLOTS
                    ]
            continue
        out = outs[side]
        for g in range(GROUP):
            column = (head * GROUP + g) * HEAD_DIM
            block = dq_t[:, g * ROWS : (g + 1) * ROWS]
            out[:ROWS, column : column + HEAD_DIM] = block.T.astype(jnp.bfloat16)
        own_dk = (dot(grad_b[KEYS:], q, NN) * SCALE).astype(jnp.bfloat16)
        own_dv = dot(soft_b[KEYS:], do, NN).astype(jnp.bfloat16)
        for n, grad in enumerate((own_dk, own_dv)):
            for part in range(2):
                column = (2 * n + part) * HALF_WIDTH + head * HEAD_DIM
                out[EXTRA_ROW:OTHER_BLOCK, column : column + HEAD_DIM] = grad[
                    part * half : (part + 1) * half
                ]


def join_kernel(mine_ref, got_ref, pdq_ref, cdq_ref, cdk_ref, cdv_ref, sems):
    core = own_core()
    copies = []
    for n, (source, half) in enumerate(((mine_ref, core), (got_ref, 1 - core))):
        wide, narrow = columns_of(half, HALF_COLUMNS), columns_of(half, HALF_WIDTH)
        pairs = [
            (source.at[:ROWS], cdq_ref.at[:, wide]),
            (source.at[PROMPT_ROW:EXTRA_ROW], pdq_ref.at[:, wide]),
        ]
        for k, target in enumerate((cdk_ref, cdv_ref)):
            for part in range(2):
                rows = slice(part * ROWS // 2, (part + 1) * ROWS // 2)
                pairs.append((packed(source, 2 * k + part), target.at[rows, narrow]))
        copies += [
            pltpu.make_async_copy(place, target, sems.at[n * len(pairs) + k])
            for k, (place, target) in enumerate(pairs)
        ]
    run(copies)


def total_kernel(terms_ref, dk_ref, dv_ref):
    for core in range(CORES):
        total = sum(
            terms_ref[PLACE[chip * CORES + core]].astype(jnp.float32) for chip in range(CHIPS)
        ).astype(jnp.bfloat16)
        columns = slice(core * HALF_WIDTH, (core + 1) * HALF_WIDTH)
        dk_ref[:, columns] = total[:, :HALF_WIDTH]
        dv_ref[:, columns] = total[:, HALF_WIDTH:]


def kernel(body, name, shapes, in_specs, out_specs, limit, cost, scratch=()):
    flops, moved, transcendentals = cost
    return pl.pallas_call(
        body,
        out_shape=tuple(jax.ShapeDtypeStruct(shape, jnp.bfloat16) for shape in shapes),
        in_specs=in_specs,
        out_specs=out_specs,
        scratch_shapes=list(scratch),
        compiler_params=pltpu.CompilerParams(vmem_limit_bytes=limit * 1024 * 1024),
        cost_estimate=pl.CostEstimate(
            flops=flops, bytes_accessed=moved, transcendentals=transcendentals
        ),
        name=name,
    )


def in_hbm(*arrays):
    return [pltpu.with_memory_space_constraint(a, pltpu.HBM) for a in arrays]


def body(
    prompt_q,
    prompt_k,
    prompt_value_rows,
    prompt_dout,
    comp_q,
    completion_keys,
    completion_values,
    comp_dout,
    comp_lengths,
    prompt_length,
):
    block = (DEVICES, SLOTS, 2 * HALF_WIDTH)
    queries = (QUERY_BLOCK, HALF_COLUMNS)
    others = (OTHER_BLOCK, HALF_COLUMNS)
    swap = [(device, device ^ 1) for device in range(DEVICES)]

    def exchange(blocks):
        return lax.all_to_all(
            blocks, "sample", split_axis=0, concat_axis=0, axis_index_groups=[ORDER], tiled=True
        )

    (outgoing,) = kernel(
        stage_kernel,
        "stage",
        [block],
        [ANY] * 2,
        (VMEM,),
        4,
        (0, 300_000, 0),
        [
            pltpu.VMEM((2, SLOTS, KEY_VALUE_HEADS * HEAD_DIM), jnp.bfloat16),
            pltpu.SemaphoreType.DMA((2,)),
        ],
    )(*in_hbm(prompt_k, prompt_value_rows))
    kv = exchange(outgoing)
    mine_q, mine_other, their_q, their_other = kernel(
        split_kernel,
        "split",
        [queries, others] * 2,
        [SMEM] + [ANY] * 7,
        (VMEM,) * 4,
        8,
        (0, 3_000_000, 0),
        [pltpu.SemaphoreType.DMA((16,))],
    )(
        comp_lengths,
        *in_hbm(
            comp_q[0],
            comp_dout[0],
            prompt_q,
            prompt_dout,
            completion_keys[0],
            completion_values[0],
        ),
        outgoing,
    )
    got_q = lax.ppermute(their_q, "sample", swap)
    got_other = lax.ppermute(their_other, "sample", swap)
    scores_in = prompt_length, mine_q, mine_other, got_q, got_other, kv
    shares = [
        pl.pallas_call(
            own_kernel,
            out_shape=jax.ShapeDtypeStruct((HALF_HEADS, 8, GROUP * ROWS), jnp.float32),
            in_specs=[VMEM] * 2,
            out_specs=VMEM,
            compiler_params=pltpu.CompilerParams(vmem_limit_bytes=16 * 1024 * 1024),
            cost_estimate=pl.CostEstimate(
                flops=1_000_000, bytes_accessed=300_000, transcendentals=0
            ),
            name="own",
        )(*blocks)
        for blocks in ((mine_q, mine_other), (got_q, got_other))
    ]
    cost = (1_000_000_000, 4_000_000, 850_000)
    (partial,) = kernel(
        attend_kernel, "attend", [block], [SMEM] + [VMEM] * 7, (VMEM,), 24, cost
    )(*scores_in, *shares)
    terms = exchange(partial)
    mine_out, theirs_out = kernel(
        grads_kernel, "grads", [others] * 2, [SMEM] + [VMEM] * 5 + [ANY], (VMEM,) * 2, 24, cost
    )(*scores_in, partial)
    got_out = lax.ppermute(theirs_out, "sample", swap)
    width = KEY_VALUE_HEADS * HEAD_DIM
    shapes = (
        (SLOTS, QUERY_HEADS * HEAD_DIM),
        (ROWS, QUERY_HEADS * HEAD_DIM),
        (ROWS, width),
        (ROWS, width),
    )
    pdq, cdq, cdk, cdv = kernel(
        join_kernel,
        "join",
        shapes,
        [VMEM] * 2,
        (ANY,) * 4,
        4,
        (0, 1_700_000, 0),
        [pltpu.SemaphoreType.DMA((12,))],
    )(mine_out, got_out)
    pdk, pdv = kernel(
        total_kernel, "total", [(SLOTS, width)] * 2, [VMEM], (VMEM,) * 2, 4, (130_000, 300_000, 0)
    )(terms)
    return (pdq, pdk, pdv, cdq[None], cdk[None], cdv[None])


def solution(mesh):
    rows = P(("prompt", "sample"), None)
    blocks = P(("prompt", "sample"), None, None)
    in_specs = (rows,) * 4 + (blocks,) * 4 + (P(("prompt", "sample")), P("prompt"))
    out_specs = (rows,) * 3 + (blocks,) * 3
    return jax.shard_map(body, mesh=mesh, in_specs=in_specs, out_specs=out_specs, check_vma=False)
```

```python
import jax
import jax.numpy as jnp
from jax import lax
from jax.experimental import pallas as pl
from jax.experimental.pallas import tpu as pltpu
from jax.sharding import PartitionSpec as P

QUERY_HEADS = 16
KEY_VALUE_HEADS = 4
HEAD_DIM = 128
GROUP = QUERY_HEADS // KEY_VALUE_HEADS
SCALE = HEAD_DIM ** (-0.5)
LOG2E = 1.4426950408889634
CHIPS = 8
CORES = 2
DEVICES = CHIPS * CORES
MASKED = -1e30

HALF_HEADS = KEY_VALUE_HEADS // CORES
HALF_WIDTH = HALF_HEADS * HEAD_DIM
HALF_COLUMNS = HALF_WIDTH * GROUP

SLOTS = 16
ROWS = 128
KEYS = DEVICES * SLOTS

PROMPT_ROW = ROWS
EXTRA_ROW = ROWS + SLOTS
QUERY_BLOCK = EXTRA_ROW + SLOTS
OTHER_BLOCK = EXTRA_ROW + ROWS // 2

ORDER = [
    chip % CHIPS * CORES + core
    for step in range(CHIPS)
    for core in range(CORES)
    for chip in [3 * step + core * (CHIPS // CORES)]
]
PLACE = [ORDER.index(device) for device in range(DEVICES)]

NT = ((1,), (1,))
NN = ((1,), (0,))
VMEM = pl.BlockSpec(memory_space=pltpu.VMEM)
SMEM = pl.BlockSpec(memory_space=pltpu.SMEM)
ANY = pl.BlockSpec(memory_space=pl.ANY)


def dot(a, b, contract):
    return lax.dot_general(a, b, (contract, ((), ())), preferred_element_type=jnp.float32)


def own_core():
    return lax.rem(lax.axis_index("sample"), CORES)


def columns_of(core, width):
    return pl.ds(pl.multiple_of(core * width, HEAD_DIM), width)


def run(copies):
    for copy in copies:
        copy.start()
    for copy in copies:
        copy.wait()


def stage_kernel(k_ref, v_ref, out_ref, kv_ref, blocks_ref, sems):
    run(
        [
            pltpu.make_async_copy(source, kv_ref.at[n], sems.at[n])
            for n, source in enumerate((k_ref, v_ref))
        ]
    )
    halves = []
    for core in range(CORES):
        columns = slice(core * HALF_WIDTH, (core + 1) * HALF_WIDTH)
        halves.append(jnp.concatenate([kv_ref[0, :, columns], kv_ref[1, :, columns]], axis=1))
    copies = []
    for first in range(0, DEVICES, 4):
        for place in range(first, first + 4):
            blocks_ref[place] = halves[ORDER[place] % CORES]
        copy = pltpu.make_async_copy(
            blocks_ref.at[first : first + 4], out_ref.at[first : first + 4], sems.at[2 + first // 4]
        )
        copy.start()
        copies.append(copy)
    for copy in copies:
        copy.wait()


def packed(ref, n):
    return ref.at[EXTRA_ROW:OTHER_BLOCK, n * HALF_WIDTH : (n + 1) * HALF_WIDTH]


def split_kernel(clen_ref, q_ref, do_ref, pq_ref, pdo_ref, ck_ref, cv_ref, _, *refs):
    core = own_core()
    sems = refs[-1]
    copies = []
    for n, half in enumerate((core, 1 - core)):
        query_block, other_block = refs[2 * n : 2 * n + 2]
        wide, narrow = columns_of(half, HALF_COLUMNS), columns_of(half, HALF_WIDTH)
        pairs = [
            (q_ref.at[:, wide], query_block.at[:ROWS]),
            (pq_ref.at[:, wide], query_block.at[PROMPT_ROW:EXTRA_ROW]),
            (do_ref.at[:, wide], other_block.at[:ROWS]),
            (pdo_ref.at[:, wide], other_block.at[PROMPT_ROW:EXTRA_ROW]),
        ]
        for k, source in enumerate((ck_ref, cv_ref)):
            for part in range(2):
                rows = slice(part * ROWS // 2, (part + 1) * ROWS // 2)
                pairs.append((source.at[rows, narrow], packed(other_block, 2 * k + part)))
        copies += [
            pltpu.make_async_copy(source, place, sems.at[n * len(pairs) + k])
            for k, (source, place) in enumerate(pairs)
        ]
    for copy in copies:
        copy.start()
    length = jnp.full((SLOTS, HALF_COLUMNS), clen_ref[0], jnp.int32).astype(jnp.float32)
    for query_block in refs[0:4:2]:
        query_block[EXTRA_ROW:QUERY_BLOCK] = length.astype(jnp.bfloat16)
    for copy in copies:
        copy.wait()


def head_columns(ref, first_row, count, head):
    parts = [
        ref[
            first_row : first_row + count,
            (head * GROUP + g) * HEAD_DIM : (head * GROUP + g + 1) * HEAD_DIM,
        ]
        for g in range(GROUP)
    ]
    return jnp.concatenate(parts, axis=0)


def own_rows(ref, head, first):
    parts = [
        packed(ref, first + part)[:, head * HEAD_DIM : (head + 1) * HEAD_DIM]
        for part in range(2)
    ]
    return jnp.concatenate(parts, axis=0)


FACTOR = SCALE * LOG2E


def exponentials(scores, peak):
    return jnp.exp2(scores * FACTOR - peak * FACTOR)


def top(scores):
    return jnp.max(scores, axis=0, keepdims=True)


def column_sum(values):
    return jnp.sum(values, axis=0, keepdims=True)


def own_allowed():
    key = lax.broadcasted_iota(jnp.int32, (ROWS, ROWS), 0)
    return key <= lax.broadcasted_iota(jnp.int32, (ROWS, ROWS), 1)


def own_kernel(query_block, other_block, share_ref):
    allowed = own_allowed()
    for head in range(HALF_HEADS):
        q = head_columns(query_block, 0, ROWS, head)
        do = head_columns(other_block, 0, ROWS, head)
        scores = dot(own_rows(other_block, head, 0), q, NT)
        soft_grad = dot(own_rows(other_block, head, 2), do, NT)
        for start in range(0, GROUP * ROWS, ROWS):
            lanes = slice(start, start + ROWS)
            piece = jnp.where(allowed, scores[:, lanes], MASKED)
            peak = top(piece)
            terms = exponentials(piece, peak)
            share_ref[head, 0:1, lanes] = peak
            share_ref[head, 1:2, lanes] = column_sum(terms)
            share_ref[head, 2:3, lanes] = column_sum(terms * soft_grad[:, lanes])


class Attention:
    def __init__(self, plen_ref, mine_q, mine_other, got_q, got_other, kv_ref, *shares):
        self.shares = shares
        self.sides = (mine_q, mine_other), (got_q, got_other)
        self.kv_ref = kv_ref
        plen = plen_ref[0]
        own = lax.axis_index("sample")
        other = own + 1 - 2 * own_core()
        row_lane = lax.broadcasted_iota(jnp.int32, (1, ROWS), 1)
        self.valid = []
        for ref, _ in self.sides:
            length = ref[EXTRA_ROW:QUERY_BLOCK, :ROWS].astype(jnp.float32)[0:1]
            live = row_lane.astype(jnp.float32) < length
            self.valid.append(jnp.where(live, 1.0, 0.0).astype(jnp.float32))
        self.safe = KEYS - 2 * SLOTS
        self.tail_ok = (
            lax.broadcasted_iota(jnp.int32, (2 * SLOTS, ROWS), 0) + self.safe < plen
        )
        self.own_ok = own_allowed()
        lanes = CORES * GROUP * SLOTS
        lane = lax.broadcasted_iota(jnp.int32, (1, lanes), 1)
        device = jnp.where(lane < GROUP * SLOTS, own, other)
        global_row = device * SLOTS + lax.rem(lane, SLOTS)
        self.prompt_valid = jnp.where(global_row < plen, 1.0, 0.0).astype(jnp.float32)
        self.prompt_ok = lax.broadcasted_iota(jnp.int32, (KEYS, lanes), 0) <= global_row

    def prompt_rows(self, start):
        parts = [
            self.kv_ref[PLACE[device], :, start : start + HEAD_DIM] for device in range(DEVICES)
        ]
        return jnp.concatenate(parts, axis=0)

    def products(self, head, side):
        keys = self.prompt_rows(head * HEAD_DIM)
        values = self.prompt_rows(HALF_WIDTH + head * HEAD_DIM)
        if side < CORES:
            query_block, other_block = self.sides[side]
            if not self.shares:
                keys = jnp.concatenate([keys, own_rows(other_block, head, 0)], axis=0)
                values = jnp.concatenate([values, own_rows(other_block, head, 2)], axis=0)
            q = head_columns(query_block, 0, ROWS, head)
            do = head_columns(other_block, 0, ROWS, head)
        else:
            q, do = (
                jnp.concatenate(
                    [head_columns(ref, PROMPT_ROW, SLOTS, head) for ref in blocks], axis=0
                )
                for blocks in zip(*self.sides)
            )
        return dot(keys, q, NT), dot(values, do, NT), (keys, q, do)

    def weights(self, head, side, scores, soft_grad):
        pieces = []
        for start in range(0, scores.shape[1], ROWS):
            lanes = slice(start, start + ROWS)
            piece, piece_grad = scores[:, lanes], soft_grad[:, lanes]
            if side < CORES:
                parts = [piece[: self.safe], jnp.where(self.tail_ok, piece[self.safe : KEYS], MASKED)]
                if not self.shares:
                    parts.append(jnp.where(self.own_ok, piece[KEYS:], MASKED))
                piece = jnp.concatenate(parts, axis=0)
                valid = self.valid[side]
            else:
                piece = jnp.where(self.prompt_ok, piece, MASKED)
                valid = self.prompt_valid
            peak = top(piece)
            own_total = own_delta = 0.0
            if side < CORES and self.shares:
                own_peak, own_total, own_delta = (
                    self.shares[side][head, n : n + 1, lanes] for n in range(3)
                )
                peak = jnp.maximum(peak, own_peak)
                weight = exponentials(own_peak, peak)
                own_total, own_delta = own_total * weight, own_delta * weight
            terms = exponentials(piece, peak)
            scale = valid / (column_sum(terms) + own_total)
            soft = terms * scale
            soft_b = soft.astype(jnp.bfloat16)
            delta = column_sum(soft_b.astype(jnp.float32) * piece_grad) + own_delta * scale
            pieces.append((soft_b, (soft * (piece_grad - delta)).astype(jnp.bfloat16)))
        return [jnp.concatenate(part, axis=1) for part in zip(*pieces)]

    def units(self):
        todo = [(head, side) for head in range(HALF_HEADS) for side in (0, 1, 2)]
        following = self.products(*todo[0])
        for n, (head, side) in enumerate(todo):
            scores, soft_grad, operands = following
            if n + 1 < len(todo):
                following = self.products(*todo[n + 1])
            yield head, side, operands, *self.weights(head, side, scores, soft_grad)


def attend_kernel(*refs):
    part_ref, blocks_ref, sems = refs[8:]
    dk = dv = None
    copies = []
    for head, side, (_, q, do), soft_b, grad_b in Attention(*refs[:8]).units():
        more_dv = dot(soft_b, do, NN)
        more_dk = dot(grad_b, q, NN)
        dv = more_dv if side == 0 else dv + more_dv
        dk = more_dk if side == 0 else dk + more_dk
        if side == CORES:
            for start, grad in ((head, dk * SCALE), (HALF_HEADS + head, dv)):
                grad = grad.astype(jnp.bfloat16)
                for device in range(DEVICES):
                    blocks_ref[start, PLACE[device]] = grad[device * SLOTS : (device + 1) * SLOTS]
                copy = pltpu.make_async_copy(
                    blocks_ref.at[start],
                    part_ref.at[:, :, start * HEAD_DIM : (start + 1) * HEAD_DIM],
                    sems.at[start],
                )
                copy.start()
                copies.append(copy)
    for copy in copies:
        copy.wait()


def grads_kernel(*refs):
    outs = refs[-2:]
    half = ROWS // 2
    for head, side, (keys, q, do), soft_b, grad_b in Attention(*refs[:6]).units():
        dq_t = dot(keys.T, grad_b, NN) * SCALE
        if side == CORES:
            dq = dq_t.T.astype(jnp.bfloat16)
            for n, out in enumerate(outs):
                for g in range(GROUP):
                    column = (head * GROUP + g) * HEAD_DIM
                    row = (n * GROUP + g) * SLOTS
                    out[PROMPT_ROW:EXTRA_ROW, column : column + HEAD_DIM] = dq[
                        row : row + SLOTS
                    ]
            continue
        out = outs[side]
        for g in range(GROUP):
            column = (head * GROUP + g) * HEAD_DIM
            block = dq_t[:, g * ROWS : (g + 1) * ROWS]
            out[:ROWS, column : column + HEAD_DIM] = block.T.astype(jnp.bfloat16)
        own_dk = (dot(grad_b[KEYS:], q, NN) * SCALE).astype(jnp.bfloat16)
        own_dv = dot(soft_b[KEYS:], do, NN).astype(jnp.bfloat16)
        for n, grad in enumerate((own_dk, own_dv)):
            for part in range(2):
                column = (2 * n + part) * HALF_WIDTH + head * HEAD_DIM
                out[EXTRA_ROW:OTHER_BLOCK, column : column + HEAD_DIM] = grad[
                    part * half : (part + 1) * half
                ]


def join_kernel(mine_ref, got_ref, pdq_ref, cdq_ref, cdk_ref, cdv_ref, sems):
    core = own_core()
    copies = []
    for n, (source, half) in enumerate(((mine_ref, core), (got_ref, 1 - core))):
        wide, narrow = columns_of(half, HALF_COLUMNS), columns_of(half, HALF_WIDTH)
        pairs = [
            (source.at[:ROWS], cdq_ref.at[:, wide]),
            (source.at[PROMPT_ROW:EXTRA_ROW], pdq_ref.at[:, wide]),
        ]
        for k, target in enumerate((cdk_ref, cdv_ref)):
            for part in range(2):
                rows = slice(part * ROWS // 2, (part + 1) * ROWS // 2)
                pairs.append((packed(source, 2 * k + part), target.at[rows, narrow]))
        copies += [
            pltpu.make_async_copy(place, target, sems.at[n * len(pairs) + k])
            for k, (place, target) in enumerate(pairs)
        ]
    run(copies)


def total_kernel(terms_ref, dk_ref, dv_ref):
    for core in range(CORES):
        total = sum(
            terms_ref[PLACE[chip * CORES + core]].astype(jnp.float32) for chip in range(CHIPS)
        ).astype(jnp.bfloat16)
        columns = slice(core * HALF_WIDTH, (core + 1) * HALF_WIDTH)
        dk_ref[:, columns] = total[:, :HALF_WIDTH]
        dv_ref[:, columns] = total[:, HALF_WIDTH:]


def kernel(body, name, shapes, in_specs, out_specs, limit, cost, scratch=()):
    flops, moved, transcendentals = cost
    return pl.pallas_call(
        body,
        out_shape=tuple(jax.ShapeDtypeStruct(shape, jnp.bfloat16) for shape in shapes),
        in_specs=in_specs,
        out_specs=out_specs,
        scratch_shapes=list(scratch),
        compiler_params=pltpu.CompilerParams(vmem_limit_bytes=limit * 1024 * 1024),
        cost_estimate=pl.CostEstimate(
            flops=flops, bytes_accessed=moved, transcendentals=transcendentals
        ),
        name=name,
    )


def in_hbm(*arrays):
    return [pltpu.with_memory_space_constraint(a, pltpu.HBM) for a in arrays]


def body(
    prompt_q,
    prompt_k,
    prompt_value_rows,
    prompt_dout,
    comp_q,
    completion_keys,
    completion_values,
    comp_dout,
    comp_lengths,
    prompt_length,
):
    block = (DEVICES, SLOTS, 2 * HALF_WIDTH)
    queries = (QUERY_BLOCK, HALF_COLUMNS)
    others = (OTHER_BLOCK, HALF_COLUMNS)
    swap = [(device, device ^ 1) for device in range(DEVICES)]

    def exchange(blocks):
        return lax.all_to_all(
            blocks, "sample", split_axis=0, concat_axis=0, axis_index_groups=[ORDER], tiled=True
        )

    (outgoing,) = kernel(
        stage_kernel,
        "stage",
        [block],
        [ANY] * 2,
        (ANY,),
        4,
        (0, 300_000, 0),
        [
            pltpu.VMEM((2, SLOTS, KEY_VALUE_HEADS * HEAD_DIM), jnp.bfloat16),
            pltpu.VMEM(block, jnp.bfloat16),
            pltpu.SemaphoreType.DMA((2 + DEVICES // 4,)),
        ],
    )(*in_hbm(prompt_k, prompt_value_rows))
    kv = exchange(outgoing)
    mine_q, mine_other, their_q, their_other = kernel(
        split_kernel,
        "split",
        [queries, others] * 2,
        [SMEM] + [ANY] * 7,
        (VMEM,) * 4,
        8,
        (0, 3_000_000, 0),
        [pltpu.SemaphoreType.DMA((16,))],
    )(
        comp_lengths,
        *in_hbm(
            comp_q[0],
            comp_dout[0],
            prompt_q,
            prompt_dout,
            completion_keys[0],
            completion_values[0],
        ),
        outgoing,
    )
    got_q = lax.ppermute(their_q, "sample", swap)
    got_other = lax.ppermute(their_other, "sample", swap)
    scores_in = prompt_length, mine_q, mine_other, got_q, got_other, kv
    shares = [
        pl.pallas_call(
            own_kernel,
            out_shape=jax.ShapeDtypeStruct((HALF_HEADS, 8, GROUP * ROWS), jnp.float32),
            in_specs=[VMEM] * 2,
            out_specs=VMEM,
            compiler_params=pltpu.CompilerParams(vmem_limit_bytes=16 * 1024 * 1024),
            cost_estimate=pl.CostEstimate(
                flops=1_000_000, bytes_accessed=300_000, transcendentals=0
            ),
            name="own",
        )(*blocks)
        for blocks in ((mine_q, mine_other), (got_q, got_other))
    ]
    cost = (1_000_000_000, 4_000_000, 850_000)
    (partial,) = kernel(
        attend_kernel,
        "attend",
        [block],
        [SMEM] + [VMEM] * 7,
        (ANY,),
        24,
        cost,
        [
            pltpu.VMEM((2 * HALF_HEADS, DEVICES, SLOTS, HEAD_DIM), jnp.bfloat16),
            pltpu.SemaphoreType.DMA((2 * HALF_HEADS,)),
        ],
    )(*scores_in, *shares)
    terms = exchange(partial)
    mine_out, theirs_out = kernel(
        grads_kernel, "grads", [others] * 2, [SMEM] + [VMEM] * 5 + [ANY], (VMEM,) * 2, 24, cost
    )(*scores_in, partial)
    got_out = lax.ppermute(theirs_out, "sample", swap)
    width = KEY_VALUE_HEADS * HEAD_DIM
    shapes = (
        (SLOTS, QUERY_HEADS * HEAD_DIM),
        (ROWS, QUERY_HEADS * HEAD_DIM),
        (ROWS, width),
        (ROWS, width),
    )
    pdq, cdq, cdk, cdv = kernel(
        join_kernel,
        "join",
        shapes,
        [VMEM] * 2,
        (ANY,) * 4,
        4,
        (0, 1_700_000, 0),
        [pltpu.SemaphoreType.DMA((12,))],
    )(mine_out, got_out)
    pdk, pdv = kernel(
        total_kernel, "total", [(SLOTS, width)] * 2, [VMEM], (VMEM,) * 2, 4, (130_000, 300_000, 0)
    )(terms)
    return (pdq, pdk, pdv, cdq[None], cdk[None], cdv[None])


def solution(mesh):
    rows = P(("prompt", "sample"), None)
    blocks = P(("prompt", "sample"), None, None)
    in_specs = (rows,) * 4 + (blocks,) * 4 + (P(("prompt", "sample")), P("prompt"))
    out_specs = (rows,) * 3 + (blocks,) * 3
    return jax.shard_map(body, mesh=mesh, in_specs=in_specs, out_specs=out_specs, check_vma=False)
```

```python
import jax
import jax.numpy as jnp
from jax import lax
from jax.experimental import pallas as pl
from jax.experimental.pallas import tpu as pltpu
from jax.sharding import PartitionSpec as P

QUERY_HEADS = 16
KEY_VALUE_HEADS = 4
HEAD_DIM = 128
GROUP = QUERY_HEADS // KEY_VALUE_HEADS
SCALE = HEAD_DIM ** (-0.5)
LOG2E = 1.4426950408889634
CHIPS = 8
CORES = 2
DEVICES = CHIPS * CORES
MASKED = -1e30

HALF_HEADS = KEY_VALUE_HEADS // CORES
HALF_WIDTH = HALF_HEADS * HEAD_DIM
HALF_COLUMNS = HALF_WIDTH * GROUP

SLOTS = 16
ROWS = 128
KEYS = DEVICES * SLOTS

PROMPT_ROW = ROWS
EXTRA_ROW = ROWS + SLOTS
QUERY_BLOCK = EXTRA_ROW + SLOTS
OTHER_BLOCK = EXTRA_ROW + ROWS // 2

ORDER = [
    chip % CHIPS * CORES + core
    for step in range(CHIPS)
    for core in range(CORES)
    for chip in [3 * step + core * (CHIPS // CORES) + 1]
]
PLACE = [ORDER.index(device) for device in range(DEVICES)]

NT = ((1,), (1,))
NN = ((1,), (0,))
VMEM = pl.BlockSpec(memory_space=pltpu.VMEM)
SMEM = pl.BlockSpec(memory_space=pltpu.SMEM)
ANY = pl.BlockSpec(memory_space=pl.ANY)


def dot(a, b, contract):
    return lax.dot_general(a, b, (contract, ((), ())), preferred_element_type=jnp.float32)


def own_core():
    return lax.rem(lax.axis_index("sample"), CORES)


def columns_of(core, width):
    return pl.ds(pl.multiple_of(core * width, HEAD_DIM), width)


def run(copies):
    for copy in copies:
        copy.start()
    for copy in copies:
        copy.wait()


def stage_kernel(k_ref, v_ref, out_ref, kv_ref, sems):
    run(
        [
            pltpu.make_async_copy(source, kv_ref.at[n], sems.at[n])
            for n, source in enumerate((k_ref, v_ref))
        ]
    )
    for core in range(CORES):
        columns = slice(core * HALF_WIDTH, (core + 1) * HALF_WIDTH)
        rows = jnp.concatenate([kv_ref[0, :, columns], kv_ref[1, :, columns]], axis=1)
        for chip in range(CHIPS):
            out_ref[PLACE[chip * CORES + core]] = rows


def packed(ref, n):
    return ref.at[EXTRA_ROW:OTHER_BLOCK, n * HALF_WIDTH : (n + 1) * HALF_WIDTH]


def split_kernel(clen_ref, q_ref, do_ref, pq_ref, pdo_ref, ck_ref, cv_ref, _, *refs):
    core = own_core()
    sems = refs[-1]
    copies = []
    for n, half in enumerate((core, 1 - core)):
        query_block, other_block = refs[2 * n : 2 * n + 2]
        wide, narrow = columns_of(half, HALF_COLUMNS), columns_of(half, HALF_WIDTH)
        pairs = [
            (q_ref.at[:, wide], query_block.at[:ROWS]),
            (pq_ref.at[:, wide], query_block.at[PROMPT_ROW:EXTRA_ROW]),
            (do_ref.at[:, wide], other_block.at[:ROWS]),
            (pdo_ref.at[:, wide], other_block.at[PROMPT_ROW:EXTRA_ROW]),
        ]
        for k, source in enumerate((ck_ref, cv_ref)):
            for part in range(2):
                rows = slice(part * ROWS // 2, (part + 1) * ROWS // 2)
                pairs.append((source.at[rows, narrow], packed(other_block, 2 * k + part)))
        copies += [
            pltpu.make_async_copy(source, place, sems.at[n * len(pairs) + k])
            for k, (source, place) in enumerate(pairs)
        ]
    for copy in copies:
        copy.start()
    length = jnp.full((SLOTS, HALF_COLUMNS), clen_ref[0], jnp.int32).astype(jnp.float32)
    for query_block in refs[0:4:2]:
        query_block[EXTRA_ROW:QUERY_BLOCK] = length.astype(jnp.bfloat16)
    for copy in copies:
        copy.wait()


def head_columns(ref, first_row, count, head):
    parts = [
        ref[
            first_row : first_row + count,
            (head * GROUP + g) * HEAD_DIM : (head * GROUP + g + 1) * HEAD_DIM,
        ]
        for g in range(GROUP)
    ]
    return jnp.concatenate(parts, axis=0)


def own_rows(ref, head, first):
    parts = [
        packed(ref, first + part)[:, head * HEAD_DIM : (head + 1) * HEAD_DIM]
        for part in range(2)
    ]
    return jnp.concatenate(parts, axis=0)


FACTOR = SCALE * LOG2E


def exponentials(scores, peak):
    return jnp.exp2(scores * FACTOR - peak * FACTOR)


def top(scores):
    return jnp.max(scores, axis=0, keepdims=True)


def column_sum(values):
    return jnp.sum(values, axis=0, keepdims=True)


def own_allowed():
    key = lax.broadcasted_iota(jnp.int32, (ROWS, ROWS), 0)
    return key <= lax.broadcasted_iota(jnp.int32, (ROWS, ROWS), 1)


def own_kernel(query_block, other_block, share_ref):
    allowed = own_allowed()
    for head in range(HALF_HEADS):
        q = head_columns(query_block, 0, ROWS, head)
        do = head_columns(other_block, 0, ROWS, head)
        scores = dot(own_rows(other_block, head, 0), q, NT)
        soft_grad = dot(own_rows(other_block, head, 2), do, NT)
        for start in range(0, GROUP * ROWS, ROWS):
            lanes = slice(start, start + ROWS)
            piece = jnp.where(allowed, scores[:, lanes], MASKED)
            peak = top(piece)
            terms = exponentials(piece, peak)
            share_ref[head, 0:1, lanes] = peak
            share_ref[head, 1:2, lanes] = column_sum(terms)
            share_ref[head, 2:3, lanes] = column_sum(terms * soft_grad[:, lanes])


class Attention:
    def __init__(self, plen_ref, mine_q, mine_other, got_q, got_other, kv_ref, *shares):
        self.shares = shares
        self.sides = (mine_q, mine_other), (got_q, got_other)
        self.kv_ref = kv_ref
        plen = plen_ref[0]
        own = lax.axis_index("sample")
        other = own + 1 - 2 * own_core()
        row_lane = lax.broadcasted_iota(jnp.int32, (1, ROWS), 1)
        self.valid = []
        for ref, _ in self.sides:
            length = ref[EXTRA_ROW:QUERY_BLOCK, :ROWS].astype(jnp.float32)[0:1]
            live = row_lane.astype(jnp.float32) < length
            self.valid.append(jnp.where(live, 1.0, 0.0).astype(jnp.float32))
        self.safe = KEYS - 2 * SLOTS
        self.tail_ok = (
            lax.broadcasted_iota(jnp.int32, (2 * SLOTS, ROWS), 0) + self.safe < plen
        )
        self.own_ok = own_allowed()
        lanes = CORES * GROUP * SLOTS
        lane = lax.broadcasted_iota(jnp.int32, (1, lanes), 1)
        device = jnp.where(lane < GROUP * SLOTS, own, other)
        global_row = device * SLOTS + lax.rem(lane, SLOTS)
        self.prompt_valid = jnp.where(global_row < plen, 1.0, 0.0).astype(jnp.float32)
        self.prompt_ok = lax.broadcasted_iota(jnp.int32, (KEYS, lanes), 0) <= global_row

    def prompt_rows(self, start):
        parts = [
            self.kv_ref[PLACE[device], :, start : start + HEAD_DIM] for device in range(DEVICES)
        ]
        return jnp.concatenate(parts, axis=0)

    def products(self, head, side):
        keys = self.prompt_rows(head * HEAD_DIM)
        values = self.prompt_rows(HALF_WIDTH + head * HEAD_DIM)
        if side < CORES:
            query_block, other_block = self.sides[side]
            if not self.shares:
                keys = jnp.concatenate([keys, own_rows(other_block, head, 0)], axis=0)
                values = jnp.concatenate([values, own_rows(other_block, head, 2)], axis=0)
            q = head_columns(query_block, 0, ROWS, head)
            do = head_columns(other_block, 0, ROWS, head)
        else:
            q, do = (
                jnp.concatenate(
                    [head_columns(ref, PROMPT_ROW, SLOTS, head) for ref in blocks], axis=0
                )
                for blocks in zip(*self.sides)
            )
        return dot(keys, q, NT), dot(values, do, NT), (keys, q, do)

    def weights(self, head, side, scores, soft_grad):
        pieces = []
        for start in range(0, scores.shape[1], ROWS):
            lanes = slice(start, start + ROWS)
            piece, piece_grad = scores[:, lanes], soft_grad[:, lanes]
            if side < CORES:
                parts = [piece[: self.safe], jnp.where(self.tail_ok, piece[self.safe : KEYS], MASKED)]
                if not self.shares:
                    parts.append(jnp.where(self.own_ok, piece[KEYS:], MASKED))
                piece = jnp.concatenate(parts, axis=0)
                valid = self.valid[side]
            else:
                piece = jnp.where(self.prompt_ok, piece, MASKED)
                valid = self.prompt_valid
            peak = top(piece)
            own_total = own_delta = 0.0
            if side < CORES and self.shares:
                own_peak, own_total, own_delta = (
                    self.shares[side][head, n : n + 1, lanes] for n in range(3)
                )
                peak = jnp.maximum(peak, own_peak)
                weight = exponentials(own_peak, peak)
                own_total, own_delta = own_total * weight, own_delta * weight
            terms = exponentials(piece, peak)
            scale = valid / (column_sum(terms) + own_total)
            soft = terms * scale
            soft_b = soft.astype(jnp.bfloat16)
            delta = column_sum(soft_b.astype(jnp.float32) * piece_grad) + own_delta * scale
            pieces.append((soft_b, (soft * (piece_grad - delta)).astype(jnp.bfloat16)))
        return [jnp.concatenate(part, axis=1) for part in zip(*pieces)]

    def units(self):
        todo = [(head, side) for head in range(HALF_HEADS) for side in (0, 1, 2)]
        following = self.products(*todo[0])
        for n, (head, side) in enumerate(todo):
            scores, soft_grad, operands = following
            if n + 1 < len(todo):
                following = self.products(*todo[n + 1])
            yield head, side, operands, *self.weights(head, side, scores, soft_grad)


def attend_kernel(*refs):
    part_ref = refs[-1]
    dk = dv = None
    for head, side, (_, q, do), soft_b, grad_b in Attention(*refs[:8]).units():
        more_dv = dot(soft_b, do, NN)
        more_dk = dot(grad_b, q, NN)
        dv = more_dv if side == 0 else dv + more_dv
        dk = more_dk if side == 0 else dk + more_dk
        if side == CORES:
            for start, grad in ((head, dk * SCALE), (HALF_HEADS + head, dv)):
                grad = grad.astype(jnp.bfloat16)
                for device in range(DEVICES):
                    part_ref[PLACE[device], :, start * HEAD_DIM : (start + 1) * HEAD_DIM] = grad[
                        device * SLOTS : (device + 1) * SLOTS
                    ]


def grads_kernel(*refs):
    outs = refs[-2:]
    half = ROWS // 2
    for head, side, (keys, q, do), soft_b, grad_b in Attention(*refs[:6]).units():
        dq_t = dot(keys.T, grad_b, NN) * SCALE
        if side == CORES:
            dq = dq_t.T.astype(jnp.bfloat16)
            for n, out in enumerate(outs):
                for g in range(GROUP):
                    column = (head * GROUP + g) * HEAD_DIM
                    row = (n * GROUP + g) * SLOTS
                    out[PROMPT_ROW:EXTRA_ROW, column : column + HEAD_DIM] = dq[
                        row : row + SLOTS
                    ]
            continue
        out = outs[side]
        for g in range(GROUP):
            column = (head * GROUP + g) * HEAD_DIM
            block = dq_t[:, g * ROWS : (g + 1) * ROWS]
            out[:ROWS, column : column + HEAD_DIM] = block.T.astype(jnp.bfloat16)
        own_dk = (dot(grad_b[KEYS:], q, NN) * SCALE).astype(jnp.bfloat16)
        own_dv = dot(soft_b[KEYS:], do, NN).astype(jnp.bfloat16)
        for n, grad in enumerate((own_dk, own_dv)):
            for part in range(2):
                column = (2 * n + part) * HALF_WIDTH + head * HEAD_DIM
                out[EXTRA_ROW:OTHER_BLOCK, column : column + HEAD_DIM] = grad[
                    part * half : (part + 1) * half
                ]


def join_kernel(mine_ref, got_ref, pdq_ref, cdq_ref, cdk_ref, cdv_ref, sems):
    core = own_core()
    copies = []
    for n, (source, half) in enumerate(((mine_ref, core), (got_ref, 1 - core))):
        wide, narrow = columns_of(half, HALF_COLUMNS), columns_of(half, HALF_WIDTH)
        pairs = [
            (source.at[:ROWS], cdq_ref.at[:, wide]),
            (source.at[PROMPT_ROW:EXTRA_ROW], pdq_ref.at[:, wide]),
        ]
        for k, target in enumerate((cdk_ref, cdv_ref)):
            for part in range(2):
                rows = slice(part * ROWS // 2, (part + 1) * ROWS // 2)
                pairs.append((packed(source, 2 * k + part), target.at[rows, narrow]))
        copies += [
            pltpu.make_async_copy(place, target, sems.at[n * len(pairs) + k])
            for k, (place, target) in enumerate(pairs)
        ]
    run(copies)


def total_kernel(terms_ref, dk_ref, dv_ref):
    for core in range(CORES):
        total = sum(
            terms_ref[PLACE[chip * CORES + core]].astype(jnp.float32) for chip in range(CHIPS)
        ).astype(jnp.bfloat16)
        columns = slice(core * HALF_WIDTH, (core + 1) * HALF_WIDTH)
        dk_ref[:, columns] = total[:, :HALF_WIDTH]
        dv_ref[:, columns] = total[:, HALF_WIDTH:]


def kernel(body, name, shapes, in_specs, out_specs, limit, cost, scratch=()):
    flops, moved, transcendentals = cost
    return pl.pallas_call(
        body,
        out_shape=tuple(jax.ShapeDtypeStruct(shape, jnp.bfloat16) for shape in shapes),
        in_specs=in_specs,
        out_specs=out_specs,
        scratch_shapes=list(scratch),
        compiler_params=pltpu.CompilerParams(vmem_limit_bytes=limit * 1024 * 1024),
        cost_estimate=pl.CostEstimate(
            flops=flops, bytes_accessed=moved, transcendentals=transcendentals
        ),
        name=name,
    )


def in_hbm(*arrays):
    return [pltpu.with_memory_space_constraint(a, pltpu.HBM) for a in arrays]


def body(
    prompt_q,
    prompt_k,
    prompt_value_rows,
    prompt_dout,
    comp_q,
    completion_keys,
    completion_values,
    comp_dout,
    comp_lengths,
    prompt_length,
):
    block = (DEVICES, SLOTS, 2 * HALF_WIDTH)
    queries = (QUERY_BLOCK, HALF_COLUMNS)
    others = (OTHER_BLOCK, HALF_COLUMNS)
    swap = [(device, device ^ 1) for device in range(DEVICES)]

    def exchange(blocks):
        return lax.all_to_all(
            blocks, "sample", split_axis=0, concat_axis=0, axis_index_groups=[ORDER], tiled=True
        )

    (outgoing,) = kernel(
        stage_kernel,
        "stage",
        [block],
        [ANY] * 2,
        (VMEM,),
        4,
        (0, 300_000, 0),
        [
            pltpu.VMEM((2, SLOTS, KEY_VALUE_HEADS * HEAD_DIM), jnp.bfloat16),
            pltpu.SemaphoreType.DMA((2,)),
        ],
    )(*in_hbm(prompt_k, prompt_value_rows))
    kv = exchange(outgoing)
    mine_q, mine_other, their_q, their_other = kernel(
        split_kernel,
        "split",
        [queries, others] * 2,
        [SMEM] + [ANY] * 7,
        (VMEM,) * 4,
        8,
        (0, 3_000_000, 0),
        [pltpu.SemaphoreType.DMA((16,))],
    )(
        comp_lengths,
        *in_hbm(
            comp_q[0],
            comp_dout[0],
            prompt_q,
            prompt_dout,
            completion_keys[0],
            completion_values[0],
        ),
        outgoing,
    )
    got_q = lax.ppermute(their_q, "sample", swap)
    got_other = lax.ppermute(their_other, "sample", swap)
    scores_in = prompt_length, mine_q, mine_other, got_q, got_other, kv
    shares = [
        pl.pallas_call(
            own_kernel,
            out_shape=jax.ShapeDtypeStruct((HALF_HEADS, 8, GROUP * ROWS), jnp.float32),
            in_specs=[VMEM] * 2,
            out_specs=VMEM,
            compiler_params=pltpu.CompilerParams(vmem_limit_bytes=16 * 1024 * 1024),
            cost_estimate=pl.CostEstimate(
                flops=1_000_000, bytes_accessed=300_000, transcendentals=0
            ),
            name="own",
        )(*blocks)
        for blocks in ((mine_q, mine_other), (got_q, got_other))
    ]
    cost = (1_000_000_000, 4_000_000, 850_000)
    (partial,) = kernel(
        attend_kernel, "attend", [block], [SMEM] + [VMEM] * 7, (VMEM,), 24, cost
    )(*scores_in, *shares)
    terms = exchange(partial)
    mine_out, theirs_out = kernel(
        grads_kernel, "grads", [others] * 2, [SMEM] + [VMEM] * 5 + [ANY], (VMEM,) * 2, 24, cost
    )(*scores_in, partial)
    got_out = lax.ppermute(theirs_out, "sample", swap)
    width = KEY_VALUE_HEADS * HEAD_DIM
    shapes = (
        (SLOTS, QUERY_HEADS * HEAD_DIM),
        (ROWS, QUERY_HEADS * HEAD_DIM),
        (ROWS, width),
        (ROWS, width),
    )
    pdq, cdq, cdk, cdv = kernel(
        join_kernel,
        "join",
        shapes,
        [VMEM] * 2,
        (ANY,) * 4,
        4,
        (0, 1_700_000, 0),
        [pltpu.SemaphoreType.DMA((12,))],
    )(mine_out, got_out)
    pdk, pdv = kernel(
        total_kernel, "total", [(SLOTS, width)] * 2, [VMEM], (VMEM,) * 2, 4, (130_000, 300_000, 0)
    )(terms)
    return (pdq, pdk, pdv, cdq[None], cdk[None], cdv[None])


def solution(mesh):
    rows = P(("prompt", "sample"), None)
    blocks = P(("prompt", "sample"), None, None)
    in_specs = (rows,) * 4 + (blocks,) * 4 + (P(("prompt", "sample")), P("prompt"))
    out_specs = (rows,) * 3 + (blocks,) * 3
    return jax.shard_map(body, mesh=mesh, in_specs=in_specs, out_specs=out_specs, check_vma=False)
```
